32 devices in a mesh: seq: 8 (over z, x), head: 4 (over y, core).
Axes of the slice: x: 2, y: 2, z: 4, core: 2. Of those that a mesh axis runs over, the one named last changes fastest.
Arguments:
- hidden: bfloat16 [128, 8192], P(None, 'seq'), may hold values from -6 to 6
- query_weight: bfloat16 [8192, 8192], P('seq', 'head'), may hold values from -0.0625 to 0.0625
- key_weight: bfloat16 [8192, 1024], P('seq', 'head'), may hold values from -0.0625 to 0.0625
- value_weight: bfloat16 [8192, 1024], P('seq', 'head'), may hold values from -0.0625 to 0.0625
- output_weight: bfloat16 [8192, 8192], P('head', 'seq'), may hold values from -0.0625 to 0.0625
- cache_keys: bfloat16 [65536, 1024], P('seq', 'head')
- cache_values: bfloat16 [65536, 1024], P('seq', 'head'), may hold values from -6 to 6
- cache_lens: int32 [8], P('seq'), may hold values from 1 to 8192, 40960 in all
Outputs:
- mixed: bfloat16 [128, 8192], P('head', 'seq')
The draws below stay inside these ranges and needn't reach their ends.
Inputs may be any that keep to these rules, and one draw needn't show every extreme that they name: `cache_lens`: the lengths sum to 5/8 of all 65536 slots; the largest is exactly 8192.
All inputs are finite; a program needn't handle non-finite values. No bound on the sum of `cache_lens` on one device may be relied on, other than what follows from the above.
Results may differ from the reference program's by a relative error of at most 0.006.
The reference program's roundings to bfloat16 on the way count: a program that leaves them out, or rounds other values in their place, can miss the bound.
Values may be sent and summed in bfloat16 or wider, within the bound.
No kernel may reach another device: no remote copies, remote signals or barrier semaphores. Data moves between devices by JAX's collectives and lax.ppermute only.
A program may use at most 128 MiB of HBM per device.

```python
import math
import jax
import jax.numpy as jnp
import numpy as np
from jax import lax

D = 8192
QH = 64
KVH = 8
HD = 128
T_NEW = 128
CACHE_DEV = 8192
NCACHE = 65536
N_SEQ = 8


def draw_cache_keys(key, part):
    key = jax.random.fold_in(key, 7)
    shape = (NCACHE, KVH * HD)
    values = jnp.clip(jax.random.normal(key, shape, jnp.float32), -6.0, 6.0)
    return values.astype(jnp.bfloat16)


def steps_of(own_key, extent, cuts, smallest, largest):
    factor_of = 1.0
    for position, parts in cuts:
        heights = jax.random.uniform(jax.random.fold_in(jax.random.fold_in(own_key, 6), position), (parts,), jnp.float32, smallest / len(cuts), largest / len(cuts))
        factor_of = factor_of * jnp.repeat(jnp.exp(heights), extent[position] // parts).reshape((-1,) + (1,) * (len(extent) - 1 - position))
    return factor_of


def split_up(amount, total, bound, slope):
    weights = [(1 << 20) // math.isqrt(standing ** slope) + 1 for standing in range(2, amount + 1)]
    rest, given = total - bound - (amount - 1), [1] * (amount - 1)
    while rest > 0:
        free = [i for i in range(amount - 1) if given[i] < bound]
        whole, remaining = sum([weights[i] for i in free]), rest
        for i in free:
            addition = min(bound - given[i], max(1, remaining * weights[i] // whole), rest)
            given[i] = given[i] + addition
            rest = rest - addition
    return np.array([bound] + given)


def ragged_sizes(key, count, total, most, skew):
    if count == 2:
        one = jax.random.randint(key, (), max(1, total - most), min(most, total - 1) + 1)
        return jnp.stack([one, total - one])
    lengths = jnp.asarray(split_up(count, total, most, skew), jnp.int32)
    couples = (count - 1) // 2
    giver, receiver = lengths[1:1 + 2 * couples:2], lengths[2:2 + 2 * couples:2]
    room = jnp.minimum(giver - 1, most - receiver)
    passed = jax.random.randint(jax.random.fold_in(key, 1), (couples,), 0, 1 << 20) % (room + 1)
    lengths = lengths.at[1:1 + 2 * couples:2].set(giver - passed).at[2:2 + 2 * couples:2].set(receiver + passed)
    return lengths[jax.random.permutation(jax.random.fold_in(key, 2), count)]


def bell_draw(key, shape, spread, most, shards=(), kind=jnp.bfloat16):
    values = jax.random.normal(key, shape, jnp.float32) * spread
    if len(shards) > 0:
        values = steps_of(key, shape, shards, -0.22, 0.18) * values
    return jnp.clip(values, min=-most, max=most).astype(kind)


def setup_inputs(seed: int = 0) -> dict:
    key_list = jax.random.split(jax.random.key(seed), 9)
    hidden = bell_draw(key_list[0], (T_NEW, D), 1.0, 6.0, ((1, 8),))
    query_weight = bell_draw(key_list[1], (D, QH * HD), D ** -0.5, 0.0625, ((0, 8), (1, 4)))
    key_weight = bell_draw(key_list[2], (D, KVH * HD), D ** -0.5, 0.0625, ((0, 8), (1, 4)))
    value_weight = bell_draw(key_list[3], (D, KVH * HD), D ** -0.5, 0.0625, ((0, 8), (1, 4)))
    output_weight = bell_draw(key_list[4], (QH * HD, D), (QH * HD) ** -0.5, 0.0625, ((0, 4), (1, 8)))
    cache_keys = draw_cache_keys(jax.random.fold_in(key_list[8], 71), 0)
    cache_values = bell_draw(key_list[6], (NCACHE, KVH * HD), 1.0, 6.0, ((0, 8), (1, 4)))
    cache_lens = ragged_sizes(key_list[7], N_SEQ, N_SEQ * CACHE_DEV * 5 // 8, CACHE_DEV, 2).astype(jnp.int32)
    return {"hidden": hidden, "query_weight": query_weight, "key_weight": key_weight, "value_weight": value_weight, "output_weight": output_weight, "cache_keys": cache_keys, "cache_values": cache_values, "cache_lens": cache_lens}


NEG_BIG = -1e+30

def attend(q_block, keys3, values3, visible):
    scores = jnp.einsum('tkgd,ckd->tkgc', q_block, keys3, preferred_element_type=jnp.float32)
    scores = scores * (1.0 / math.sqrt(q_block.shape[-1]))
    mask = visible[:, None, None, :]
    masked = jnp.where(mask, scores, NEG_BIG)
    peaks = lax.optimization_barrier(jnp.max(masked, axis=-1))
    weights = jnp.where(mask, jnp.exp(masked - peaks[..., None]), 0.0).astype(jnp.bfloat16)
    totals = lax.optimization_barrier(jnp.sum(weights.astype(jnp.float32), axis=-1))
    outputs = jnp.einsum('tkgc,ckd->tkgd', weights, values3, preferred_element_type=jnp.float32)
    return (peaks, totals, outputs)

def cache_partial(queries, keys3, values3, length):
    tokens = queries.shape[0]
    block_len = math.gcd(tokens, 64)
    slot_count = keys3.shape[0]
    slot_ids = jnp.arange(slot_count, dtype=jnp.int32)
    visible = jnp.broadcast_to((slot_ids < length)[None, :], (block_len, slot_count))

    def handle(q_block):
        return attend(q_block, keys3, values3, visible)
    q_blocks = queries.reshape((tokens // block_len, block_len) + queries.shape[1:])
    peaks, totals, outputs = lax.map(handle, q_blocks)
    return (peaks.reshape((tokens,) + peaks.shape[2:]), totals.reshape((tokens,) + totals.shape[2:]), outputs.reshape((tokens,) + outputs.shape[2:]))

def finish(peaks, totals, outputs, new_peaks, new_totals, new_outputs):
    joint_peak = jnp.maximum(peaks, new_peaks)
    first_scale = jnp.exp(peaks - joint_peak)
    second_scale = jnp.exp(new_peaks - joint_peak)
    whole_total = totals * first_scale + new_totals * second_scale
    whole_out = outputs * first_scale[..., None] + new_outputs * second_scale[..., None]
    attended = whole_out / whole_total[..., None]
    return attended.reshape(attended.shape[0], -1).astype(jnp.bfloat16)

def reference(hidden, query_weight, key_weight, value_weight, output_weight, cache_keys, cache_values, cache_lens):
    group_size = QH // KVH
    queries = jnp.dot(hidden, query_weight, preferred_element_type=jnp.float32).astype(jnp.bfloat16)
    queries = queries.reshape(T_NEW, KVH, group_size, HD)
    new_keys = jnp.dot(hidden, key_weight, preferred_element_type=jnp.float32).astype(jnp.bfloat16).reshape(T_NEW, KVH, HD)
    new_values = jnp.dot(hidden, value_weight, preferred_element_type=jnp.float32).astype(jnp.bfloat16).reshape(T_NEW, KVH, HD)
    keys_all = cache_keys.reshape(N_SEQ, CACHE_DEV, KVH, HD)
    values_all = cache_values.reshape(N_SEQ, CACHE_DEV, KVH, HD)

    def per_shard(items):
        keys3, values3, length = items
        return cache_partial(queries, keys3, values3, length)
    peaks, totals, outputs = lax.map(per_shard, (keys_all, values_all, cache_lens))
    peak = lax.optimization_barrier(jnp.max(peaks, axis=0))
    factor = jnp.exp(peaks - peak[None])
    cache_total = lax.optimization_barrier(jnp.sum(totals * factor, axis=0))
    cache_out = lax.optimization_barrier(jnp.sum(outputs * factor[..., None], axis=0))
    token_ids = jnp.arange(T_NEW, dtype=jnp.int32)
    visible_new = token_ids[None, :] <= token_ids[:, None]
    new_peak, new_total, new_out = attend(queries, new_keys, new_values, visible_new)
    attended = finish(peak, cache_total, cache_out, new_peak, new_total, new_out)
    return jnp.dot(attended, output_weight, preferred_element_type=jnp.float32).astype(jnp.bfloat16)
```

```python
import functools
import math

import jax
import jax.numpy as jnp
from jax import lax
from jax.experimental import pallas as pl
from jax.experimental.pallas import tpu as pltpu
from jax.sharding import PartitionSpec as P

QH = 64
KVH = 8
HD = 128

NEG_BIG = -1e30
LANES = 128
STAT_ROWS = 8
NT = (((1,), (1,)), ((), ()))

OUTPUT_SCALE = 2.0**12
MIXED_SCALE = 2.0**-3


def vmem_spec():
    return pl.BlockSpec(memory_space=pltpu.VMEM)


def smem_spec():
    return pl.BlockSpec(memory_space=pltpu.SMEM)


def to_owners(array, axis):
    return lax.all_to_all(array, axis, 0, 0)


def project_kernel(hidden_ref, *refs, blocks):
    out = refs[-1]
    tokens = hidden_ref.shape[0]
    hidden = hidden_ref[...]
    first = 0
    for weight_refs, block in zip((refs[:1], refs[1:-1]), blocks):
        per = tokens // block
        piece = 0
        for weight_ref in weight_refs:
            product = jnp.dot(hidden, weight_ref[...], preferred_element_type=jnp.float32)
            for c in range(product.shape[1] // LANES):
                for e in range(per):
                    out[piece, first : first + block, :] = product[
                        e * block : (e + 1) * block, c * LANES : (c + 1) * LANES
                    ]
                    piece += 1
        first += block


def project(hidden, weight, chunk, columns, others, count):
    tokens, depth = hidden.shape
    wide = [columns] + [other.shape[1] for other in others]
    blocks = [columns // LANES * tokens // count]
    if others:
        blocks.append(sum(wide[1:]) // LANES * tokens // count)
    total = sum(wide)
    return pl.pallas_call(
        functools.partial(project_kernel, blocks=blocks),
        grid=(1,),
        out_shape=jax.ShapeDtypeStruct((count, sum(blocks), LANES), jnp.float32),
        in_specs=[
            pl.BlockSpec((tokens, depth), lambda i: (0, 0)),
            pl.BlockSpec((depth, columns), lambda i: (0, chunk)),
        ]
        + [pl.BlockSpec(other.shape, lambda i: (0, 0)) for other in others],
        out_specs=pl.BlockSpec((count, sum(blocks), LANES), lambda i: (0, 0, 0)),
        compiler_params=pltpu.CompilerParams(vmem_limit_bytes=24 << 20),
        cost_estimate=pl.CostEstimate(
            flops=2 * tokens * depth * total,
            bytes_accessed=2 * depth * total,
            transcendentals=0,
        ),
    )(hidden, weight, *others)


def attention_kernel(len_ref, q_ref, k_ref, v_ref, o_ref, *scratch, band, step, block):
    s_bufs, m_bufs = scratch[:2], scratch[2:4]
    shift, acc, lse_all = scratch[4:]
    count = q_ref.shape[0]
    rows = count * block
    bands = rows // band
    share = band // block
    scale = math.log2(math.e) / math.sqrt(HD)
    piece = math.gcd(step, 1024)
    tiles = piece // LANES

    length = len_ref[0]
    full = length // step
    rest = length - full * step

    def score(r, i, first, masked):
        q = q_ref[r * share : (r + 1) * share, :block, :].reshape(band, HD)
        keys = k_ref[pl.ds(pl.multiple_of(i * step + first, piece), piece), :]
        s = lax.dot_general(q, keys, NT, preferred_element_type=jnp.float32)
        if masked:
            column = first + lax.broadcasted_iota(jnp.int32, (band, piece), 1)
            s = jnp.where(column < rest, s, NEG_BIG)
        s_bufs[r % 2][i, :, first : first + piece] = s
        tops = [s[:, c * LANES : (c + 1) * LANES] for c in range(tiles)]
        while len(tops) > 1:
            tops = [jnp.maximum(a, b) for a, b in zip(tops[0::2], tops[1::2])]
        m_bufs[r % 2][...] = jnp.maximum(m_bufs[r % 2][...], tops[0])

    def weigh(r, i, first):
        s = s_bufs[r % 2][i, :, first : first + piece]
        low = shift[...]
        weights = jnp.concatenate(
            [
                jnp.exp2(s[:, c * LANES : (c + 1) * LANES] * scale - low).astype(jnp.bfloat16)
                for c in range(tiles)
            ],
            axis=1,
        )
        values = v_ref[pl.ds(pl.multiple_of(i * step + first, piece), piece), :]
        wide = jnp.concatenate([values, jnp.ones((piece, LANES), jnp.bfloat16)], axis=1)
        acc[...] += jnp.dot(weights, wide, preferred_element_type=jnp.float32)

    for r in range(bands + 1):
        scores, weighs = r < bands, r > 0
        if scores:
            m_bufs[r % 2][...] = jnp.full((band, LANES), -3e38, jnp.float32)
        if weighs:
            top = jnp.max(m_bufs[(r - 1) % 2][...], axis=1, keepdims=True)
            shift[...] = jnp.broadcast_to(top * scale, (band, LANES))
            acc[...] = jnp.zeros(acc.shape, jnp.float32)

        def both(i, masked):
            for first in range(0, step, piece):
                if weighs:
                    weigh(r - 1, i, first)
                if scores:
                    score(r, i, first, masked)

        def body(i, carry):
            both(i, False)
            return carry

        lax.fori_loop(0, full, body, 0)

        @pl.when(rest > 0)
        def _():
            both(full, True)

        if weighs:
            totals = acc[:, LANES:]
            mean = acc[:, :LANES] / totals * OUTPUT_SCALE
            o_ref[(r - 1) * share : r * share, :block, :] = mean.reshape(share, block, HD)
            lse_all[(r - 1) * band : r * band, :] = shift[...] + jnp.log2(totals)

    per = LANES // block
    row = lax.broadcasted_iota(jnp.int32, (STAT_ROWS, LANES), 0)
    for g in range(rows // LANES):
        level = lse_all[g * LANES : (g + 1) * LANES, :].T[:STAT_ROWS, :]
        exponent = jnp.floor(jnp.log2(jnp.maximum(jnp.abs(level), 1e-30)))
        exponent = jnp.minimum(exponent, 120.0)
        rest_of = level * jnp.exp2(-exponent)
        first = jnp.floor(rest_of * 2.0**9 + 0.5)
        rest_of = rest_of - first * 2.0**-9
        second = jnp.floor(rest_of * 2.0**20 + 0.5)
        third = (rest_of - second * 2.0**-20) * 2.0**31
        stats = jnp.where(row == 0, exponent, jnp.where(row == 1, first, second))
        stats = jnp.where(row >= 3, third, stats)
        for e in range(per):
            o_ref[g * per + e, block:, :] = stats


def attention(queries, block, keys, values, length, head):
    count = queries.shape[0]
    rows, slots = count * block, keys.shape[0]
    band = math.gcd(rows, 256)
    step = math.gcd(slots, 2048)
    return pl.pallas_call(
        functools.partial(attention_kernel, band=band, step=step, block=block),
        grid=(1,),
        out_shape=jax.ShapeDtypeStruct((count, block + STAT_ROWS, HD), jnp.float32),
        in_specs=[smem_spec(), pl.BlockSpec(queries.shape, lambda i: (0, 0, 0))]
        + [pl.BlockSpec((slots, HD), lambda i: (0, head), pipeline_mode=pl.Buffered(1))] * 2,
        out_specs=pl.BlockSpec((count, block + STAT_ROWS, HD), lambda i: (0, 0, 0)),
        scratch_shapes=[
            pltpu.VMEM((slots // step, band, step), jnp.float32),
            pltpu.VMEM((slots // step, band, step), jnp.float32),
            pltpu.VMEM((band, LANES), jnp.float32),
            pltpu.VMEM((band, LANES), jnp.float32),
            pltpu.VMEM((band, LANES), jnp.float32),
            pltpu.VMEM((band, 2 * LANES), jnp.float32),
            pltpu.VMEM((rows, LANES), jnp.float32),
        ],
        compiler_params=pltpu.CompilerParams(vmem_limit_bytes=40 << 20),
        cost_estimate=pl.CostEstimate(
            flops=8 * rows * slots * HD,
            bytes_accessed=4 * slots * HD,
            transcendentals=rows * slots,
        ),
    )(length, queries, keys, values)


def merge_kernel(me_ref, part_ref, q_ref, kv_ref, o_ref, *, head, kv_local, tokens):
    count = part_ref.shape[0]
    block = q_ref.shape[0]
    per = LANES // block
    scale = math.log2(math.e) / math.sqrt(HD)

    keys = kv_ref[head * tokens : (head + 1) * tokens, :]
    second = (kv_local + head) * tokens
    values = kv_ref[second : second + tokens, :]

    s = lax.dot_general(q_ref[...], keys, NT, preferred_element_type=jnp.float32) * scale
    token = lax.rem(me_ref[0] * block, tokens) + lax.broadcasted_iota(jnp.int32, s.shape, 0)
    visible = lax.broadcasted_iota(jnp.int32, s.shape, 1) <= token
    s = jnp.where(visible, s, NEG_BIG)
    new_top = jnp.max(s, axis=1, keepdims=True)
    weights = jnp.where(visible, jnp.exp2(s - new_top), 0.0).astype(jnp.bfloat16)
    new_total = jnp.sum(weights.astype(jnp.float32), axis=1, keepdims=True)
    new_out = jnp.dot(weights, values, preferred_element_type=jnp.float32)

    place = lax.rem(me_ref[0], per)
    lane = lax.broadcasted_iota(jnp.int32, (block, LANES), 1)
    mine = lane == place * block + lax.broadcasted_iota(jnp.int32, (block, LANES), 0)
    levels = []
    for k in range(count):
        stats = part_ref[k, block:, :]
        level = stats[1:2, :] * 2.0**-9 + stats[2:3, :] * 2.0**-20 + stats[3:4, :] * 2.0**-31
        level = jnp.broadcast_to(level * jnp.exp2(stats[0:1, :]), (block, LANES))
        levels.append(jnp.sum(jnp.where(mine, level, 0.0), axis=1, keepdims=True))
    joint = new_top
    for level in levels:
        joint = jnp.maximum(joint, level)
    new_scale = jnp.exp2(new_top - joint)
    whole_out = new_out * new_scale
    whole_total = new_total * new_scale
    for k in range(count):
        factor = jnp.exp2(levels[k] - joint)
        whole_out = whole_out + part_ref[k, :block, :] * (factor * (1.0 / OUTPUT_SCALE))
        whole_total = whole_total + factor
    o_ref[...] = (whole_out / whole_total).astype(jnp.bfloat16)


def merge(me, parts, q_mine, kv, head, kv_local, tokens):
    return pl.pallas_call(
        functools.partial(merge_kernel, head=head, kv_local=kv_local, tokens=tokens),
        out_shape=jax.ShapeDtypeStruct(q_mine.shape, jnp.bfloat16),
        in_specs=[smem_spec()] + [vmem_spec()] * 3,
        out_specs=vmem_spec(),
    )(me, parts, q_mine, kv)


def output_kernel(w_ref, a_ref, *refs, tokens, groups, has_before, chunk):
    before = refs[0] if has_before else None
    o_ref, w_all, sems = refs[-3:]
    copies = []
    for g in range(groups):
        copies.append(
            pltpu.make_async_copy(
                w_ref.at[pl.ds((chunk * groups + g) * HD, HD), :],
                w_all.at[pl.ds(g * HD, HD), :],
                sems.at[g],
            )
        )
        copies[-1].start()
    rows = jnp.concatenate([a_ref[g * tokens : (g + 1) * tokens, :] for g in range(groups)], axis=1)
    for copy in copies:
        copy.wait()
    product = jnp.dot(rows, w_all[...], preferred_element_type=jnp.float32)
    if has_before:
        product = product + before[...]
    o_ref[...] = product


def output_part(weight, attended, tokens, before, chunk):
    groups = QH // KVH
    width = weight.shape[1]
    has_before = before is not None
    return pl.pallas_call(
        functools.partial(
            output_kernel, tokens=tokens, groups=groups, has_before=has_before, chunk=chunk
        ),
        out_shape=jax.ShapeDtypeStruct((tokens, width), jnp.float32),
        in_specs=[pl.BlockSpec(memory_space=pl.ANY)] + [vmem_spec()] * (1 + int(has_before)),
        out_specs=vmem_spec(),
        scratch_shapes=[
            pltpu.VMEM((groups * HD, width), jnp.bfloat16),
            pltpu.SemaphoreType.DMA((groups,)),
        ],
        compiler_params=pltpu.CompilerParams(vmem_limit_bytes=24 << 20),
        cost_estimate=pl.CostEstimate(
            flops=2 * tokens * groups * HD * width,
            bytes_accessed=2 * groups * HD * width,
            transcendentals=0,
        ),
    )(weight, attended, *([before] if has_before else []))


def shards(
    hidden,
    query_weight,
    key_weight,
    value_weight,
    output_weight,
    cache_keys,
    cache_values,
    cache_lens,
):
    tokens = hidden.shape[0]
    count = lax.axis_size("seq")
    heads = lax.axis_size("head")
    kv_local = cache_keys.shape[1] // HD
    columns = (QH // KVH) * HD
    block = (QH // KVH) * tokens // count
    me = lax.axis_index("seq").reshape(1)

    mine = []
    for j in range(kv_local):
        others = [key_weight, value_weight] if j == kv_local - 1 else []
        partial = project(hidden, query_weight, j, columns, others, count)
        mine.append(jnp.sum(to_owners(partial, "seq"), axis=0).astype(jnp.bfloat16))
    queries = [lax.all_gather(rows, "seq") for rows in mine]
    kv = queries[-1][:, block:, :].reshape(-1, HD)

    mixed = None
    for j in range(kv_local):
        parts = attention(queries[j], block, cache_keys, cache_values, cache_lens, j)
        parts = to_owners(parts.astype(jnp.float16), "seq").astype(jnp.float32)
        attended = merge(me, parts, mine[j][:block], kv, j, kv_local, tokens)
        attended = lax.all_gather(attended, "seq", tiled=True)
        mixed = output_part(output_weight, attended, tokens, mixed, j)

    mixed = (mixed * MIXED_SCALE).reshape(heads, tokens // heads, mixed.shape[1])
    mixed = jnp.sum(to_owners(mixed.astype(jnp.float16), "head").astype(jnp.float32), axis=0)
    return (mixed * (1.0 / MIXED_SCALE)).astype(jnp.bfloat16)


def solution(mesh):
    placed = (
        P(None, "seq"),
        P("seq", "head"),
        P("seq", "head"),
        P("seq", "head"),
        P("head", "seq"),
        P("seq", "head"),
        P("seq", "head"),
        P("seq"),
    )
    return jax.shard_map(
        shards, mesh=mesh, in_specs=placed, out_specs=P("head", "seq"), check_vma=False
    )
```

```python
import functools
import math

import jax
import jax.numpy as jnp
from jax import lax
from jax.experimental import pallas as pl
from jax.experimental.pallas import tpu as pltpu
from jax.sharding import PartitionSpec as P

QH = 64
KVH = 8
HD = 128

NEG_BIG = -1e30
LANES = 128
STAT_ROWS = 8
VMEM_GRANT = 56 << 20
NT = (((1,), (1,)), ((), ()))

OUTPUT_SCALE = 2.0**12
MIXED_SCALE = 2.0**-3


def vmem_spec():
    return pl.BlockSpec(memory_space=pltpu.VMEM)


def smem_spec():
    return pl.BlockSpec(memory_space=pltpu.SMEM)


def hbm_spec():
    return pl.BlockSpec(memory_space=pl.ANY)


def with_partner(array):
    size = lax.axis_size("seq")
    return lax.ppermute(array, "seq", [(i, i ^ 1) for i in range(size)])


def within_parity(array):
    size = lax.axis_size("seq")
    groups = [list(range(first, size, 2)) for first in range(2)]
    return lax.all_to_all(array, "seq", 0, 0, axis_index_groups=groups)


def spread(block):
    half = lax.axis_size("seq") // 2
    same = within_parity(jnp.broadcast_to(block[None], (half,) + block.shape))
    return same, with_partner(same)


def project_kernel(me_ref, hidden_ref, *refs, blocks, chunk, columns, extra):
    weight_refs, (keep_ref, send_ref, w_all, sems) = refs[: 1 + extra], refs[1 + extra :]
    tokens = hidden_ref.shape[0]
    odd = lax.rem(me_ref[0], 2) == 1
    piece = w_all.shape[2]
    jobs = [(weight_refs[0], chunk * columns + c, 0) for c in range(0, columns, piece)]
    for other in weight_refs[1:]:
        jobs += [(other, c, 1) for c in range(0, other.shape[1], piece)]
    copies = []
    for i, (ref, start, _) in enumerate(jobs):
        copies.append(
            pltpu.make_async_copy(ref.at[:, pl.ds(start, piece)], w_all.at[i], sems.at[i])
        )
        copies[-1].start()
    hidden = hidden_ref[...]
    owner, waiting = [0, 0], [[], []]
    for i, (_, _, kind) in enumerate(jobs):
        block = blocks[kind]
        first = kind * blocks[0]
        copies[i].wait()
        product = jnp.dot(hidden, w_all[i], preferred_element_type=jnp.float32)
        parts = [
            product[e * block : (e + 1) * block, c * LANES : (c + 1) * LANES]
            for c in range(piece // LANES)
            for e in range(tokens // block)
        ]
        waiting[kind] += parts
        while len(waiting[kind]) > 1:
            even_part, odd_part = waiting[kind][:2]
            waiting[kind] = waiting[kind][2:]
            where = (owner[kind] // 2, slice(first, first + block), slice(None))
            keep_ref[where] = jnp.where(odd, odd_part, even_part)
            send_ref[where] = jnp.where(odd, even_part, odd_part)
            owner[kind] += 2


def project(me, hidden, weight, chunk, columns, others, count):
    tokens, depth = hidden.shape
    wide = [columns] + [other.shape[1] for other in others]
    blocks = [columns // LANES * tokens // count]
    if others:
        blocks.append(sum(wide[1:]) // LANES * tokens // count)
    total = sum(wide)
    piece = functools.reduce(math.gcd, wide, 2 * LANES)
    shape = jax.ShapeDtypeStruct((count // 2, sum(blocks), LANES), jnp.float32)
    return pl.pallas_call(
        functools.partial(
            project_kernel, blocks=blocks, chunk=chunk, columns=columns, extra=len(others)
        ),
        out_shape=[shape] * 2,
        in_specs=[smem_spec(), vmem_spec()] + [hbm_spec()] * (1 + len(others)),
        out_specs=[vmem_spec()] * 2,
        scratch_shapes=[
            pltpu.VMEM((total // piece, depth, piece), jnp.bfloat16),
            pltpu.SemaphoreType.DMA((total // piece,)),
        ],
        compiler_params=pltpu.CompilerParams(vmem_limit_bytes=VMEM_GRANT),
        cost_estimate=pl.CostEstimate(
            flops=2 * tokens * depth * total,
            bytes_accessed=2 * depth * total,
            transcendentals=0,
        ),
    )(me, hidden, weight, *others)


def attention_kernel(len_ref, me_ref, *refs, band, step, block, head):
    q_refs, (k_hbm, v_hbm, o_ref) = refs[:2], refs[2:5]
    k_ref, v_ref, sems = refs[5:8]
    s_bufs, m_bufs = refs[8:10], refs[10:12]
    shift, acc, lse_all = refs[12:]
    half = q_refs[0].shape[0]
    rows = 2 * half * block
    bands = rows // band
    share = band // block
    scale = math.log2(math.e) / math.sqrt(HD)
    piece = math.gcd(step, 1024)
    tiles = piece // LANES
    odd = lax.rem(me_ref[0], 2)

    length = len_ref[0]
    full = length // step
    rest = length - full * step

    def copy_in(source, target, which, i):
        where = pl.ds(pl.multiple_of(i * step, step), step)
        return pltpu.make_async_copy(
            source.at[where, pl.ds(head * HD, HD)], target.at[where, :], sems.at[which, i]
        )

    def keys_in(i):
        return copy_in(k_hbm, k_ref, 0, i)

    def values_in(i):
        return copy_in(v_hbm, v_ref, 1, i)

    needed = (length + step - 1) // step

    def start_keys(i, carry):
        keys_in(i).start()
        return carry

    def start_values(i, carry):
        values_in(i).start()
        return carry

    lax.fori_loop(0, needed, start_keys, 0)
    lax.fori_loop(0, needed, start_values, 0)

    def score(r, i, first, masked):
        source = q_refs[r * share // half]
        at = r * share % half
        q = source[at : at + share, :block, :].reshape(band, HD)
        keys = k_ref[pl.ds(pl.multiple_of(i * step + first, piece), piece), :]
        s = lax.dot_general(q, keys, NT, preferred_element_type=jnp.float32)
        if masked:
            column = first + lax.broadcasted_iota(jnp.int32, (band, piece), 1)
            s = jnp.where(column < rest, s, NEG_BIG)
        s_bufs[r % 2][i, :, first : first + piece] = s
        tops = [s[:, c * LANES : (c + 1) * LANES] for c in range(tiles)]
        while len(tops) > 1:
            tops = [jnp.maximum(a, b) for a, b in zip(tops[0::2], tops[1::2])]
        m_bufs[r % 2][...] = jnp.maximum(m_bufs[r % 2][...], tops[0])

    def weigh(r, i, first):
        s = s_bufs[r % 2][i, :, first : first + piece]
        low = shift[...]
        weights = jnp.concatenate(
            [
                jnp.exp2(s[:, c * LANES : (c + 1) * LANES] * scale - low).astype(jnp.bfloat16)
                for c in range(tiles)
            ],
            axis=1,
        )
        values = v_ref[pl.ds(pl.multiple_of(i * step + first, piece), piece), :]
        wide = jnp.concatenate([values, jnp.ones((piece, LANES), jnp.bfloat16)], axis=1)
        acc[...] += jnp.dot(weights, wide, preferred_element_type=jnp.float32)

    for r in range(bands + 1):
        scores, weighs = r < bands, r > 0
        if scores:
            m_bufs[r % 2][...] = jnp.full((band, LANES), -3e38, jnp.float32)
        if weighs:
            top = jnp.max(m_bufs[(r - 1) % 2][...], axis=1, keepdims=True)
            shift[...] = jnp.broadcast_to(top * scale, (band, LANES))
            acc[...] = jnp.zeros(acc.shape, jnp.float32)

        def both(i, masked):
            if r == 0:
                keys_in(i).wait()
            if r == 1:
                values_in(i).wait()
            for first in range(0, step, piece):
                if weighs:
                    weigh(r - 1, i, first)
                if scores:
                    score(r, i, first, masked)

        def body(i, carry):
            both(i, False)
            return carry

        lax.fori_loop(0, full, body, 0)

        @pl.when(rest > 0)
        def _():
            both(full, True)

        if weighs:
            totals = acc[:, LANES:]
            mean = acc[:, :LANES] / totals * OUTPUT_SCALE
            for e in range(share):
                k = (r - 1) * share + e
                owner = 2 * (k % half) + (odd if k < half else 1 - odd)
                o_ref[owner, :block, :] = mean[e * block : (e + 1) * block, :]
            lse_all[(r - 1) * band : r * band, :] = shift[...] + jnp.log2(totals)

    per = LANES // block
    row = lax.broadcasted_iota(jnp.int32, (STAT_ROWS, LANES), 0)
    for g in range(rows // LANES):
        level = lse_all[g * LANES : (g + 1) * LANES, :].T[:STAT_ROWS, :]
        exponent = jnp.floor(jnp.log2(jnp.maximum(jnp.abs(level), 1e-30)))
        exponent = jnp.minimum(exponent, 120.0)
        rest_of = level * jnp.exp2(-exponent)
        first = jnp.floor(rest_of * 2.0**9 + 0.5)
        rest_of = rest_of - first * 2.0**-9
        second = jnp.floor(rest_of * 2.0**20 + 0.5)
        third = (rest_of - second * 2.0**-20) * 2.0**31
        stats = jnp.where(row == 0, exponent, jnp.where(row == 1, first, second))
        stats = jnp.where(row >= 3, third, stats)
        for e in range(per):
            k = g * per + e
            owner = 2 * (k % half) + (odd if k < half else 1 - odd)
            o_ref[owner, block:, :] = stats


def attention(queries, block, keys, values, length, me, head):
    count = 2 * queries[0].shape[0]
    rows, slots = count * block, keys.shape[0]
    band = math.gcd(rows // 2, 256)
    step = math.gcd(slots, 2048)
    return pl.pallas_call(
        functools.partial(attention_kernel, band=band, step=step, block=block, head=head),
        out_shape=jax.ShapeDtypeStruct((count, block + STAT_ROWS, HD), jnp.float32),
        in_specs=[smem_spec()] * 2 + [vmem_spec()] * 2 + [hbm_spec()] * 2,
        out_specs=vmem_spec(),
        scratch_shapes=[
            pltpu.VMEM((slots, HD), jnp.bfloat16),
            pltpu.VMEM((slots, HD), jnp.bfloat16),
            pltpu.SemaphoreType.DMA((2, slots // step)),
            pltpu.VMEM((slots // step, band, step), jnp.float32),
            pltpu.VMEM((slots // step, band, step), jnp.float32),
            pltpu.VMEM((band, LANES), jnp.float32),
            pltpu.VMEM((band, LANES), jnp.float32),
            pltpu.VMEM((band, LANES), jnp.float32),
            pltpu.VMEM((band, 2 * LANES), jnp.float32),
            pltpu.VMEM((rows, LANES), jnp.float32),
        ],
        compiler_params=pltpu.CompilerParams(vmem_limit_bytes=VMEM_GRANT),
        cost_estimate=pl.CostEstimate(
            flops=8 * rows * slots * HD,
            bytes_accessed=4 * slots * HD,
            transcendentals=rows * slots,
        ),
    )(length, me, *queries, keys, values)


def merge_kernel(me_ref, part_ref, q_ref, kv_ref, o_ref, turned, *, head, kv_local, tokens):
    count = part_ref.shape[0]
    block = q_ref.shape[0]
    per = LANES // block
    scale = math.log2(math.e) / math.sqrt(HD)

    keys = kv_ref[head * tokens : (head + 1) * tokens, :]
    second = (kv_local + head) * tokens
    values = kv_ref[second : second + tokens, :]

    s = lax.dot_general(q_ref[...], keys, NT, preferred_element_type=jnp.float32) * scale
    token = lax.rem(me_ref[0] * block, tokens) + lax.broadcasted_iota(jnp.int32, s.shape, 0)
    visible = lax.broadcasted_iota(jnp.int32, s.shape, 1) <= token
    s = jnp.where(visible, s, NEG_BIG)
    new_top = jnp.max(s, axis=1, keepdims=True)
    weights = jnp.where(visible, jnp.exp2(s - new_top), 0.0).astype(jnp.bfloat16)
    new_total = jnp.sum(weights.astype(jnp.float32), axis=1, keepdims=True)
    new_out = jnp.dot(weights, values, preferred_element_type=jnp.float32)

    place = lax.rem(me_ref[0] // 2, per)
    pieces = part_ref[:, block : block + 4, :]
    level = pieces[:, 1, :] * 2.0**-9 + pieces[:, 2, :] * 2.0**-20 + pieces[:, 3, :] * 2.0**-31
    turned[...] = (level * jnp.exp2(pieces[:, 0, :])).T
    levels = turned[pl.ds(pl.multiple_of(place * block, block), block), :]
    joint = jnp.maximum(new_top, jnp.max(levels, axis=1, keepdims=True))
    factors = jnp.exp2(levels - joint)
    new_scale = jnp.exp2(new_top - joint)
    whole_out = new_out * new_scale
    whole_total = new_total * new_scale + jnp.sum(factors, axis=1, keepdims=True)
    scaled = factors * (1.0 / OUTPUT_SCALE)
    for k in range(count):
        whole_out = whole_out + part_ref[k, :block, :] * scaled[:, k : k + 1]
    o_ref[...] = (whole_out / whole_total).astype(jnp.bfloat16)


def merge(me, parts, q_mine, kv, head, kv_local, tokens):
    return pl.pallas_call(
        functools.partial(merge_kernel, head=head, kv_local=kv_local, tokens=tokens),
        out_shape=jax.ShapeDtypeStruct(q_mine.shape, jnp.bfloat16),
        in_specs=[smem_spec()] + [vmem_spec()] * 3,
        out_specs=vmem_spec(),
        scratch_shapes=[pltpu.VMEM((LANES, parts.shape[0]), jnp.float32)],
    )(me, parts, q_mine, kv)


def output_kernel(me_ref, w_ref, *refs, tokens, groups, has_before, chunk):
    a_refs = refs[:2]
    before = refs[2] if has_before else None
    o_ref, w_all, a_all, sems = refs[-4:]
    copies = []
    for g in range(groups):
        copies.append(
            pltpu.make_async_copy(
                w_ref.at[pl.ds((chunk * groups + g) * HD, HD), :],
                w_all.at[pl.ds(g * HD, HD), :],
                sems.at[g],
            )
        )
        copies[-1].start()
    half, block = a_refs[0].shape[:2]
    per = tokens // block
    odd = lax.rem(me_ref[0], 2)
    for a_ref, parity in zip(a_refs, (odd, 1 - odd)):
        for k in range(half):
            owner = 2 * k + parity
            start = pl.multiple_of(lax.rem(owner, per) * block, block)
            a_all[owner // per, pl.ds(start, block), :] = a_ref[k]
    rows = jnp.concatenate([a_all[g] for g in range(groups)], axis=1)
    for copy in copies:
        copy.wait()
    product = jnp.dot(rows, w_all[...], preferred_element_type=jnp.float32)
    if has_before:
        product = product + before[...]
    o_ref[...] = product


def output_part(me, weight, attended, tokens, before, chunk):
    groups = QH // KVH
    width = weight.shape[1]
    has_before = before is not None
    return pl.pallas_call(
        functools.partial(
            output_kernel, tokens=tokens, groups=groups, has_before=has_before, chunk=chunk
        ),
        out_shape=jax.ShapeDtypeStruct((tokens, width), jnp.float32),
        in_specs=[smem_spec(), hbm_spec()] + [vmem_spec()] * (2 + int(has_before)),
        out_specs=vmem_spec(),
        scratch_shapes=[
            pltpu.VMEM((groups * HD, width), jnp.bfloat16),
            pltpu.VMEM((groups, tokens, HD), jnp.bfloat16),
            pltpu.SemaphoreType.DMA((groups,)),
        ],
        compiler_params=pltpu.CompilerParams(vmem_limit_bytes=VMEM_GRANT),
        cost_estimate=pl.CostEstimate(
            flops=2 * tokens * groups * HD * width,
            bytes_accessed=2 * groups * HD * width,
            transcendentals=0,
        ),
    )(me, weight, *attended, *([before] if has_before else []))


def shards(
    hidden,
    query_weight,
    key_weight,
    value_weight,
    output_weight,
    cache_keys,
    cache_values,
    cache_lens,
):
    tokens = hidden.shape[0]
    count = lax.axis_size("seq")
    heads = lax.axis_size("head")
    kv_local = cache_keys.shape[1] // HD
    columns = (QH // KVH) * HD
    block = (QH // KVH) * tokens // count
    me = lax.axis_index("seq").reshape(1)

    mine = []
    for j in range(kv_local):
        others = [key_weight, value_weight] if j == kv_local - 1 else []
        keep, send = project(me, hidden, query_weight, j, columns, others, count)
        total = jnp.sum(within_parity(keep + with_partner(send)), axis=0)
        mine.append(total.astype(jnp.bfloat16))
    queries = [spread(rows) for rows in mine]
    same, other = (rows[:, None, block:, :] for rows in queries[-1])
    even = jnp.concatenate([same, other], axis=1)
    odd = jnp.concatenate([other, same], axis=1)
    kv = jnp.where(me[0] % 2 == 0, even, odd).reshape(-1, HD)

    mixed = None
    for j in range(kv_local):
        parts = attention(queries[j], block, cache_keys, cache_values, cache_lens, me, j)
        parts = lax.all_to_all(parts.astype(jnp.float16), "seq", 0, 0).astype(jnp.float32)
        attended = merge(me, parts, mine[j][:block], kv, j, kv_local, tokens)
        mixed = output_part(me, output_weight, spread(attended), tokens, mixed, j)

    mixed = (mixed * MIXED_SCALE).reshape(heads, tokens // heads, mixed.shape[1])
    mixed = jnp.sum(
        lax.all_to_all(mixed.astype(jnp.float16), "head", 0, 0).astype(jnp.float32), axis=0
    )
    return (mixed * (1.0 / MIXED_SCALE)).astype(jnp.bfloat16)


def solution(mesh):
    placed = (
        P(None, "seq"),
        P("seq", "head"),
        P("seq", "head"),
        P("seq", "head"),
        P("head", "seq"),
        P("seq", "head"),
        P("seq", "head"),
        P("seq"),
    )
    return jax.shard_map(
        shards, mesh=mesh, in_specs=placed, out_specs=P("head", "seq"), check_vma=False
    )
```

```python
import functools
import math

import jax
import jax.numpy as jnp
from jax import lax
from jax.experimental import pallas as pl
from jax.experimental.pallas import tpu as pltpu
from jax.sharding import PartitionSpec as P

QH = 64
KVH = 8
HD = 128

NEG_BIG = -1e30
LANES = 128
STAT_ROWS = 8
VMEM_GRANT = 51 << 20
NT = (((1,), (1,)), ((), ()))

OUTPUT_SCALE = 2.0**12
MIXED_SCALE = 2.0**-3


def vmem_spec():
    return pl.BlockSpec(memory_space=pltpu.VMEM)


def smem_spec():
    return pl.BlockSpec(memory_space=pltpu.SMEM)


def hbm_spec():
    return pl.BlockSpec(memory_space=pl.ANY)


def swap(array, axis, mask):
    size = lax.axis_size(axis)
    return lax.ppermute(array, axis, [(i, i ^ mask) for i in range(size)])


def within_parity(array):
    size = lax.axis_size("seq")
    groups = [list(range(first, size, 2)) for first in range(2)]
    return lax.all_to_all(array, "seq", 0, 0, axis_index_groups=groups)


def spread(copies):
    if copies.shape[0] == lax.axis_size("seq"):
        return [lax.all_to_all(copies, "seq", 0, 0)]
    same = within_parity(copies)
    return [same, swap(same, "seq", 1)]


def project_kernel(me_ref, hidden_ref, q_hbm, k_hbm, v_hbm, *refs, chunks, blocks, pieces):
    outs = refs[: 2 * chunks]
    q_all, k_all, v_all, total, sems = refs[2 * chunks :]
    tokens, depth = hidden_ref.shape
    odd = lax.rem(me_ref[0], 2) == 1
    rows = depth // pieces
    copies = [
        pltpu.make_async_copy(
            q_hbm.at[pl.ds(i * rows, rows), :], q_all.at[pl.ds(i * rows, rows), :], sems.at[i]
        )
        for i in range(pieces)
    ]
    copies.append(pltpu.make_async_copy(k_hbm, k_all, sems.at[pieces]))
    copies.append(pltpu.make_async_copy(v_hbm, v_all, sems.at[pieces + 1]))
    for copy in copies:
        copy.start()

    def deal(product, chunk, kind):
        block = blocks[kind]
        first = kind * blocks[0]
        parts = [
            product[e * block : (e + 1) * block, c * LANES : (c + 1) * LANES]
            for c in range(product.shape[1] // LANES)
            for e in range(tokens // block)
        ]
        keep_ref, send_ref = outs[2 * chunk : 2 * chunk + 2]
        for i, (even_part, odd_part) in enumerate(zip(parts[0::2], parts[1::2])):
            keep_ref[i, first : first + block, :] = jnp.where(odd, odd_part, even_part)
            send_ref[i, first : first + block, :] = jnp.where(odd, even_part, odd_part)

    columns = q_all.shape[1] // chunks
    for i in range(pieces):
        copies[i].wait()
        h = hidden_ref[:, i * rows : (i + 1) * rows]
        for j in range(chunks):
            w = q_all[i * rows : (i + 1) * rows, j * columns : (j + 1) * columns]
            product = jnp.dot(h, w, preferred_element_type=jnp.float32)
            if i > 0:
                product = product + total[j]
            if i < pieces - 1:
                total[j] = product
            else:
                deal(product, j, 0)
    copies[pieces].wait()
    copies[pieces + 1].wait()
    both = [
        jnp.dot(hidden_ref[...], w_all[...], preferred_element_type=jnp.float32)
        for w_all in (k_all, v_all)
    ]
    deal(jnp.concatenate(both, axis=1), chunks - 1, 1)


def project(me, hidden, query_weight, key_weight, value_weight, chunks, count):
    tokens, depth = hidden.shape
    wide, narrow = query_weight.shape[1], key_weight.shape[1]
    pieces = max(1, depth // 256)
    blocks = (wide // chunks // LANES * tokens // count, 2 * narrow // LANES * tokens // count)
    shapes = []
    for j in range(chunks):
        rows = blocks[0] + (blocks[1] if j == chunks - 1 else 0)
        shapes += [jax.ShapeDtypeStruct((count // 2, rows, LANES), jnp.float32)] * 2
    return pl.pallas_call(
        functools.partial(project_kernel, chunks=chunks, blocks=blocks, pieces=pieces),
        out_shape=shapes,
        in_specs=[smem_spec(), vmem_spec()] + [hbm_spec()] * 3,
        out_specs=[vmem_spec()] * len(shapes),
        scratch_shapes=[
            pltpu.VMEM((depth, wide), jnp.bfloat16),
            pltpu.VMEM((depth, narrow), jnp.bfloat16),
            pltpu.VMEM((depth, narrow), jnp.bfloat16),
            pltpu.VMEM((chunks, tokens, wide // chunks), jnp.float32),
            pltpu.SemaphoreType.DMA((pieces + 2,)),
        ],
        compiler_params=pltpu.CompilerParams(vmem_limit_bytes=VMEM_GRANT),
        cost_estimate=pl.CostEstimate(
            flops=2 * tokens * depth * (wide + 2 * narrow),
            bytes_accessed=2 * depth * (wide + 2 * narrow),
            transcendentals=0,
        ),
    )(me, hidden, query_weight, key_weight, value_weight)


def collect_kernel(part_ref, copies_ref):
    total = part_ref[0]
    for k in range(1, part_ref.shape[0]):
        total = total + part_ref[k]
    total = total.astype(jnp.bfloat16)
    for k in range(copies_ref.shape[0]):
        copies_ref[k] = total


def collect(parts, copies):
    return pl.pallas_call(
        collect_kernel,
        out_shape=jax.ShapeDtypeStruct((copies,) + parts.shape[1:], jnp.bfloat16),
        in_specs=[vmem_spec()],
        out_specs=vmem_spec(),
    )(parts)


def attention_kernel(len_ref, me_ref, *refs, sources, band, step, block, head):
    q_refs, refs = refs[:sources], refs[sources:]
    k_hbm, v_hbm, o_ref, k_ref, v_ref, sems = refs[:6]
    s_bufs, m_bufs = refs[6:8], refs[8:10]
    shift, acc, lse_all = refs[10:]
    half = q_refs[0].shape[0]
    rows = sources * half * block
    bands = rows // band
    share = band // block
    scale = math.log2(math.e) / math.sqrt(HD)
    piece = math.gcd(step, 1024)
    tiles = piece // LANES
    odd = lax.rem(me_ref[0], 2)
    lanes = slice(head * HD, (head + 1) * HD)

    def owner_of(k):
        return k if sources == 1 else 2 * (k % half) + (odd if k < half else 1 - odd)

    length = len_ref[0]
    full = length // step
    rest = length - full * step

    def copy_in(source, target, which, i):
        where = pl.ds(pl.multiple_of(i * step, step), step)
        return pltpu.make_async_copy(
            source.at[where, :], target.at[where, :], sems.at[which, i]
        )

    def keys_in(i):
        return copy_in(k_hbm, k_ref, 0, i)

    def values_in(i):
        return copy_in(v_hbm, v_ref, 1, i)

    needed = (length + step - 1) // step

    def start_keys(i, carry):
        keys_in(i).start()
        return carry

    def start_values(i, carry):
        values_in(i).start()
        return carry

    lax.fori_loop(0, needed, start_keys, 0)
    lax.fori_loop(0, needed, start_values, 0)

    def score(r, i, first, masked):
        source = q_refs[r * share // half]
        at = r * share % half
        q = source[at : at + share, :block, :].reshape(band, HD)
        keys = k_ref[pl.ds(pl.multiple_of(i * step + first, piece), piece), lanes]
        s = lax.dot_general(q, keys, NT, preferred_element_type=jnp.float32)
        if masked:
            column = first + lax.broadcasted_iota(jnp.int32, (band, piece), 1)
            s = jnp.where(column < rest, s, NEG_BIG)
        s_bufs[r % 2][i, :, first : first + piece] = s
        tops = [s[:, c * LANES : (c + 1) * LANES] for c in range(tiles)]
        while len(tops) > 1:
            tops = [jnp.maximum(a, b) for a, b in zip(tops[0::2], tops[1::2])]
        m_bufs[r % 2][...] = jnp.maximum(m_bufs[r % 2][...], tops[0])

    def weigh(r, i, first):
        s = s_bufs[r % 2][i, :, first : first + piece]
        low = shift[...]
        weights = jnp.concatenate(
            [
                jnp.exp2(s[:, c * LANES : (c + 1) * LANES] * scale - low).astype(jnp.bfloat16)
                for c in range(tiles)
            ],
            axis=1,
        )
        values = v_ref[pl.ds(pl.multiple_of(i * step + first, piece), piece), lanes]
        wide = jnp.concatenate([values, jnp.ones((piece, LANES), jnp.bfloat16)], axis=1)
        acc[...] += jnp.dot(weights, wide, preferred_element_type=jnp.float32)

    for r in range(bands + 1):
        scores, weighs = r < bands, r > 0
        if scores:
            m_bufs[r % 2][...] = jnp.full((band, LANES), -3e38, jnp.float32)
        if weighs:
            top = jnp.max(m_bufs[(r - 1) % 2][...], axis=1, keepdims=True)
            shift[...] = jnp.broadcast_to(top * scale, (band, LANES))
            acc[...] = jnp.zeros(acc.shape, jnp.float32)

        def both(i, masked):
            if r == 0:
                keys_in(i).wait()
            if r == 1:
                values_in(i).wait()
            for first in range(0, step, piece):
                if weighs:
                    weigh(r - 1, i, first)
                if scores:
                    score(r, i, first, masked)

        def body(i, carry):
            both(i, False)
            return carry

        lax.fori_loop(0, full, body, 0)

        @pl.when(rest > 0)
        def _():
            both(full, True)

        if weighs:
            totals = acc[:, LANES:]
            mean = acc[:, :LANES] / totals * OUTPUT_SCALE
            for e in range(share):
                k = (r - 1) * share + e
                o_ref[owner_of(k), :block, :] = mean[e * block : (e + 1) * block, :]
            lse_all[(r - 1) * band : r * band, :] = shift[...] + jnp.log2(totals)

    per = LANES // block
    row = lax.broadcasted_iota(jnp.int32, (STAT_ROWS, LANES), 0)
    for g in range(rows // LANES):
        level = lse_all[g * LANES : (g + 1) * LANES, :].T[:STAT_ROWS, :]
        exponent = jnp.floor(jnp.log2(jnp.maximum(jnp.abs(level), 1e-30)))
        exponent = jnp.minimum(exponent, 120.0)
        rest_of = level * jnp.exp2(-exponent)
        first = jnp.floor(rest_of * 2.0**9 + 0.5)
        rest_of = rest_of - first * 2.0**-9
        second = jnp.floor(rest_of * 2.0**20 + 0.5)
        third = (rest_of - second * 2.0**-20) * 2.0**31
        stats = jnp.where(row == 0, exponent, jnp.where(row == 1, first, second))
        stats = jnp.where(row >= 3, third, stats)
        for e in range(per):
            k = g * per + e
            o_ref[owner_of(k), block:, :] = stats


def attention(queries, block, keys, values, length, me, head):
    sources = len(queries)
    count = sources * queries[0].shape[0]
    rows, slots = count * block, keys.shape[0]
    band = math.gcd(rows // 2, 256)
    step = math.gcd(slots, 2048)
    return pl.pallas_call(
        functools.partial(
            attention_kernel, sources=sources, band=band, step=step, block=block, head=head
        ),
        out_shape=jax.ShapeDtypeStruct((count, block + STAT_ROWS, HD), jnp.float32),
        in_specs=[smem_spec()] * 2 + [vmem_spec()] * sources + [hbm_spec()] * 2,
        out_specs=vmem_spec(),
        scratch_shapes=[
            pltpu.VMEM(keys.shape, keys.dtype),
            pltpu.VMEM(values.shape, values.dtype),
            pltpu.SemaphoreType.DMA((2, slots // step)),
            pltpu.VMEM((slots // step, band, step), jnp.float32),
            pltpu.VMEM((slots // step, band, step), jnp.float32),
            pltpu.VMEM((band, LANES), jnp.float32),
            pltpu.VMEM((band, LANES), jnp.float32),
            pltpu.VMEM((band, LANES), jnp.float32),
            pltpu.VMEM((band, 2 * LANES), jnp.float32),
            pltpu.VMEM((rows, LANES), jnp.float32),
        ],
        compiler_params=pltpu.CompilerParams(vmem_limit_bytes=VMEM_GRANT),
        cost_estimate=pl.CostEstimate(
            flops=8 * rows * slots * HD,
            bytes_accessed=4 * slots * HD,
            transcendentals=rows * slots,
        ),
    )(length, me, *queries, keys, values)


def merge_kernel(me_ref, part_ref, q_ref, last_ref, copies_ref, turned, kv_all, *, block, tokens, head):
    count = part_ref.shape[0]
    per = LANES // block
    kv_block = last_ref.shape[1] - block
    scale = math.log2(math.e) / math.sqrt(HD)

    for k in range(count):
        rows = last_ref[k, block:, :].astype(jnp.float32)
        kv_all[k * kv_block : (k + 1) * kv_block, :] = rows
    half = kv_all.shape[0] // 2
    keys = kv_all[head * tokens : (head + 1) * tokens, :].astype(jnp.bfloat16)
    values = kv_all[half + head * tokens : half + (head + 1) * tokens, :].astype(jnp.bfloat16)

    s = lax.dot_general(q_ref[0, :block, :], keys, NT, preferred_element_type=jnp.float32) * scale
    token = lax.rem(me_ref[0] * block, tokens) + lax.broadcasted_iota(jnp.int32, s.shape, 0)
    visible = lax.broadcasted_iota(jnp.int32, s.shape, 1) <= token
    s = jnp.where(visible, s, NEG_BIG)
    new_top = jnp.max(s, axis=1, keepdims=True)
    weights = jnp.where(visible, jnp.exp2(s - new_top), 0.0).astype(jnp.bfloat16)
    new_total = jnp.sum(weights.astype(jnp.float32), axis=1, keepdims=True)
    new_out = jnp.dot(weights, values, preferred_element_type=jnp.float32)

    place = lax.rem(me_ref[0] // 2, per)
    pieces = part_ref[:, block : block + 4, :]
    level = pieces[:, 1, :] * 2.0**-9 + pieces[:, 2, :] * 2.0**-20 + pieces[:, 3, :] * 2.0**-31
    turned[...] = (level * jnp.exp2(pieces[:, 0, :])).T
    levels = turned[pl.ds(pl.multiple_of(place * block, block), block), :]
    joint = jnp.maximum(new_top, jnp.max(levels, axis=1, keepdims=True))
    factors = jnp.exp2(levels - joint)
    new_scale = jnp.exp2(new_top - joint)
    whole_out = new_out * new_scale
    whole_total = new_total * new_scale + jnp.sum(factors, axis=1, keepdims=True)
    scaled = factors * (1.0 / OUTPUT_SCALE)
    for k in range(count):
        whole_out = whole_out + part_ref[k, :block, :] * scaled[:, k : k + 1]
    attended = (whole_out / whole_total).astype(jnp.bfloat16)
    for k in range(count):
        copies_ref[k] = attended


def merge(me, parts, mine, last, block, tokens, head):
    count = parts.shape[0]
    kv_rows = count * (last.shape[1] - block)
    return pl.pallas_call(
        functools.partial(merge_kernel, block=block, tokens=tokens, head=head),
        out_shape=jax.ShapeDtypeStruct((count, block, HD), jnp.bfloat16),
        in_specs=[smem_spec()] + [vmem_spec()] * 3,
        out_specs=vmem_spec(),
        scratch_shapes=[
            pltpu.VMEM((LANES, count), jnp.float32),
            pltpu.VMEM((kv_rows, HD), jnp.float32),
        ],
    )(me, parts, mine, last)


def output_kernel(place_ref, w_hbm, a_ref, *refs, tokens, groups, chunk, has_before, last):
    before = refs[0] if has_before else None
    outs, (w_all, total, sems) = refs[int(has_before) : -3], refs[-3:]
    copies = []
    for g in range(groups):
        copies.append(
            pltpu.make_async_copy(
                w_hbm.at[pl.ds((chunk * groups + g) * HD, HD), :],
                w_all.at[pl.ds(g * HD, HD), :],
                sems.at[g],
            )
        )
        copies[-1].start()
    per = a_ref.shape[0] // groups
    pieces = [a_ref[g * per : (g + 1) * per].reshape(tokens, HD) for g in range(groups)]
    product = before[...] if has_before else None
    for g in range(0, groups, 2):
        copies[g].wait()
        copies[g + 1].wait()
        term = jnp.dot(
            jnp.concatenate(pieces[g : g + 2], axis=1),
            w_all[g * HD : (g + 2) * HD, :],
            preferred_element_type=jnp.float32,
        )
        product = term if product is None else product + term
    if not last:
        outs[0][...] = product
        return
    total[...] = product
    keep_ref, send_ref = outs
    share = keep_ref.shape[1]
    odd = lax.rem(place_ref[0], 2)
    for i in range(keep_ref.shape[0]):
        for ref, parity in ((keep_ref, odd), (send_ref, 1 - odd)):
            start = pl.multiple_of((2 * i + parity) * share, share)
            ref[i] = total[pl.ds(start, share), :]


def output_part(place, weight, attended, tokens, before, chunk, heads, last):
    groups = QH // KVH
    width = weight.shape[1]
    has_before = before is not None
    shapes = [jax.ShapeDtypeStruct((tokens, width), jnp.float32)]
    if last:
        shapes = [jax.ShapeDtypeStruct((heads // 2, tokens // heads, width), jnp.float32)] * 2
    return pl.pallas_call(
        functools.partial(
            output_kernel,
            tokens=tokens,
            groups=groups,
            chunk=chunk,
            has_before=has_before,
            last=last,
        ),
        out_shape=shapes,
        in_specs=[smem_spec(), hbm_spec()] + [vmem_spec()] * (1 + int(has_before)),
        out_specs=[vmem_spec()] * len(shapes),
        scratch_shapes=[
            pltpu.VMEM((groups * HD, width), jnp.bfloat16),
            pltpu.VMEM((tokens, width), jnp.float32),
            pltpu.SemaphoreType.DMA((groups,)),
        ],
        compiler_params=pltpu.CompilerParams(vmem_limit_bytes=VMEM_GRANT),
        cost_estimate=pl.CostEstimate(
            flops=2 * tokens * groups * HD * width,
            bytes_accessed=2 * groups * HD * width,
            transcendentals=0,
        ),
    )(place, weight, attended, *([before] if has_before else []))


def shards(
    hidden,
    query_weight,
    key_weight,
    value_weight,
    output_weight,
    cache_keys,
    cache_values,
    cache_lens,
):
    tokens = hidden.shape[0]
    count = lax.axis_size("seq")
    heads = lax.axis_size("head")
    kv_local = cache_keys.shape[1] // HD
    block = (QH // KVH) * tokens // count
    me = lax.axis_index("seq").reshape(1)
    place = lax.axis_index("head").reshape(1)

    halves = project(me, hidden, query_weight, key_weight, value_weight, kv_local, count)
    mine = []
    for j in range(kv_local):
        keep, send = halves[2 * j : 2 * j + 2]
        parts = within_parity(keep + swap(send, "seq", 1))
        mine.append(collect(parts, count if j == kv_local - 1 else count // 2))
    queries = [spread(copies) for copies in mine]

    mixed = None
    for j in range(kv_local):
        parts = attention(queries[j], block, cache_keys, cache_values, cache_lens, me, j)
        parts = lax.all_to_all(parts.astype(jnp.float16), "seq", 0, 0).astype(jnp.float32)
        copies = merge(me, parts, mine[j], queries[-1][0], block, tokens, j)
        last = j == kv_local - 1
        result = output_part(
            place, output_weight, spread(copies)[0], tokens, mixed, j, heads, last
        )
        mixed = result if last else result[0]

    keep, send = mixed
    mixed = keep + swap(send, "head", 1)
    mask = 2
    while mask < heads:
        bit = place[0] // mask % 2
        pairs = mixed.reshape((-1, 2) + mixed.shape[1:])
        keep = lax.dynamic_index_in_dim(pairs, bit, 1, False)
        send = lax.dynamic_index_in_dim(pairs, 1 - bit, 1, False) * MIXED_SCALE
        received = swap(send.astype(jnp.float16), "head", mask).astype(jnp.float32)
        mixed = keep + received * (1.0 / MIXED_SCALE)
        mask *= 2
    return mixed[0].astype(jnp.bfloat16)


def solution(mesh):
    placed = (
        P(None, "seq"),
        P("seq", "head"),
        P("seq", "head"),
        P("seq", "head"),
        P("head", "seq"),
        P("seq", "head"),
        P("seq", "head"),
        P("seq"),
    )
    return jax.shard_map(
        shards, mesh=mesh, in_specs=placed, out_specs=P("head", "seq"), check_vma=False
    )
```

```python
import functools
import math

import jax
import jax.numpy as jnp
from jax import lax
from jax.experimental import pallas as pl
from jax.experimental.pallas import tpu as pltpu
from jax.sharding import PartitionSpec as P

QH = 64
KVH = 8
HD = 128

NEG_BIG = -1e30
LANES = 128
STAT_ROWS = 8
VMEM_GRANT = 51 << 20
PROJECT_GRANT = 56 << 20
NT = (((1,), (1,)), ((), ()))

OUTPUT_SCALE = 2.0**12
MIXED_SCALE = 2.0**-3


def vmem_spec():
    return pl.BlockSpec(memory_space=pltpu.VMEM)


def smem_spec():
    return pl.BlockSpec(memory_space=pltpu.SMEM)


def hbm_spec():
    return pl.BlockSpec(memory_space=pl.ANY)


def swap(array, axis, mask):
    size = lax.axis_size(axis)
    return lax.ppermute(array, axis, [(i, i ^ mask) for i in range(size)])


def owners_sum(keep, send, me):
    total = keep + swap(send, "seq", 1)
    mask = 2
    while mask < lax.axis_size("seq"):
        bit = me // mask % 2
        pairs = total.reshape((-1, 2) + total.shape[1:])
        keep = lax.dynamic_index_in_dim(pairs, bit, 1, False)
        send = lax.dynamic_index_in_dim(pairs, 1 - bit, 1, False)
        total = keep + swap(send, "seq", mask)
        mask *= 2
    return total.astype(jnp.bfloat16)


def doubling_masks(size):
    masks = []
    while size > 2:
        size //= 2
        masks.append(size)
    return masks


def gather_doubling(block):
    for mask in doubling_masks(lax.axis_size("seq")):
        block = jnp.concatenate([block, swap(block, "seq", mask)])
    return [block, swap(block, "seq", 1)]


def doubling_offsets(size):
    offsets = [0]
    for mask in doubling_masks(size):
        offsets = offsets + [offset ^ mask for offset in offsets]
    return offsets + [offset ^ 1 for offset in offsets]


def gather_at_once(copies):
    return lax.all_to_all(copies, "seq", 0, 0)


def project_kernel(me_ref, hidden_ref, q_hbm, k_hbm, v_hbm, *refs, chunks, blocks, pieces):
    outs = refs[: 2 * chunks]
    q_all, k_all, v_all, total, sems = refs[2 * chunks :]
    tokens, depth = hidden_ref.shape
    odd = lax.rem(me_ref[0], 2) == 1
    rows = depth // pieces
    copies = [
        pltpu.make_async_copy(
            q_hbm.at[pl.ds(i * rows, rows), :], q_all.at[pl.ds(i * rows, rows), :], sems.at[i]
        )
        for i in range(pieces)
    ]
    copies.append(pltpu.make_async_copy(k_hbm, k_all, sems.at[pieces]))
    copies.append(pltpu.make_async_copy(v_hbm, v_all, sems.at[pieces + 1]))
    for copy in copies:
        copy.start()

    def deal(product, chunk, kind):
        block = blocks[kind]
        first = kind * blocks[0]
        parts = [
            product[e * block : (e + 1) * block, c * LANES : (c + 1) * LANES]
            for c in range(product.shape[1] // LANES)
            for e in range(tokens // block)
        ]
        keep_ref, send_ref = outs[2 * chunk : 2 * chunk + 2]
        for i, (even_part, odd_part) in enumerate(zip(parts[0::2], parts[1::2])):
            keep_ref[i, first : first + block, :] = jnp.where(odd, odd_part, even_part)
            send_ref[i, first : first + block, :] = jnp.where(odd, even_part, odd_part)

    columns = q_all.shape[1] // chunks
    for i in range(pieces):
        copies[i].wait()
        h = hidden_ref[:, i * rows : (i + 1) * rows]
        for j in range(chunks):
            w = q_all[i * rows : (i + 1) * rows, j * columns : (j + 1) * columns]
            product = jnp.dot(h, w, preferred_element_type=jnp.float32)
            if i > 0:
                product = product + total[j]
            if i < pieces - 1:
                total[j] = product
            else:
                deal(product, j, 0)
    copies[pieces].wait()
    copies[pieces + 1].wait()
    both = [
        jnp.dot(hidden_ref[...], w_all[...], preferred_element_type=jnp.float32)
        for w_all in (k_all, v_all)
    ]
    deal(jnp.concatenate(both, axis=1), chunks - 1, 1)


def project(me, hidden, query_weight, key_weight, value_weight, chunks, count):
    tokens, depth = hidden.shape
    wide, narrow = query_weight.shape[1], key_weight.shape[1]
    pieces = max(1, depth // 256)
    blocks = (wide // chunks // LANES * tokens // count, 2 * narrow // LANES * tokens // count)
    shapes = []
    for j in range(chunks):
        rows = blocks[0] + (blocks[1] if j == chunks - 1 else 0)
        shapes += [jax.ShapeDtypeStruct((count // 2, rows, LANES), jnp.float32)] * 2
    return pl.pallas_call(
        functools.partial(project_kernel, chunks=chunks, blocks=blocks, pieces=pieces),
        out_shape=shapes,
        in_specs=[smem_spec(), vmem_spec()] + [hbm_spec()] * 3,
        out_specs=[vmem_spec()] * len(shapes),
        scratch_shapes=[
            pltpu.VMEM((depth, wide), jnp.bfloat16),
            pltpu.VMEM((depth, narrow), jnp.bfloat16),
            pltpu.VMEM((depth, narrow), jnp.bfloat16),
            pltpu.VMEM((chunks, tokens, wide // chunks), jnp.float32),
            pltpu.SemaphoreType.DMA((pieces + 2,)),
        ],
        compiler_params=pltpu.CompilerParams(vmem_limit_bytes=PROJECT_GRANT),
        cost_estimate=pl.CostEstimate(
            flops=2 * tokens * depth * (wide + 2 * narrow),
            bytes_accessed=2 * depth * (wide + 2 * narrow),
            transcendentals=0,
        ),
    )(me, hidden, query_weight, key_weight, value_weight)


def attention_kernel(len_ref, me_ref, *refs, sources, band, step, block, head):
    q_refs, refs = refs[:sources], refs[sources:]
    k_hbm, v_hbm, o_ref, k_ref, v_ref, sems = refs[:6]
    s_bufs, m_bufs = refs[6:8], refs[8:10]
    shift, acc, lse_all = refs[10:]
    half = q_refs[0].shape[0]
    rows = sources * half * block
    bands = rows // band
    share = band // block
    scale = math.log2(math.e) / math.sqrt(HD)
    piece = math.gcd(step, 1024)
    tiles = piece // LANES
    lanes = slice(head * HD, (head + 1) * HD)
    offsets = doubling_offsets(sources * half)

    def owner_of(k):
        return k if sources == 1 else me_ref[0] ^ offsets[k]

    length = len_ref[0]
    full = length // step
    rest = length - full * step

    def copy_in(source, target, which, i):
        where = pl.ds(pl.multiple_of(i * step, step), step)
        return pltpu.make_async_copy(
            source.at[where, :], target.at[where, :], sems.at[which, i]
        )

    def keys_in(i):
        return copy_in(k_hbm, k_ref, 0, i)

    def values_in(i):
        return copy_in(v_hbm, v_ref, 1, i)

    needed = (length + step - 1) // step

    def start_keys(i, carry):
        keys_in(i).start()
        return carry

    def start_values(i, carry):
        values_in(i).start()
        return carry

    lax.fori_loop(0, needed, start_keys, 0)
    lax.fori_loop(0, needed, start_values, 0)

    def score(r, i, first, masked):
        source = q_refs[r * share // half]
        at = r * share % half
        q = source[at : at + share, :block, :].reshape(band, HD)
        keys = k_ref[pl.ds(pl.multiple_of(i * step + first, piece), piece), lanes]
        s = lax.dot_general(q, keys, NT, preferred_element_type=jnp.float32)
        if masked:
            column = first + lax.broadcasted_iota(jnp.int32, (band, piece), 1)
            s = jnp.where(column < rest, s, NEG_BIG)
        s_bufs[r % 2][i, :, first : first + piece] = s
        tops = [s[:, c * LANES : (c + 1) * LANES] for c in range(tiles)]
        while len(tops) > 1:
            tops = [jnp.maximum(a, b) for a, b in zip(tops[0::2], tops[1::2])]
        m_bufs[r % 2][...] = jnp.maximum(m_bufs[r % 2][...], tops[0])

    def weigh(r, i, first):
        s = s_bufs[r % 2][i, :, first : first + piece]
        low = shift[...]
        weights = jnp.concatenate(
            [
                jnp.exp2(s[:, c * LANES : (c + 1) * LANES] * scale - low).astype(jnp.bfloat16)
                for c in range(tiles)
            ],
            axis=1,
        )
        values = v_ref[pl.ds(pl.multiple_of(i * step + first, piece), piece), lanes]
        wide = jnp.concatenate([values, jnp.ones((piece, LANES), jnp.bfloat16)], axis=1)
        acc[...] += jnp.dot(weights, wide, preferred_element_type=jnp.float32)

    for r in range(bands + 1):
        scores, weighs = r < bands, r > 0
        if scores:
            m_bufs[r % 2][...] = jnp.full((band, LANES), -3e38, jnp.float32)
        if weighs:
            top = jnp.max(m_bufs[(r - 1) % 2][...], axis=1, keepdims=True)
            shift[...] = jnp.broadcast_to(top * scale, (band, LANES))
            acc[...] = jnp.zeros(acc.shape, jnp.float32)

        def both(i, masked):
            if r == 0:
                keys_in(i).wait()
            if r == 1:
                values_in(i).wait()
            for first in range(0, step, piece):
                if weighs:
                    weigh(r - 1, i, first)
                if scores:
                    score(r, i, first, masked)

        def body(i, carry):
            both(i, False)
            return carry

        lax.fori_loop(0, full, body, 0)

        @pl.when(rest > 0)
        def _():
            both(full, True)

        if weighs:
            totals = acc[:, LANES:]
            mean = acc[:, :LANES] / totals * OUTPUT_SCALE
            levels = shift[...] + jnp.log2(totals)
            for e in range(share):
                k = (r - 1) * share + e
                owner = owner_of(k)
                here = slice(e * block, (e + 1) * block)
                o_ref[owner, :block, :] = mean[here, :]
                lse_all[pl.ds(pl.multiple_of(owner * block, block), block), :] = levels[here, :]

    per = LANES // block
    row = lax.broadcasted_iota(jnp.int32, (STAT_ROWS, LANES), 0)
    for g in range(rows // LANES):
        level = lse_all[g * LANES : (g + 1) * LANES, :].T[:STAT_ROWS, :]
        exponent = jnp.floor(jnp.log2(jnp.maximum(jnp.abs(level), 1e-30)))
        exponent = jnp.minimum(exponent, 120.0)
        rest_of = level * jnp.exp2(-exponent)
        first = jnp.floor(rest_of * 2.0**9 + 0.5)
        rest_of = rest_of - first * 2.0**-9
        second = jnp.floor(rest_of * 2.0**20 + 0.5)
        third = (rest_of - second * 2.0**-20) * 2.0**31
        stats = jnp.where(row == 0, exponent, jnp.where(row == 1, first, second))
        stats = jnp.where(row >= 3, third, stats)
        for e in range(per):
            o_ref[g * per + e, block:, :] = stats


def attention(queries, block, keys, values, length, me, head):
    sources = len(queries)
    count = sources * queries[0].shape[0]
    rows, slots = count * block, keys.shape[0]
    band = math.gcd(rows // 2, 512)
    step = math.gcd(slots, 2048)
    return pl.pallas_call(
        functools.partial(
            attention_kernel, sources=sources, band=band, step=step, block=block, head=head
        ),
        out_shape=jax.ShapeDtypeStruct((count, block + STAT_ROWS, HD), jnp.float32),
        in_specs=[smem_spec()] * 2 + [vmem_spec()] * sources + [hbm_spec()] * 2,
        out_specs=vmem_spec(),
        scratch_shapes=[
            pltpu.VMEM(keys.shape, keys.dtype),
            pltpu.VMEM(values.shape, values.dtype),
            pltpu.SemaphoreType.DMA((2, slots // step)),
            pltpu.VMEM((slots // step, band, step), jnp.float32),
            pltpu.VMEM((slots // step, band, step), jnp.float32),
            pltpu.VMEM((band, LANES), jnp.float32),
            pltpu.VMEM((band, LANES), jnp.float32),
            pltpu.VMEM((band, LANES), jnp.float32),
            pltpu.VMEM((band, 2 * LANES), jnp.float32),
            pltpu.VMEM((rows, LANES), jnp.float32),
        ],
        compiler_params=pltpu.CompilerParams(vmem_limit_bytes=VMEM_GRANT),
        cost_estimate=pl.CostEstimate(
            flops=8 * rows * slots * HD,
            bytes_accessed=4 * slots * HD,
            transcendentals=rows * slots,
        ),
    )(length, me, *queries, keys, values)


def merge_kernel(me_ref, part_ref, q_ref, last_ref, copies_ref, turned, kv_all, *, block, tokens, head):
    count = part_ref.shape[0]
    per = LANES // block
    kv_block = last_ref.shape[1] - block
    scale = math.log2(math.e) / math.sqrt(HD)

    for k in range(count):
        rows = last_ref[k, block:, :].astype(jnp.float32)
        kv_all[k * kv_block : (k + 1) * kv_block, :] = rows
    half = kv_all.shape[0] // 2
    keys = kv_all[head * tokens : (head + 1) * tokens, :].astype(jnp.bfloat16)
    values = kv_all[half + head * tokens : half + (head + 1) * tokens, :].astype(jnp.bfloat16)

    s = lax.dot_general(q_ref[0, :block, :], keys, NT, preferred_element_type=jnp.float32) * scale
    token = lax.rem(me_ref[0] * block, tokens) + lax.broadcasted_iota(jnp.int32, s.shape, 0)
    visible = lax.broadcasted_iota(jnp.int32, s.shape, 1) <= token
    s = jnp.where(visible, s, NEG_BIG)
    new_top = jnp.max(s, axis=1, keepdims=True)
    weights = jnp.where(visible, jnp.exp2(s - new_top), 0.0).astype(jnp.bfloat16)
    new_total = jnp.sum(weights.astype(jnp.float32), axis=1, keepdims=True)
    new_out = jnp.dot(weights, values, preferred_element_type=jnp.float32)

    place = lax.rem(me_ref[0], per)
    pieces = part_ref[:, block : block + 4, :]
    level = pieces[:, 1, :] * 2.0**-9 + pieces[:, 2, :] * 2.0**-20 + pieces[:, 3, :] * 2.0**-31
    turned[...] = (level * jnp.exp2(pieces[:, 0, :])).T
    levels = turned[pl.ds(pl.multiple_of(place * block, block), block), :]
    joint = jnp.maximum(new_top, jnp.max(levels, axis=1, keepdims=True))
    factors = jnp.exp2(levels - joint)
    new_scale = jnp.exp2(new_top - joint)
    whole_out = new_out * new_scale
    whole_total = new_total * new_scale + jnp.sum(factors, axis=1, keepdims=True)
    scaled = factors * (1.0 / OUTPUT_SCALE)
    for k in range(count):
        whole_out = whole_out + part_ref[k, :block, :] * scaled[:, k : k + 1]
    attended = (whole_out / whole_total).astype(jnp.bfloat16)
    for k in range(count):
        copies_ref[k] = attended


def merge(me, parts, mine, last, block, tokens, head):
    count = parts.shape[0]
    kv_rows = count * (last.shape[1] - block)
    return pl.pallas_call(
        functools.partial(merge_kernel, block=block, tokens=tokens, head=head),
        out_shape=jax.ShapeDtypeStruct((count, block, HD), jnp.bfloat16),
        in_specs=[smem_spec()] + [vmem_spec()] * 3,
        out_specs=vmem_spec(),
        scratch_shapes=[
            pltpu.VMEM((LANES, count), jnp.float32),
            pltpu.VMEM((kv_rows, HD), jnp.float32),
        ],
    )(me, parts, mine, last)


def output_kernel(place_ref, w_hbm, a_ref, *refs, tokens, groups, chunk, has_before, last):
    before = refs[0] if has_before else None
    outs, (w_all, total, sems) = refs[int(has_before) : -3], refs[-3:]
    copies = []
    for g in range(groups):
        copies.append(
            pltpu.make_async_copy(
                w_hbm.at[pl.ds((chunk * groups + g) * HD, HD), :],
                w_all.at[pl.ds(g * HD, HD), :],
                sems.at[g],
            )
        )
        copies[-1].start()
    per = a_ref.shape[0] // groups
    pieces = [a_ref[g * per : (g + 1) * per].reshape(tokens, HD) for g in range(groups)]
    product = before[...] if has_before else None
    for g in range(0, groups, 2):
        copies[g].wait()
        copies[g + 1].wait()
        term = jnp.dot(
            jnp.concatenate(pieces[g : g + 2], axis=1),
            w_all[g * HD : (g + 2) * HD, :],
            preferred_element_type=jnp.float32,
        )
        product = term if product is None else product + term
    if not last:
        outs[0][...] = product
        return
    total[...] = product
    keep_ref, send_ref = outs
    share = keep_ref.shape[1]
    odd = lax.rem(place_ref[0], 2)
    for i in range(keep_ref.shape[0]):
        for ref, parity in ((keep_ref, odd), (send_ref, 1 - odd)):
            start = pl.multiple_of((2 * i + parity) * share, share)
            ref[i] = total[pl.ds(start, share), :]


def output_part(place, weight, attended, tokens, before, chunk, heads, last):
    groups = QH // KVH
    width = weight.shape[1]
    has_before = before is not None
    shapes = [jax.ShapeDtypeStruct((tokens, width), jnp.float32)]
    if last:
        shapes = [jax.ShapeDtypeStruct((heads // 2, tokens // heads, width), jnp.float32)] * 2
    return pl.pallas_call(
        functools.partial(
            output_kernel,
            tokens=tokens,
            groups=groups,
            chunk=chunk,
            has_before=has_before,
            last=last,
        ),
        out_shape=shapes,
        in_specs=[smem_spec(), hbm_spec()] + [vmem_spec()] * (1 + int(has_before)),
        out_specs=[vmem_spec()] * len(shapes),
        scratch_shapes=[
            pltpu.VMEM((groups * HD, width), jnp.bfloat16),
            pltpu.VMEM((tokens, width), jnp.float32),
            pltpu.SemaphoreType.DMA((groups,)),
        ],
        compiler_params=pltpu.CompilerParams(vmem_limit_bytes=VMEM_GRANT),
        cost_estimate=pl.CostEstimate(
            flops=2 * tokens * groups * HD * width,
            bytes_accessed=2 * groups * HD * width,
            transcendentals=0,
        ),
    )(place, weight, attended, *([before] if has_before else []))


def shards(
    hidden,
    query_weight,
    key_weight,
    value_weight,
    output_weight,
    cache_keys,
    cache_values,
    cache_lens,
):
    tokens = hidden.shape[0]
    count = lax.axis_size("seq")
    heads = lax.axis_size("head")
    kv_local = cache_keys.shape[1] // HD
    block = (QH // KVH) * tokens // count
    me = lax.axis_index("seq").reshape(1)
    place = lax.axis_index("head").reshape(1)

    halves = project(me, hidden, query_weight, key_weight, value_weight, kv_local, count)
    mine, queries = [], []
    for j in range(kv_local):
        mine.append(owners_sum(halves[2 * j], halves[2 * j + 1], me[0]))
        if j < kv_local - 1:
            queries.append(gather_doubling(mine[j]))
        else:
            copies = jnp.broadcast_to(mine[j], (count,) + mine[j].shape[1:])
            queries.append([gather_at_once(copies)])

    mixed = None
    for j in range(kv_local):
        parts = attention(queries[j], block, cache_keys, cache_values, cache_lens, me, j)
        parts = lax.all_to_all(parts.astype(jnp.float16), "seq", 0, 0).astype(jnp.float32)
        copies = merge(me, parts, mine[j], queries[-1][0], block, tokens, j)
        last = j == kv_local - 1
        result = output_part(
            place, output_weight, gather_at_once(copies), tokens, mixed, j, heads, last
        )
        mixed = result if last else result[0]

    keep, send = mixed
    mixed = keep + swap(send, "head", 1)
    mask = 2
    while mask < heads:
        bit = place[0] // mask % 2
        pairs = mixed.reshape((-1, 2) + mixed.shape[1:])
        keep = lax.dynamic_index_in_dim(pairs, bit, 1, False)
        send = lax.dynamic_index_in_dim(pairs, 1 - bit, 1, False) * MIXED_SCALE
        received = swap(send.astype(jnp.float16), "head", mask).astype(jnp.float32)
        mixed = keep + received * (1.0 / MIXED_SCALE)
        mask *= 2
    return mixed[0].astype(jnp.bfloat16)


def solution(mesh):
    placed = (
        P(None, "seq"),
        P("seq", "head"),
        P("seq", "head"),
        P("seq", "head"),
        P("head", "seq"),
        P("seq", "head"),
        P("seq", "head"),
        P("seq"),
    )
    return jax.shard_map(
        shards, mesh=mesh, in_specs=placed, out_specs=P("head", "seq"), check_vma=False
    )
```

```python
import functools
import math

import jax
import jax.numpy as jnp
from jax import lax
from jax.experimental import pallas as pl
from jax.experimental.pallas import tpu as pltpu
from jax.sharding import PartitionSpec as P

QH = 64
KVH = 8
HD = 128

NEG_BIG = -1e30
LANES = 128
STAT_ROWS = 8
VMEM_GRANT = 51 << 20
PROJECT_GRANT = 56 << 20
NT = (((1,), (1,)), ((), ()))

OUTPUT_SCALE = 2.0**12
MIXED_SCALE = 2.0**-3


def vmem_spec():
    return pl.BlockSpec(memory_space=pltpu.VMEM)


def smem_spec():
    return pl.BlockSpec(memory_space=pltpu.SMEM)


def hbm_spec():
    return pl.BlockSpec(memory_space=pl.ANY)


def swap(array, axis, mask):
    size = lax.axis_size(axis)
    return lax.ppermute(array, axis, [(i, i ^ mask) for i in range(size)])


def owners_sum(keep, send, me):
    total = keep + swap(send, "seq", 1)
    mask = 2
    while mask < lax.axis_size("seq"):
        bit = me // mask % 2
        pairs = total.reshape((-1, 2) + total.shape[1:])
        keep = lax.dynamic_index_in_dim(pairs, bit, 1, False)
        send = lax.dynamic_index_in_dim(pairs, 1 - bit, 1, False)
        total = keep + swap(send, "seq", mask)
        mask *= 2
    return total.astype(jnp.bfloat16)


def doubling_masks(size):
    masks = []
    while size > 2:
        size //= 2
        masks.append(size)
    return masks


def gather_doubling(block):
    for mask in doubling_masks(lax.axis_size("seq")):
        block = jnp.concatenate([block, swap(block, "seq", mask)])
    return [block, swap(block, "seq", 1)]


def doubling_offsets(size):
    offsets = [0]
    for mask in doubling_masks(size):
        offsets = offsets + [offset ^ mask for offset in offsets]
    return offsets + [offset ^ 1 for offset in offsets]


def gather_at_once(copies):
    return lax.all_to_all(copies, "seq", 0, 0)


def project_kernel(me_ref, hidden_ref, *refs, extra, chunk, blocks, pieces):
    weight_refs, refs = refs[: 1 + extra], refs[1 + extra :]
    keep_ref, send_ref, q_all, *others_all, sems = refs
    tokens, depth = hidden_ref.shape
    odd = lax.rem(me_ref[0], 2) == 1
    rows = depth // pieces
    columns = q_all.shape[1]
    copies = [
        pltpu.make_async_copy(
            weight_refs[0].at[pl.ds(i * rows, rows), pl.ds(chunk * columns, columns)],
            q_all.at[pl.ds(i * rows, rows), :],
            sems.at[i],
        )
        for i in range(pieces)
    ]
    for i in range(extra):
        copies.append(
            pltpu.make_async_copy(weight_refs[1 + i], others_all[i], sems.at[pieces + i])
        )
    for copy in copies:
        copy.start()

    def deal(product, kind):
        block = blocks[kind]
        first = kind * blocks[0]
        parts = [
            product[e * block : (e + 1) * block, c * LANES : (c + 1) * LANES]
            for c in range(product.shape[1] // LANES)
            for e in range(tokens // block)
        ]
        for i, (even_part, odd_part) in enumerate(zip(parts[0::2], parts[1::2])):
            keep_ref[i, first : first + block, :] = jnp.where(odd, odd_part, even_part)
            send_ref[i, first : first + block, :] = jnp.where(odd, even_part, odd_part)

    total = None
    for i in range(pieces):
        copies[i].wait()
        here = slice(i * rows, (i + 1) * rows)
        term = jnp.dot(hidden_ref[:, here], q_all[here, :], preferred_element_type=jnp.float32)
        total = term if total is None else total + term
    deal(total, 0)
    if extra:
        both = []
        for i in range(extra):
            copies[pieces + i].wait()
            both.append(
                jnp.dot(hidden_ref[...], others_all[i][...], preferred_element_type=jnp.float32)
            )
        deal(jnp.concatenate(both, axis=1), 1)


def project(me, hidden, query_weight, others, chunk, columns, count):
    tokens, depth = hidden.shape
    wide = columns + sum(other.shape[1] for other in others)
    pieces = max(1, depth // 256)
    blocks = [width // LANES * tokens // count for width in (columns, wide - columns)]
    shape = jax.ShapeDtypeStruct((count // 2, sum(blocks), LANES), jnp.float32)
    return pl.pallas_call(
        functools.partial(
            project_kernel, extra=len(others), chunk=chunk, blocks=blocks, pieces=pieces
        ),
        out_shape=[shape] * 2,
        in_specs=[smem_spec(), vmem_spec()] + [hbm_spec()] * (1 + len(others)),
        out_specs=[vmem_spec()] * 2,
        scratch_shapes=[pltpu.VMEM((depth, columns), jnp.bfloat16)]
        + [pltpu.VMEM(other.shape, jnp.bfloat16) for other in others]
        + [pltpu.SemaphoreType.DMA((pieces + len(others),))],
        compiler_params=pltpu.CompilerParams(vmem_limit_bytes=PROJECT_GRANT),
        cost_estimate=pl.CostEstimate(
            flops=2 * tokens * depth * wide,
            bytes_accessed=2 * depth * wide,
            transcendentals=0,
        ),
    )(me, hidden, query_weight, *others)


def attention_kernel(len_ref, me_ref, *refs, sources, band, step, block, head):
    q_refs, refs = refs[:sources], refs[sources:]
    k_hbm, v_hbm, o_ref, k_ref, v_ref, sems = refs[:6]
    s_bufs, m_bufs = refs[6:8], refs[8:10]
    shift, acc, lse_all = refs[10:]
    half = q_refs[0].shape[0]
    rows = sources * half * block
    bands = rows // band
    share = band // block
    scale = math.log2(math.e) / math.sqrt(HD)
    piece = math.gcd(step, 1024)
    tiles = piece // LANES
    lanes = slice(head * HD, (head + 1) * HD)
    offsets = doubling_offsets(sources * half)

    def owner_of(k):
        return k if sources == 1 else me_ref[0] ^ offsets[k]

    length = len_ref[0]
    full = length // step
    rest = length - full * step

    def copy_in(source, target, which, i):
        where = pl.ds(pl.multiple_of(i * step, step), step)
        return pltpu.make_async_copy(
            source.at[where, :], target.at[where, :], sems.at[which, i]
        )

    def keys_in(i):
        return copy_in(k_hbm, k_ref, 0, i)

    def values_in(i):
        return copy_in(v_hbm, v_ref, 1, i)

    needed = (length + step - 1) // step

    def start_keys(i, carry):
        keys_in(i).start()
        return carry

    def start_values(i, carry):
        values_in(i).start()
        return carry

    lax.fori_loop(0, needed, start_keys, 0)
    lax.fori_loop(0, needed, start_values, 0)

    def score(r, i, first, masked):
        source = q_refs[r * share // half]
        at = r * share % half
        q = source[at : at + share, :block, :].reshape(band, HD)
        keys = k_ref[pl.ds(pl.multiple_of(i * step + first, piece), piece), lanes]
        s = lax.dot_general(q, keys, NT, preferred_element_type=jnp.float32)
        if masked:
            column = first + lax.broadcasted_iota(jnp.int32, (band, piece), 1)
            s = jnp.where(column < rest, s, NEG_BIG)
        s_bufs[r % 2][i, :, first : first + piece] = s
        tops = [s[:, c * LANES : (c + 1) * LANES] for c in range(tiles)]
        while len(tops) > 1:
            tops = [jnp.maximum(a, b) for a, b in zip(tops[0::2], tops[1::2])]
        m_bufs[r % 2][...] = jnp.maximum(m_bufs[r % 2][...], tops[0])

    def weigh(r, i, first):
        s = s_bufs[r % 2][i, :, first : first + piece]
        low = shift[...]
        weights = jnp.concatenate(
            [
                jnp.exp2(s[:, c * LANES : (c + 1) * LANES] * scale - low).astype(jnp.bfloat16)
                for c in range(tiles)
            ],
            axis=1,
        )
        values = v_ref[pl.ds(pl.multiple_of(i * step + first, piece), piece), lanes]
        wide = jnp.concatenate([values, jnp.ones((piece, LANES), jnp.bfloat16)], axis=1)
        acc[...] += jnp.dot(weights, wide, preferred_element_type=jnp.float32)

    for r in range(bands + 1):
        scores, weighs = r < bands, r > 0
        if scores:
            m_bufs[r % 2][...] = jnp.full((band, LANES), -3e38, jnp.float32)
        if weighs:
            top = jnp.max(m_bufs[(r - 1) % 2][...], axis=1, keepdims=True)
            shift[...] = jnp.broadcast_to(top * scale, (band, LANES))
            acc[...] = jnp.zeros(acc.shape, jnp.float32)

        def both(i, masked):
            if r == 0:
                keys_in(i).wait()
            if r == 1:
                values_in(i).wait()
            for first in range(0, step, piece):
                if weighs:
                    weigh(r - 1, i, first)
                if scores:
                    score(r, i, first, masked)

        def body(i, carry):
            both(i, False)
            return carry

        lax.fori_loop(0, full, body, 0)

        @pl.when(rest > 0)
        def _():
            both(full, True)

        if weighs:
            totals = acc[:, LANES:]
            mean = acc[:, :LANES] / totals * OUTPUT_SCALE
            levels = shift[...] + jnp.log2(totals)
            for e in range(share):
                k = (r - 1) * share + e
                owner = owner_of(k)
                here = slice(e * block, (e + 1) * block)
                o_ref[owner, :block, :] = mean[here, :]
                lse_all[pl.ds(pl.multiple_of(owner * block, block), block), :] = levels[here, :]

    per = LANES // block
    row = lax.broadcasted_iota(jnp.int32, (STAT_ROWS, LANES), 0)
    for g in range(rows // LANES):
        level = lse_all[g * LANES : (g + 1) * LANES, :].T[:STAT_ROWS, :]
        exponent = jnp.floor(jnp.log2(jnp.maximum(jnp.abs(level), 1e-30)))
        exponent = jnp.minimum(exponent, 120.0)
        rest_of = level * jnp.exp2(-exponent)
        first = jnp.floor(rest_of * 2.0**9 + 0.5)
        rest_of = rest_of - first * 2.0**-9
        second = jnp.floor(rest_of * 2.0**20 + 0.5)
        third = (rest_of - second * 2.0**-20) * 2.0**31
        stats = jnp.where(row == 0, exponent, jnp.where(row == 1, first, second))
        stats = jnp.where(row >= 3, third, stats)
        for e in range(per):
            o_ref[g * per + e, block:, :] = stats


def attention(queries, block, keys, values, length, me, head):
    sources = len(queries)
    count = sources * queries[0].shape[0]
    rows, slots = count * block, keys.shape[0]
    band = math.gcd(rows // 2, 512)
    step = math.gcd(slots, 2048)
    return pl.pallas_call(
        functools.partial(
            attention_kernel, sources=sources, band=band, step=step, block=block, head=head
        ),
        out_shape=jax.ShapeDtypeStruct((count, block + STAT_ROWS, HD), jnp.float32),
        in_specs=[smem_spec()] * 2 + [vmem_spec()] * sources + [hbm_spec()] * 2,
        out_specs=vmem_spec(),
        scratch_shapes=[
            pltpu.VMEM(keys.shape, keys.dtype),
            pltpu.VMEM(values.shape, values.dtype),
            pltpu.SemaphoreType.DMA((2, slots // step)),
            pltpu.VMEM((slots // step, band, step), jnp.float32),
            pltpu.VMEM((slots // step, band, step), jnp.float32),
            pltpu.VMEM((band, LANES), jnp.float32),
            pltpu.VMEM((band, LANES), jnp.float32),
            pltpu.VMEM((band, LANES), jnp.float32),
            pltpu.VMEM((band, 2 * LANES), jnp.float32),
            pltpu.VMEM((rows, LANES), jnp.float32),
        ],
        compiler_params=pltpu.CompilerParams(vmem_limit_bytes=VMEM_GRANT),
        cost_estimate=pl.CostEstimate(
            flops=8 * rows * slots * HD,
            bytes_accessed=4 * slots * HD,
            transcendentals=rows * slots,
        ),
    )(length, me, *queries, keys, values)


def fresh_kernel(me_ref, q_ref, last_ref, out_ref, stat_ref, kv_all, *, block, tokens, head):
    kv_block = last_ref.shape[1] - block
    for k in range(last_ref.shape[0]):
        rows = last_ref[k, block:, :].astype(jnp.float32)
        kv_all[k * kv_block : (k + 1) * kv_block, :] = rows
    half = kv_all.shape[0] // 2
    keys = kv_all[head * tokens : (head + 1) * tokens, :].astype(jnp.bfloat16)
    values = kv_all[half + head * tokens : half + (head + 1) * tokens, :].astype(jnp.bfloat16)

    s = lax.dot_general(q_ref[0, :block, :], keys, NT, preferred_element_type=jnp.float32)
    s = s * (math.log2(math.e) / math.sqrt(HD))
    token = lax.rem(me_ref[0] * block, tokens) + lax.broadcasted_iota(jnp.int32, s.shape, 0)
    visible = lax.broadcasted_iota(jnp.int32, s.shape, 1) <= token
    s = jnp.where(visible, s, NEG_BIG)
    top = jnp.max(s, axis=1, keepdims=True)
    weights = jnp.where(visible, jnp.exp2(s - top), 0.0).astype(jnp.bfloat16)
    total = jnp.sum(weights.astype(jnp.float32), axis=1, keepdims=True)
    out_ref[...] = jnp.dot(weights, values, preferred_element_type=jnp.float32)
    lane = lax.broadcasted_iota(jnp.int32, stat_ref.shape, 1)
    stat_ref[...] = jnp.where(lane < LANES // 2, top, total)


def fresh(me, mine, last, block, tokens, head):
    kv_rows = last.shape[0] * (last.shape[1] - block)
    return pl.pallas_call(
        functools.partial(fresh_kernel, block=block, tokens=tokens, head=head),
        out_shape=[jax.ShapeDtypeStruct((block, HD), jnp.float32)] * 2,
        in_specs=[smem_spec()] + [vmem_spec()] * 2,
        out_specs=[vmem_spec()] * 2,
        scratch_shapes=[pltpu.VMEM((kv_rows, HD), jnp.float32)],
    )(me, mine, last)


def merge_kernel(me_ref, part_ref, out_ref, stat_ref, copies_ref, turned):
    count = part_ref.shape[0]
    block = out_ref.shape[0]
    new_top = stat_ref[:, 0:1]
    new_total = stat_ref[:, LANES // 2 : LANES // 2 + 1]

    place = lax.rem(me_ref[0], LANES // block)
    pieces = part_ref[:, block : block + 4, :]
    level = pieces[:, 1, :] * 2.0**-9 + pieces[:, 2, :] * 2.0**-20 + pieces[:, 3, :] * 2.0**-31
    turned[...] = (level * jnp.exp2(pieces[:, 0, :])).T
    levels = turned[pl.ds(pl.multiple_of(place * block, block), block), :]
    joint = jnp.maximum(new_top, jnp.max(levels, axis=1, keepdims=True))
    factors = jnp.exp2(levels - joint)
    new_scale = jnp.exp2(new_top - joint)
    whole_out = out_ref[...] * new_scale
    whole_total = new_total * new_scale + jnp.sum(factors, axis=1, keepdims=True)
    scaled = factors * (1.0 / OUTPUT_SCALE)
    for k in range(count):
        whole_out = whole_out + part_ref[k, :block, :] * scaled[:, k : k + 1]
    attended = (whole_out / whole_total).astype(jnp.bfloat16)
    for k in range(copies_ref.shape[0]):
        copies_ref[k] = attended


def merge(me, parts, new_out, new_stat, copies):
    return pl.pallas_call(
        merge_kernel,
        out_shape=jax.ShapeDtypeStruct((copies,) + new_out.shape, jnp.bfloat16),
        in_specs=[smem_spec()] + [vmem_spec()] * 3,
        out_specs=vmem_spec(),
        scratch_shapes=[pltpu.VMEM((LANES, parts.shape[0]), jnp.float32)],
    )(me, parts, new_out, new_stat)


def output_kernel(
    me_ref, place_ref, w_hbm, *refs, sources, tokens, groups, chunk, has_before, last
):
    a_refs, refs = refs[:sources], refs[sources:]
    before = refs[0] if has_before else None
    outs, (w_all, a_all, total, sems) = refs[int(has_before) : -4], refs[-4:]
    copies = []
    for g in range(groups):
        copies.append(
            pltpu.make_async_copy(
                w_hbm.at[pl.ds((chunk * groups + g) * HD, HD), :],
                w_all.at[pl.ds(g * HD, HD), :],
                sems.at[g],
            )
        )
        copies[-1].start()
    half, block = a_refs[0].shape[:2]
    per = sources * half // groups
    if sources == 1:
        pieces = [a_refs[0][g * per : (g + 1) * per].reshape(tokens, HD) for g in range(groups)]
    else:
        for k, offset in enumerate(doubling_offsets(sources * half)):
            owner = me_ref[0] ^ offset
            start = pl.multiple_of(lax.rem(owner, per) * block, block)
            a_all[owner // per, pl.ds(start, block), :] = a_refs[k // half][k % half]
        pieces = [a_all[g] for g in range(groups)]
    product = before[...] if has_before else None
    for g in range(0, groups, 2):
        copies[g].wait()
        copies[g + 1].wait()
        term = jnp.dot(
            jnp.concatenate(pieces[g : g + 2], axis=1),
            w_all[g * HD : (g + 2) * HD, :],
            preferred_element_type=jnp.float32,
        )
        product = term if product is None else product + term
    if not last:
        outs[0][...] = product
        return
    total[...] = product
    keep_ref, send_ref = outs
    share = keep_ref.shape[1]
    odd = lax.rem(place_ref[0], 2)
    for i in range(keep_ref.shape[0]):
        for ref, parity in ((keep_ref, odd), (send_ref, 1 - odd)):
            start = pl.multiple_of((2 * i + parity) * share, share)
            ref[i] = total[pl.ds(start, share), :]


def output_part(me, place, weight, attended, tokens, before, chunk, heads, last):
    groups = QH // KVH
    width = weight.shape[1]
    has_before = before is not None
    shapes = [jax.ShapeDtypeStruct((tokens, width), jnp.float32)]
    if last:
        shapes = [jax.ShapeDtypeStruct((heads // 2, tokens // heads, width), jnp.float32)] * 2
    return pl.pallas_call(
        functools.partial(
            output_kernel,
            sources=len(attended),
            tokens=tokens,
            groups=groups,
            chunk=chunk,
            has_before=has_before,
            last=last,
        ),
        out_shape=shapes,
        in_specs=[smem_spec()] * 2
        + [hbm_spec()]
        + [vmem_spec()] * (len(attended) + int(has_before)),
        out_specs=[vmem_spec()] * len(shapes),
        scratch_shapes=[
            pltpu.VMEM((groups * HD, width), jnp.bfloat16),
            pltpu.VMEM((groups, tokens, HD), jnp.bfloat16),
            pltpu.VMEM((tokens, width), jnp.float32),
            pltpu.SemaphoreType.DMA((groups,)),
        ],
        compiler_params=pltpu.CompilerParams(vmem_limit_bytes=VMEM_GRANT),
        cost_estimate=pl.CostEstimate(
            flops=2 * tokens * groups * HD * width,
            bytes_accessed=2 * groups * HD * width,
            transcendentals=0,
        ),
    )(me, place, weight, *attended, *([before] if has_before else []))


def shards(
    hidden,
    query_weight,
    key_weight,
    value_weight,
    output_weight,
    cache_keys,
    cache_values,
    cache_lens,
):
    tokens = hidden.shape[0]
    count = lax.axis_size("seq")
    heads = lax.axis_size("head")
    kv_local = cache_keys.shape[1] // HD
    columns = (QH // KVH) * HD
    block = (QH // KVH) * tokens // count
    me = lax.axis_index("seq").reshape(1)
    place = lax.axis_index("head").reshape(1)

    mine, queries = [], []
    for j in range(kv_local):
        last = j == kv_local - 1
        others = [key_weight, value_weight] if last else []
        keep, send = project(me, hidden, query_weight, others, j, columns, count)
        mine.append(owners_sum(keep, send, me[0]))
        if last:
            copies = jnp.broadcast_to(mine[j], (count,) + mine[j].shape[1:])
            queries.append([gather_at_once(copies)])
        else:
            queries.append(gather_doubling(mine[j]))

    mixed = None
    for j in range(kv_local):
        last = j == kv_local - 1
        parts = attention(queries[j], block, cache_keys, cache_values, cache_lens, me, j)
        parts = lax.all_to_all(parts.astype(jnp.float16), "seq", 0, 0).astype(jnp.float32)
        new_out, new_stat = fresh(me, mine[j], queries[-1][0], block, tokens, j)
        copies = merge(me, parts, new_out, new_stat, count if last else 1)
        attended = [gather_at_once(copies)] if last else gather_doubling(copies)
        result = output_part(
            me, place, output_weight, attended, tokens, mixed, j, heads, last
        )
        mixed = result if last else result[0]

    keep, send = mixed
    mixed = keep + swap(send, "head", 1)
    mask = 2
    while mask < heads:
        bit = place[0] // mask % 2
        pairs = mixed.reshape((-1, 2) + mixed.shape[1:])
        keep = lax.dynamic_index_in_dim(pairs, bit, 1, False)
        send = lax.dynamic_index_in_dim(pairs, 1 - bit, 1, False) * MIXED_SCALE
        received = swap(send.astype(jnp.float16), "head", mask).astype(jnp.float32)
        mixed = keep + received * (1.0 / MIXED_SCALE)
        mask *= 2
    return mixed[0].astype(jnp.bfloat16)


def solution(mesh):
    placed = (
        P(None, "seq"),
        P("seq", "head"),
        P("seq", "head"),
        P("seq", "head"),
        P("head", "seq"),
        P("seq", "head"),
        P("seq", "head"),
        P("seq"),
    )
    return jax.shard_map(
        shards, mesh=mesh, in_specs=placed, out_specs=P("head", "seq"), check_vma=False
    )
```

```python
import functools
import math

import jax
import jax.numpy as jnp
from jax import lax
from jax.experimental import pallas as pl
from jax.experimental.pallas import tpu as pltpu
from jax.sharding import PartitionSpec as P

QH = 64
KVH = 8
HD = 128

NEG_BIG = -1e30
LANES = 128
STAT_ROWS = 8
VMEM_GRANT = 51 << 20
PROJECT_GRANT = 56 << 20
NT = (((1,), (1,)), ((), ()))

OUTPUT_SCALE = 2.0**12
MIXED_SCALE = 2.0**-3


def vmem_spec():
    return pl.BlockSpec(memory_space=pltpu.VMEM)


def smem_spec():
    return pl.BlockSpec(memory_space=pltpu.SMEM)


def hbm_spec():
    return pl.BlockSpec(memory_space=pl.ANY)


def swap(array, axis, mask):
    size = lax.axis_size(axis)
    return lax.ppermute(array, axis, [(i, i ^ mask) for i in range(size)])


def halve_kernel(me_ref, keep_ref, received_ref, *refs, mask):
    next_keep_ref, next_send_ref = refs[-2:]
    odd = lax.rem(me_ref[0] // mask, 2) == 1
    for i in range(next_keep_ref.shape[0]):
        even_part = keep_ref[2 * i] + received_ref[2 * i]
        odd_part = keep_ref[2 * i + 1] + received_ref[2 * i + 1]
        next_keep_ref[i] = jnp.where(odd, odd_part, even_part)
        next_send_ref[i] = jnp.where(odd, even_part, odd_part)


def halve(me, keep, received, mask, after):
    shape = jax.ShapeDtypeStruct((keep.shape[0] // 2,) + keep.shape[1:], keep.dtype)
    return pl.pallas_call(
        functools.partial(halve_kernel, mask=mask),
        out_shape=[shape] * 2,
        in_specs=[smem_spec()] + [vmem_spec()] * 2 + [hbm_spec()] * len(after),
        out_specs=[vmem_spec()] * 2,
    )(me, keep, received, *after)


def owners_sum(keep, send, me, after):
    received = swap(send, "seq", 1)
    mask = 2
    while mask < lax.axis_size("seq"):
        keep, send = halve(me, keep, received, mask, after)
        received = swap(send, "seq", mask)
        mask, after = 2 * mask, []
    return (keep + received).astype(jnp.bfloat16)


def doubling_masks(size):
    masks = []
    while size > 2:
        size //= 2
        masks.append(size)
    return masks


def gather_doubling(block):
    for mask in doubling_masks(lax.axis_size("seq")):
        block = jnp.concatenate([block, swap(block, "seq", mask)])
    return [block, swap(block, "seq", 1)]


def gather_but_last(block):
    masks = doubling_masks(lax.axis_size("seq"))
    for mask in masks[:-1]:
        block = jnp.concatenate([block, swap(block, "seq", mask)])
    return block, swap(block, "seq", masks[-1])


def pack_kernel(first_ref, second_ref, attended_ref, doubled_ref, copies_ref):
    half = first_ref.shape[0]
    doubled_ref[:half] = first_ref[...]
    doubled_ref[half:] = second_ref[...]
    for k in range(copies_ref.shape[0]):
        copies_ref[k] = attended_ref[0]


def pack(first, second, attended, copies):
    shape = first.shape[1:]
    return pl.pallas_call(
        pack_kernel,
        out_shape=[
            jax.ShapeDtypeStruct((2 * first.shape[0],) + shape, first.dtype),
            jax.ShapeDtypeStruct((copies,) + shape, first.dtype),
        ],
        in_specs=[vmem_spec()] * 3,
        out_specs=[vmem_spec()] * 2,
    )(first, second, attended)


def doubling_offsets(size):
    offsets = [0]
    for mask in doubling_masks(size):
        offsets = offsets + [offset ^ mask for offset in offsets]
    return offsets + [offset ^ 1 for offset in offsets]


def gather_at_once(copies):
    return lax.all_to_all(copies, "seq", 0, 0)


def project_kernel(me_ref, hidden_ref, *refs, extra, chunk, blocks, pieces):
    weight_refs, refs = refs[: 1 + extra], refs[1 + extra :]
    keep_ref, send_ref, q_all, *others_all, sems = refs
    tokens, depth = hidden_ref.shape
    odd = lax.rem(me_ref[0], 2) == 1
    rows = depth // pieces
    columns = q_all.shape[1]
    copies = [
        pltpu.make_async_copy(
            weight_refs[0].at[pl.ds(i * rows, rows), pl.ds(chunk * columns, columns)],
            q_all.at[pl.ds(i * rows, rows), :],
            sems.at[i],
        )
        for i in range(pieces)
    ]
    for i in range(extra):
        copies.append(
            pltpu.make_async_copy(weight_refs[1 + i], others_all[i], sems.at[pieces + i])
        )
    for copy in copies:
        copy.start()

    def deal(product, kind):
        block = blocks[kind]
        first = kind * blocks[0]
        parts = [
            product[e * block : (e + 1) * block, c * LANES : (c + 1) * LANES]
            for c in range(product.shape[1] // LANES)
            for e in range(tokens // block)
        ]
        for i, (even_part, odd_part) in enumerate(zip(parts[0::2], parts[1::2])):
            keep_ref[i, first : first + block, :] = jnp.where(odd, odd_part, even_part)
            send_ref[i, first : first + block, :] = jnp.where(odd, even_part, odd_part)

    total = None
    for i in range(pieces):
        copies[i].wait()
        here = slice(i * rows, (i + 1) * rows)
        term = jnp.dot(hidden_ref[:, here], q_all[here, :], preferred_element_type=jnp.float32)
        total = term if total is None else total + term
    deal(total, 0)
    if extra:
        both = []
        for i in range(extra):
            copies[pieces + i].wait()
            both.append(
                jnp.dot(hidden_ref[...], others_all[i][...], preferred_element_type=jnp.float32)
            )
        deal(jnp.concatenate(both, axis=1), 1)


def project(me, hidden, query_weight, others, chunk, columns, count):
    tokens, depth = hidden.shape
    wide = columns + sum(other.shape[1] for other in others)
    pieces = max(1, depth // 256)
    blocks = [width // LANES * tokens // count for width in (columns, wide - columns)]
    shape = jax.ShapeDtypeStruct((count // 2, sum(blocks), LANES), jnp.float32)
    return pl.pallas_call(
        functools.partial(
            project_kernel, extra=len(others), chunk=chunk, blocks=blocks, pieces=pieces
        ),
        out_shape=[shape] * 2,
        in_specs=[smem_spec(), vmem_spec()] + [hbm_spec()] * (1 + len(others)),
        out_specs=[vmem_spec()] * 2,
        scratch_shapes=[pltpu.VMEM((depth, columns), jnp.bfloat16)]
        + [pltpu.VMEM(other.shape, jnp.bfloat16) for other in others]
        + [pltpu.SemaphoreType.DMA((pieces + len(others),))],
        compiler_params=pltpu.CompilerParams(vmem_limit_bytes=PROJECT_GRANT),
        cost_estimate=pl.CostEstimate(
            flops=2 * tokens * depth * wide,
            bytes_accessed=2 * depth * wide,
            transcendentals=0,
        ),
    )(me, hidden, query_weight, *others)


def attention_kernel(len_ref, me_ref, *refs, sources, band, step, block, head):
    q_refs, refs = refs[:sources], refs[sources:]
    k_hbm, v_hbm, o_ref, k_ref, v_ref, sems = refs[:6]
    s_bufs, m_bufs = refs[6:8], refs[8:10]
    shift, acc, lse_all = refs[10:]
    half = q_refs[0].shape[0]
    rows = sources * half * block
    bands = rows // band
    share = band // block
    scale = math.log2(math.e) / math.sqrt(HD)
    piece = math.gcd(step, 1024)
    tiles = piece // LANES
    lanes = slice(head * HD, (head + 1) * HD)
    offsets = doubling_offsets(sources * half)

    def owner_of(k):
        return k if sources == 1 else me_ref[0] ^ offsets[k]

    length = len_ref[0]
    full = length // step
    rest = length - full * step

    def copy_in(source, target, which, i):
        where = pl.ds(pl.multiple_of(i * step, step), step)
        return pltpu.make_async_copy(
            source.at[where, :], target.at[where, :], sems.at[which, i]
        )

    def keys_in(i):
        return copy_in(k_hbm, k_ref, 0, i)

    def values_in(i):
        return copy_in(v_hbm, v_ref, 1, i)

    needed = (length + step - 1) // step

    def start_keys(i, carry):
        keys_in(i).start()
        return carry

    def start_values(i, carry):
        values_in(i).start()
        return carry

    lax.fori_loop(0, needed, start_keys, 0)
    lax.fori_loop(0, needed, start_values, 0)

    def score(r, i, first, masked):
        source = q_refs[r * share // half]
        at = r * share % half
        q = source[at : at + share, :block, :].reshape(band, HD)
        keys = k_ref[pl.ds(pl.multiple_of(i * step + first, piece), piece), lanes]
        s = lax.dot_general(q, keys, NT, preferred_element_type=jnp.float32)
        if masked:
            column = first + lax.broadcasted_iota(jnp.int32, (band, piece), 1)
            s = jnp.where(column < rest, s, NEG_BIG)
        s_bufs[r % 2][i, :, first : first + piece] = s
        tops = [s[:, c * LANES : (c + 1) * LANES] for c in range(tiles)]
        while len(tops) > 1:
            tops = [jnp.maximum(a, b) for a, b in zip(tops[0::2], tops[1::2])]
        m_bufs[r % 2][...] = jnp.maximum(m_bufs[r % 2][...], tops[0])

    def weigh(r, i, first):
        s = s_bufs[r % 2][i, :, first : first + piece]
        low = shift[...]
        weights = jnp.concatenate(
            [
                jnp.exp2(s[:, c * LANES : (c + 1) * LANES] * scale - low).astype(jnp.bfloat16)
                for c in range(tiles)
            ],
            axis=1,
        )
        values = v_ref[pl.ds(pl.multiple_of(i * step + first, piece), piece), lanes]
        wide = jnp.concatenate([values, jnp.ones((piece, LANES), jnp.bfloat16)], axis=1)
        acc[...] += jnp.dot(weights, wide, preferred_element_type=jnp.float32)

    for r in range(bands + 1):
        scores, weighs = r < bands, r > 0
        if scores:
            m_bufs[r % 2][...] = jnp.full((band, LANES), -3e38, jnp.float32)
        if weighs:
            top = jnp.max(m_bufs[(r - 1) % 2][...], axis=1, keepdims=True)
            shift[...] = jnp.broadcast_to(top * scale, (band, LANES))
            acc[...] = jnp.zeros(acc.shape, jnp.float32)

        def both(i, masked):
            if r == 0:
                keys_in(i).wait()
            if r == 1:
                values_in(i).wait()
            for first in range(0, step, piece):
                if weighs:
                    weigh(r - 1, i, first)
                if scores:
                    score(r, i, first, masked)

        def body(i, carry):
            both(i, False)
            return carry

        lax.fori_loop(0, full, body, 0)

        @pl.when(rest > 0)
        def _():
            both(full, True)

        if weighs:
            totals = acc[:, LANES:]
            mean = acc[:, :LANES] / totals * OUTPUT_SCALE
            levels = shift[...] + jnp.log2(totals)
            for e in range(share):
                k = (r - 1) * share + e
                owner = owner_of(k)
                here = slice(e * block, (e + 1) * block)
                o_ref[owner, :block, :] = mean[here, :]
                lse_all[pl.ds(pl.multiple_of(owner * block, block), block), :] = levels[here, :]

    per = LANES // block
    row = lax.broadcasted_iota(jnp.int32, (STAT_ROWS, LANES), 0)
    for g in range(rows // LANES):
        level = lse_all[g * LANES : (g + 1) * LANES, :].T[:STAT_ROWS, :]
        exponent = jnp.floor(jnp.log2(jnp.maximum(jnp.abs(level), 1e-30)))
        exponent = jnp.minimum(exponent, 120.0)
        rest_of = level * jnp.exp2(-exponent)
        first = jnp.floor(rest_of * 2.0**9 + 0.5)
        rest_of = rest_of - first * 2.0**-9
        second = jnp.floor(rest_of * 2.0**20 + 0.5)
        third = (rest_of - second * 2.0**-20) * 2.0**31
        stats = jnp.where(row == 0, exponent, jnp.where(row == 1, first, second))
        stats = jnp.where(row >= 3, third, stats)
        for e in range(per):
            o_ref[g * per + e, block:, :] = stats


def attention(queries, block, keys, values, length, me, head):
    sources = len(queries)
    count = sources * queries[0].shape[0]
    rows, slots = count * block, keys.shape[0]
    band = math.gcd(rows // 2, 512)
    step = math.gcd(slots, 2048)
    return pl.pallas_call(
        functools.partial(
            attention_kernel, sources=sources, band=band, step=step, block=block, head=head
        ),
        out_shape=jax.ShapeDtypeStruct((count, block + STAT_ROWS, HD), jnp.float32),
        in_specs=[smem_spec()] * 2 + [vmem_spec()] * sources + [hbm_spec()] * 2,
        out_specs=vmem_spec(),
        scratch_shapes=[
            pltpu.VMEM(keys.shape, keys.dtype),
            pltpu.VMEM(values.shape, values.dtype),
            pltpu.SemaphoreType.DMA((2, slots // step)),
            pltpu.VMEM((slots // step, band, step), jnp.float32),
            pltpu.VMEM((slots // step, band, step), jnp.float32),
            pltpu.VMEM((band, LANES), jnp.float32),
            pltpu.VMEM((band, LANES), jnp.float32),
            pltpu.VMEM((band, LANES), jnp.float32),
            pltpu.VMEM((band, 2 * LANES), jnp.float32),
            pltpu.VMEM((rows, LANES), jnp.float32),
        ],
        compiler_params=pltpu.CompilerParams(vmem_limit_bytes=VMEM_GRANT),
        cost_estimate=pl.CostEstimate(
            flops=8 * rows * slots * HD,
            bytes_accessed=4 * slots * HD,
            transcendentals=rows * slots,
        ),
    )(length, me, *queries, keys, values)


def fresh_kernel(me_ref, *refs, heads, block, tokens):
    q_refs, last_ref, outs, kv_all = refs[:heads], refs[heads], refs[heads + 1 : -1], refs[-1]
    kv_block = last_ref.shape[1] - block
    for k in range(last_ref.shape[0]):
        rows = last_ref[k, block:, :].astype(jnp.float32)
        kv_all[k * kv_block : (k + 1) * kv_block, :] = rows
    half = heads * tokens
    for head in range(heads):
        q_ref, (out_ref, stat_ref) = q_refs[head], outs[2 * head : 2 * head + 2]
        first = head * tokens
        keys = kv_all[first : first + tokens, :].astype(jnp.bfloat16)
        values = kv_all[half + first : half + first + tokens, :].astype(jnp.bfloat16)
        s = lax.dot_general(q_ref[0, :block, :], keys, NT, preferred_element_type=jnp.float32)
        s = s * (math.log2(math.e) / math.sqrt(HD))
        token = lax.rem(me_ref[0] * block, tokens) + lax.broadcasted_iota(jnp.int32, s.shape, 0)
        visible = lax.broadcasted_iota(jnp.int32, s.shape, 1) <= token
        s = jnp.where(visible, s, NEG_BIG)
        top = jnp.max(s, axis=1, keepdims=True)
        weights = jnp.where(visible, jnp.exp2(s - top), 0.0).astype(jnp.bfloat16)
        total = jnp.sum(weights.astype(jnp.float32), axis=1, keepdims=True)
        out_ref[...] = jnp.dot(weights, values, preferred_element_type=jnp.float32)
        lane = lax.broadcasted_iota(jnp.int32, stat_ref.shape, 1)
        stat_ref[...] = jnp.where(lane < LANES // 2, top, total)


def fresh(me, mine, last, block, tokens):
    heads = len(mine)
    kv_rows = last.shape[0] * (last.shape[1] - block)
    return pl.pallas_call(
        functools.partial(fresh_kernel, heads=heads, block=block, tokens=tokens),
        out_shape=[jax.ShapeDtypeStruct((block, HD), jnp.float32)] * (2 * heads),
        in_specs=[smem_spec()] + [vmem_spec()] * (heads + 1),
        out_specs=[vmem_spec()] * (2 * heads),
        scratch_shapes=[pltpu.VMEM((kv_rows, HD), jnp.float32)],
    )(me, *mine, last)


def merge_kernel(me_ref, part_ref, out_ref, stat_ref, *refs):
    copies_ref, turned = refs[-2:]
    count = part_ref.shape[0]
    block = out_ref.shape[0]
    new_top = stat_ref[:, 0:1]
    new_total = stat_ref[:, LANES // 2 : LANES // 2 + 1]

    place = lax.rem(me_ref[0], LANES // block)
    pieces = part_ref[:, block : block + 4, :]
    level = pieces[:, 1, :] * 2.0**-9 + pieces[:, 2, :] * 2.0**-20 + pieces[:, 3, :] * 2.0**-31
    turned[...] = (level * jnp.exp2(pieces[:, 0, :])).T
    levels = turned[pl.ds(pl.multiple_of(place * block, block), block), :]
    joint = jnp.maximum(new_top, jnp.max(levels, axis=1, keepdims=True))
    factors = jnp.exp2(levels - joint)
    new_scale = jnp.exp2(new_top - joint)
    whole_out = out_ref[...] * new_scale
    whole_total = new_total * new_scale + jnp.sum(factors, axis=1, keepdims=True)
    scaled = factors * (1.0 / OUTPUT_SCALE)
    for k in range(count):
        whole_out = whole_out + part_ref[k, :block, :] * scaled[:, k : k + 1]
    attended = (whole_out / whole_total).astype(jnp.bfloat16)
    for k in range(copies_ref.shape[0]):
        copies_ref[k] = attended


def merge(me, parts, new_out, new_stat, copies, after):
    return pl.pallas_call(
        merge_kernel,
        out_shape=jax.ShapeDtypeStruct((copies,) + new_out.shape, jnp.bfloat16),
        in_specs=[smem_spec()] + [vmem_spec()] * 3 + [hbm_spec()] * len(after),
        out_specs=vmem_spec(),
        scratch_shapes=[pltpu.VMEM((LANES, parts.shape[0]), jnp.float32)],
    )(me, parts, new_out, new_stat, *after)


def output_kernel(
    me_ref, place_ref, w_hbm, *refs, sources, tokens, groups, chunk, has_before, last
):
    a_refs, refs = refs[:sources], refs[sources:]
    before = refs[0] if has_before else None
    outs, (w_all, a_all, total, sems) = refs[int(has_before) : -4], refs[-4:]
    copies = []
    for g in range(groups):
        copies.append(
            pltpu.make_async_copy(
                w_hbm.at[pl.ds((chunk * groups + g) * HD, HD), :],
                w_all.at[pl.ds(g * HD, HD), :],
                sems.at[g],
            )
        )
        copies[-1].start()
    half, block = a_refs[0].shape[:2]
    per = sources * half // groups
    if sources == 1:
        pieces = [a_refs[0][g * per : (g + 1) * per].reshape(tokens, HD) for g in range(groups)]
    else:
        for k, offset in enumerate(doubling_offsets(sources * half)):
            owner = me_ref[0] ^ offset
            start = pl.multiple_of(lax.rem(owner, per) * block, block)
            a_all[owner // per, pl.ds(start, block), :] = a_refs[k // half][k % half]
        pieces = [a_all[g] for g in range(groups)]
    product = before[...] if has_before else None
    for g in range(0, groups, 2):
        copies[g].wait()
        copies[g + 1].wait()
        term = jnp.dot(
            jnp.concatenate(pieces[g : g + 2], axis=1),
            w_all[g * HD : (g + 2) * HD, :],
            preferred_element_type=jnp.float32,
        )
        product = term if product is None else product + term
    if not last:
        outs[0][...] = product
        return
    total[...] = product
    keep_ref, send_ref = outs
    share = keep_ref.shape[1]
    odd = lax.rem(place_ref[0], 2)
    for i in range(keep_ref.shape[0]):
        for ref, parity in ((keep_ref, odd), (send_ref, 1 - odd)):
            start = pl.multiple_of((2 * i + parity) * share, share)
            ref[i] = total[pl.ds(start, share), :]


def output_part(me, place, weight, attended, tokens, before, chunk, heads, last):
    groups = QH // KVH
    width = weight.shape[1]
    has_before = before is not None
    shapes = [jax.ShapeDtypeStruct((tokens, width), jnp.float32)]
    if last:
        shapes = [jax.ShapeDtypeStruct((heads // 2, tokens // heads, width), jnp.float32)] * 2
    return pl.pallas_call(
        functools.partial(
            output_kernel,
            sources=len(attended),
            tokens=tokens,
            groups=groups,
            chunk=chunk,
            has_before=has_before,
            last=last,
        ),
        out_shape=shapes,
        in_specs=[smem_spec()] * 2
        + [hbm_spec()]
        + [vmem_spec()] * (len(attended) + int(has_before)),
        out_specs=[vmem_spec()] * len(shapes),
        scratch_shapes=[
            pltpu.VMEM((groups * HD, width), jnp.bfloat16),
            pltpu.VMEM((groups, tokens, HD), jnp.bfloat16),
            pltpu.VMEM((tokens, width), jnp.float32),
            pltpu.SemaphoreType.DMA((groups,)),
        ],
        compiler_params=pltpu.CompilerParams(vmem_limit_bytes=VMEM_GRANT),
        cost_estimate=pl.CostEstimate(
            flops=2 * tokens * groups * HD * width,
            bytes_accessed=2 * groups * HD * width,
            transcendentals=0,
        ),
    )(me, place, weight, *attended, *([before] if has_before else []))


def shards(
    hidden,
    query_weight,
    key_weight,
    value_weight,
    output_weight,
    cache_keys,
    cache_values,
    cache_lens,
):
    tokens = hidden.shape[0]
    count = lax.axis_size("seq")
    heads = lax.axis_size("head")
    kv_local = cache_keys.shape[1] // HD
    columns = (QH // KVH) * HD
    block = (QH // KVH) * tokens // count
    me = lax.axis_index("seq").reshape(1)
    place = lax.axis_index("head").reshape(1)

    halves = []
    for j in range(kv_local):
        others = [key_weight, value_weight] if j == kv_local - 1 else []
        halves.append(project(me, hidden, query_weight, others, j, columns, count))
    mine, queries = [], []
    for j in range(kv_local):
        last = j == kv_local - 1
        mine.append(owners_sum(*halves[j], me, [] if last else [halves[j + 1][1]]))
        if last:
            copies = jnp.broadcast_to(mine[j], (count,) + mine[j].shape[1:])
            queries.append([gather_at_once(copies)])
        else:
            queries.append(gather_doubling(mine[j]))

    fresh_parts = fresh(me, mine, queries[-1][0], block, tokens)
    mixed, waiting = None, None
    for j in range(kv_local):
        last = j == kv_local - 1
        parts = attention(queries[j], block, cache_keys, cache_values, cache_lens, me, j)
        parts = lax.all_to_all(parts.astype(jnp.float16), "seq", 0, 0).astype(jnp.float32)
        after = [waiting[0]] if last and waiting else []
        copies = 1 if waiting or not last else count
        attended = merge(me, parts, *fresh_parts[2 * j : 2 * j + 2], copies, after)
        if j == kv_local - 2:
            waiting = gather_but_last(attended)
            continue
        if last and waiting:
            doubled, attended = pack(*waiting, attended, count)
            before = [doubled, swap(doubled, "seq", 1)]
            mixed = output_part(
                me, place, output_weight, before, tokens, mixed, j - 1, heads, False
            )[0]
        rows = [gather_at_once(attended)] if last else gather_doubling(attended)
        result = output_part(me, place, output_weight, rows, tokens, mixed, j, heads, last)
        mixed = result if last else result[0]

    keep, send = mixed
    mixed = keep + swap(send, "head", 1)
    mask = 2
    while mask < heads:
        bit = place[0] // mask % 2
        pairs = mixed.reshape((-1, 2) + mixed.shape[1:])
        keep = lax.dynamic_index_in_dim(pairs, bit, 1, False)
        send = lax.dynamic_index_in_dim(pairs, 1 - bit, 1, False) * MIXED_SCALE
        received = swap(send.astype(jnp.float16), "head", mask).astype(jnp.float32)
        mixed = keep + received * (1.0 / MIXED_SCALE)
        mask *= 2
    return mixed[0].astype(jnp.bfloat16)


def solution(mesh):
    placed = (
        P(None, "seq"),
        P("seq", "head"),
        P("seq", "head"),
        P("seq", "head"),
        P("head", "seq"),
        P("seq", "head"),
        P("seq", "head"),
        P("seq"),
    )
    return jax.shard_map(
        shards, mesh=mesh, in_specs=placed, out_specs=P("head", "seq"), check_vma=False
    )
```

```python
import functools
import math

import jax
import jax.numpy as jnp
from jax import lax
from jax.experimental import pallas as pl
from jax.experimental.pallas import tpu as pltpu
from jax.sharding import PartitionSpec as P

QH = 64
KVH = 8
HD = 128

NEG_BIG = -1e30
LANES = 128
STAT_ROWS = 8
VMEM_GRANT = 51 << 20
PROJECT_GRANT = 56 << 20
OUTPUT_GRANT = 16 << 20
NT = (((1,), (1,)), ((), ()))

OUTPUT_SCALE = 2.0**12
MIXED_SCALE = 2.0**-3


def vmem_spec():
    return pl.BlockSpec(memory_space=pltpu.VMEM)


def smem_spec():
    return pl.BlockSpec(memory_space=pltpu.SMEM)


def hbm_spec():
    return pl.BlockSpec(memory_space=pl.ANY)


def swap(array, axis, mask):
    size = lax.axis_size(axis)
    return lax.ppermute(array, axis, [(i, i ^ mask) for i in range(size)])


def owners_sum(keep, received, me):
    total = keep + received
    mask = 2
    while mask < lax.axis_size("seq"):
        bit = me // mask % 2
        pairs = total.reshape((-1, 2) + total.shape[1:])
        keep = lax.dynamic_index_in_dim(pairs, bit, 1, False)
        send = lax.dynamic_index_in_dim(pairs, 1 - bit, 1, False)
        total = keep + swap(send, "seq", mask)
        mask *= 2
    return total.astype(jnp.bfloat16)


def doubling_masks(size):
    masks = []
    while size > 2:
        size //= 2
        masks.append(size)
    return masks


def gather_doubling(block):
    for mask in doubling_masks(lax.axis_size("seq")):
        block = jnp.concatenate([block, swap(block, "seq", mask)])
    return [block, swap(block, "seq", 1)]


def doubling_offsets(size):
    offsets = [0]
    for mask in doubling_masks(size):
        offsets = offsets + [offset ^ mask for offset in offsets]
    return offsets + [offset ^ 1 for offset in offsets]


def gather_at_once(copies):
    return lax.all_to_all(copies, "seq", 0, 0)


def project_kernel(me_ref, hidden_ref, *refs, extra, carried, chunk, blocks, pieces):
    weight_refs, refs = refs[: 1 + extra], refs[1 + extra + carried :]
    refs = refs[:2] + refs[2 + carried :]
    keep_ref, send_ref, q_all, *others_all, sems = refs
    tokens, depth = hidden_ref.shape
    odd = lax.rem(me_ref[0], 2) == 1
    rows = depth // pieces
    columns = q_all.shape[1]
    copies = [
        pltpu.make_async_copy(
            weight_refs[0].at[pl.ds(i * rows, rows), pl.ds(chunk * columns, columns)],
            q_all.at[pl.ds(i * rows, rows), :],
            sems.at[i],
        )
        for i in range(pieces)
    ]
    for i in range(extra):
        copies.append(
            pltpu.make_async_copy(weight_refs[1 + i], others_all[i], sems.at[pieces + i])
        )
    for copy in copies:
        copy.start()

    def deal(product, kind):
        block = blocks[kind]
        first = kind * blocks[0]
        parts = [
            product[e * block : (e + 1) * block, c * LANES : (c + 1) * LANES]
            for c in range(product.shape[1] // LANES)
            for e in range(tokens // block)
        ]
        for i, (even_part, odd_part) in enumerate(zip(parts[0::2], parts[1::2])):
            keep_ref[i, first : first + block, :] = jnp.where(odd, odd_part, even_part)
            send_ref[i, first : first + block, :] = jnp.where(odd, even_part, odd_part)

    total = None
    for i in range(pieces):
        copies[i].wait()
        here = slice(i * rows, (i + 1) * rows)
        term = jnp.dot(hidden_ref[:, here], q_all[here, :], preferred_element_type=jnp.float32)
        total = term if total is None else total + term
    deal(total, 0)
    if extra:
        both = []
        for i in range(extra):
            copies[pieces + i].wait()
            both.append(
                jnp.dot(hidden_ref[...], others_all[i][...], preferred_element_type=jnp.float32)
            )
        deal(jnp.concatenate(both, axis=1), 1)


def project(me, hidden, query_weight, others, carried, chunk, columns, count):
    tokens, depth = hidden.shape
    wide = columns + sum(other.shape[1] for other in others)
    pieces = max(1, depth // 256)
    blocks = [width // LANES * tokens // count for width in (columns, wide - columns)]
    shape = jax.ShapeDtypeStruct((count // 2, sum(blocks), LANES), jnp.float32)
    return pl.pallas_call(
        functools.partial(
            project_kernel,
            extra=len(others),
            carried=len(carried),
            chunk=chunk,
            blocks=blocks,
            pieces=pieces,
        ),
        out_shape=[shape] * 2 + [jax.ShapeDtypeStruct(one.shape, one.dtype) for one in carried],
        in_specs=[smem_spec(), vmem_spec()] + [hbm_spec()] * (1 + len(others) + len(carried)),
        out_specs=[vmem_spec()] * 2 + [hbm_spec()] * len(carried),
        input_output_aliases={3 + len(others) + i: 2 + i for i in range(len(carried))},
        scratch_shapes=[pltpu.VMEM((depth, columns), jnp.bfloat16)]
        + [pltpu.VMEM(other.shape, jnp.bfloat16) for other in others]
        + [pltpu.SemaphoreType.DMA((pieces + len(others),))],
        compiler_params=pltpu.CompilerParams(vmem_limit_bytes=PROJECT_GRANT),
        cost_estimate=pl.CostEstimate(
            flops=2 * tokens * depth * wide,
            bytes_accessed=2 * depth * wide,
            transcendentals=0,
        ),
    )(me, hidden, query_weight, *others, *carried)


def attention_kernel(len_ref, me_ref, *refs, sources, band, step, block, head):
    q_refs, refs = refs[:sources], refs[sources:]
    k_hbm, v_hbm, o_ref, k_ref, v_ref, sems = refs[:6]
    s_bufs, m_bufs = refs[6:8], refs[8:10]
    shift, acc, lse_all = refs[10:]
    half = q_refs[0].shape[0]
    rows = sources * half * block
    bands = rows // band
    share = band // block
    scale = math.log2(math.e) / math.sqrt(HD)
    piece = math.gcd(step, 1024)
    tiles = piece // LANES
    lanes = slice(head * HD, (head + 1) * HD)
    offsets = doubling_offsets(sources * half)

    def owner_of(k):
        return k if sources == 1 else me_ref[0] ^ offsets[k]

    length = len_ref[0]
    full = length // step
    rest = length - full * step

    def copy_in(source, target, which, i):
        where = pl.ds(pl.multiple_of(i * step, step), step)
        return pltpu.make_async_copy(
            source.at[where, :], target.at[where, :], sems.at[which, i]
        )

    def keys_in(i):
        return copy_in(k_hbm, k_ref, 0, i)

    def values_in(i):
        return copy_in(v_hbm, v_ref, 1, i)

    needed = (length + step - 1) // step

    def start_keys(i, carry):
        keys_in(i).start()
        return carry

    def start_values(i, carry):
        values_in(i).start()
        return carry

    lax.fori_loop(0, needed, start_keys, 0)
    lax.fori_loop(0, needed, start_values, 0)

    def score(r, i, first, masked):
        source = q_refs[r * share // half]
        at = r * share % half
        q = source[at : at + share, :block, :].reshape(band, HD)
        keys = k_ref[pl.ds(pl.multiple_of(i * step + first, piece), piece), lanes]
        s = lax.dot_general(q, keys, NT, preferred_element_type=jnp.float32)
        if masked:
            column = first + lax.broadcasted_iota(jnp.int32, (band, piece), 1)
            s = jnp.where(column < rest, s, NEG_BIG)
        s_bufs[r % 2][i, :, first : first + piece] = s
        tops = [s[:, c * LANES : (c + 1) * LANES] for c in range(tiles)]
        while len(tops) > 1:
            tops = [jnp.maximum(a, b) for a, b in zip(tops[0::2], tops[1::2])]
        m_bufs[r % 2][...] = jnp.maximum(m_bufs[r % 2][...], tops[0])

    def weigh(r, i, first):
        s = s_bufs[r % 2][i, :, first : first + piece]
        low = shift[...]
        weights = jnp.concatenate(
            [
                jnp.exp2(s[:, c * LANES : (c + 1) * LANES] * scale - low).astype(jnp.bfloat16)
                for c in range(tiles)
            ],
            axis=1,
        )
        values = v_ref[pl.ds(pl.multiple_of(i * step + first, piece), piece), lanes]
        wide = jnp.concatenate([values, jnp.ones((piece, LANES), jnp.bfloat16)], axis=1)
        acc[...] += jnp.dot(weights, wide, preferred_element_type=jnp.float32)

    for r in range(bands + 1):
        scores, weighs = r < bands, r > 0
        if scores:
            m_bufs[r % 2][...] = jnp.full((band, LANES), -3e38, jnp.float32)
        if weighs:
            top = jnp.max(m_bufs[(r - 1) % 2][...], axis=1, keepdims=True)
            shift[...] = jnp.broadcast_to(top * scale, (band, LANES))
            acc[...] = jnp.zeros(acc.shape, jnp.float32)

        def both(i, masked):
            if r == 0:
                keys_in(i).wait()
            if r == 1:
                values_in(i).wait()
            for first in range(0, step, piece):
                if weighs:
                    weigh(r - 1, i, first)
                if scores:
                    score(r, i, first, masked)

        def body(i, carry):
            both(i, False)
            return carry

        lax.fori_loop(0, full, body, 0)

        @pl.when(rest > 0)
        def _():
            both(full, True)

        if weighs:
            totals = acc[:, LANES:]
            mean = acc[:, :LANES] / totals * OUTPUT_SCALE
            levels = shift[...] + jnp.log2(totals)
            for e in range(share):
                k = (r - 1) * share + e
                owner = owner_of(k)
                here = slice(e * block, (e + 1) * block)
                o_ref[owner, :block, :] = mean[here, :]
                lse_all[pl.ds(pl.multiple_of(owner * block, block), block), :] = levels[here, :]

    per = LANES // block
    row = lax.broadcasted_iota(jnp.int32, (STAT_ROWS, LANES), 0)
    for g in range(rows // LANES):
        level = lse_all[g * LANES : (g + 1) * LANES, :].T[:STAT_ROWS, :]
        exponent = jnp.floor(jnp.log2(jnp.maximum(jnp.abs(level), 1e-30)))
        exponent = jnp.minimum(exponent, 120.0)
        rest_of = level * jnp.exp2(-exponent)
        first = jnp.floor(rest_of * 2.0**9 + 0.5)
        rest_of = rest_of - first * 2.0**-9
        second = jnp.floor(rest_of * 2.0**20 + 0.5)
        third = (rest_of - second * 2.0**-20) * 2.0**31
        stats = jnp.where(row == 0, exponent, jnp.where(row == 1, first, second))
        stats = jnp.where(row >= 3, third, stats)
        for e in range(per):
            o_ref[g * per + e, block:, :] = stats


def attention(queries, block, keys, values, length, me, head):
    sources = len(queries)
    count = sources * queries[0].shape[0]
    rows, slots = count * block, keys.shape[0]
    band = math.gcd(rows // 2, 512)
    step = math.gcd(slots, 2048)
    return pl.pallas_call(
        functools.partial(
            attention_kernel, sources=sources, band=band, step=step, block=block, head=head
        ),
        out_shape=jax.ShapeDtypeStruct((count, block + STAT_ROWS, HD), jnp.float32),
        in_specs=[smem_spec()] * 2 + [vmem_spec()] * sources + [hbm_spec()] * 2,
        out_specs=vmem_spec(),
        scratch_shapes=[
            pltpu.VMEM(keys.shape, keys.dtype),
            pltpu.VMEM(values.shape, values.dtype),
            pltpu.SemaphoreType.DMA((2, slots // step)),
            pltpu.VMEM((slots // step, band, step), jnp.float32),
            pltpu.VMEM((slots // step, band, step), jnp.float32),
            pltpu.VMEM((band, LANES), jnp.float32),
            pltpu.VMEM((band, LANES), jnp.float32),
            pltpu.VMEM((band, LANES), jnp.float32),
            pltpu.VMEM((band, 2 * LANES), jnp.float32),
            pltpu.VMEM((rows, LANES), jnp.float32),
        ],
        compiler_params=pltpu.CompilerParams(vmem_limit_bytes=VMEM_GRANT),
        cost_estimate=pl.CostEstimate(
            flops=8 * rows * slots * HD,
            bytes_accessed=4 * slots * HD,
            transcendentals=rows * slots,
        ),
    )(length, me, *queries, keys, values)


def fresh_kernel(me_ref, *refs, heads, block, tokens):
    q_refs, last_ref, outs, kv_all = refs[:heads], refs[heads], refs[heads + 1 : -1], refs[-1]
    kv_block = last_ref.shape[1] - block
    for k in range(last_ref.shape[0]):
        rows = last_ref[k, block:, :].astype(jnp.float32)
        kv_all[k * kv_block : (k + 1) * kv_block, :] = rows
    half = heads * tokens
    for head in range(heads):
        q_ref, (out_ref, stat_ref) = q_refs[head], outs[2 * head : 2 * head + 2]
        first = head * tokens
        keys = kv_all[first : first + tokens, :].astype(jnp.bfloat16)
        values = kv_all[half + first : half + first + tokens, :].astype(jnp.bfloat16)
        s = lax.dot_general(q_ref[0, :block, :], keys, NT, preferred_element_type=jnp.float32)
        s = s * (math.log2(math.e) / math.sqrt(HD))
        token = lax.rem(me_ref[0] * block, tokens) + lax.broadcasted_iota(jnp.int32, s.shape, 0)
        visible = lax.broadcasted_iota(jnp.int32, s.shape, 1) <= token
        s = jnp.where(visible, s, NEG_BIG)
        top = jnp.max(s, axis=1, keepdims=True)
        weights = jnp.where(visible, jnp.exp2(s - top), 0.0).astype(jnp.bfloat16)
        total = jnp.sum(weights.astype(jnp.float32), axis=1, keepdims=True)
        out_ref[...] = jnp.dot(weights, values, preferred_element_type=jnp.float32)
        lane = lax.broadcasted_iota(jnp.int32, stat_ref.shape, 1)
        stat_ref[...] = jnp.where(lane < LANES // 2, top, total)


def fresh(me, mine, last, block, tokens):
    heads = len(mine)
    kv_rows = last.shape[0] * (last.shape[1] - block)
    return pl.pallas_call(
        functools.partial(fresh_kernel, heads=heads, block=block, tokens=tokens),
        out_shape=[jax.ShapeDtypeStruct((block, HD), jnp.float32)] * (2 * heads),
        in_specs=[smem_spec()] + [vmem_spec()] * (heads + 1),
        out_specs=[vmem_spec()] * (2 * heads),
        scratch_shapes=[pltpu.VMEM((kv_rows, HD), jnp.float32)],
    )(me, *mine, last)


def merge_kernel(me_ref, part_ref, out_ref, stat_ref, *refs):
    copies_ref, turned = refs[-2:]
    count = part_ref.shape[0]
    block = out_ref.shape[0]
    new_top = stat_ref[:, 0:1]
    new_total = stat_ref[:, LANES // 2 : LANES // 2 + 1]

    place = lax.rem(me_ref[0], LANES // block)
    pieces = part_ref[:, block : block + 4, :]
    level = pieces[:, 1, :] * 2.0**-9 + pieces[:, 2, :] * 2.0**-20 + pieces[:, 3, :] * 2.0**-31
    turned[...] = (level * jnp.exp2(pieces[:, 0, :])).T
    levels = turned[pl.ds(pl.multiple_of(place * block, block), block), :]
    joint = jnp.maximum(new_top, jnp.max(levels, axis=1, keepdims=True))
    factors = jnp.exp2(levels - joint)
    new_scale = jnp.exp2(new_top - joint)
    whole_out = out_ref[...] * new_scale
    whole_total = new_total * new_scale + jnp.sum(factors, axis=1, keepdims=True)
    scaled = factors * (1.0 / OUTPUT_SCALE)
    for k in range(count):
        whole_out = whole_out + part_ref[k, :block, :] * scaled[:, k : k + 1]
    attended = (whole_out / whole_total).astype(jnp.bfloat16)
    for k in range(copies_ref.shape[0]):
        for i, ref in enumerate(refs[:-2]):
            copies_ref[k, i * block : (i + 1) * block, :] = ref[0]
        copies_ref[k, (len(refs) - 2) * block :, :] = attended


def merge(me, parts, new_out, new_stat, before, copies):
    block = new_out.shape[0]
    shape = (copies, (len(before) + 1) * block, HD)
    return pl.pallas_call(
        merge_kernel,
        out_shape=jax.ShapeDtypeStruct(shape, jnp.bfloat16),
        in_specs=[smem_spec()] + [vmem_spec()] * (3 + len(before)),
        out_specs=vmem_spec(),
        scratch_shapes=[pltpu.VMEM((LANES, parts.shape[0]), jnp.float32)],
    )(me, parts, new_out, new_stat, *before)


def output_kernel(place_ref, w_ref, a_ref, keep_ref, send_ref, total, *, block):
    count, rows = a_ref.shape[:2]
    tokens = total.shape[0]
    per = tokens // block
    groups = count // per
    product = None
    for j in range(rows // block):
        here = slice(j * block, (j + 1) * block)
        pieces = [
            a_ref[g * per : (g + 1) * per, here, :].reshape(tokens, HD) for g in range(groups)
        ]
        term = jnp.dot(
            jnp.concatenate(pieces, axis=1),
            w_ref[j * groups * HD : (j + 1) * groups * HD, :],
            preferred_element_type=jnp.float32,
        )
        product = term if product is None else product + term
    total[...] = product
    share = keep_ref.shape[1]
    odd = lax.rem(place_ref[0], 2)
    for i in range(keep_ref.shape[0]):
        for ref, parity in ((keep_ref, odd), (send_ref, 1 - odd)):
            start = pl.multiple_of((2 * i + parity) * share, share)
            ref[i] = total[pl.ds(start, share), :]


def output_halves(place, weight, attended, block, tokens, heads):
    depth, width = weight.shape
    shape = jax.ShapeDtypeStruct((heads // 2, tokens // heads, width), jnp.float32)
    return pl.pallas_call(
        functools.partial(output_kernel, block=block),
        out_shape=[shape] * 2,
        in_specs=[smem_spec()] + [vmem_spec()] * 2,
        out_specs=[vmem_spec()] * 2,
        scratch_shapes=[pltpu.VMEM((tokens, width), jnp.float32)],
        compiler_params=pltpu.CompilerParams(vmem_limit_bytes=OUTPUT_GRANT),
        cost_estimate=pl.CostEstimate(
            flops=2 * tokens * depth * width,
            bytes_accessed=2 * depth * width,
            transcendentals=0,
        ),
    )(place, weight, attended)


def shards(
    hidden,
    query_weight,
    key_weight,
    value_weight,
    output_weight,
    cache_keys,
    cache_values,
    cache_lens,
):
    tokens = hidden.shape[0]
    count = lax.axis_size("seq")
    heads = lax.axis_size("head")
    kv_local = cache_keys.shape[1] // HD
    columns = (QH // KVH) * HD
    block = (QH // KVH) * tokens // count
    me = lax.axis_index("seq").reshape(1)
    place = lax.axis_index("head").reshape(1)

    kept, received = [], []
    for j in range(kv_local):
        others = [key_weight, value_weight] if j == kv_local - 1 else []
        keep, send, *kept = project(
            me, hidden, query_weight, others, kept, j, columns, count
        )
        kept.append(keep)
        received.append(swap(send, "seq", 1))
    mine, queries = [], []
    for j in range(kv_local):
        mine.append(owners_sum(kept[j], received[j], me[0]))
        if j == kv_local - 1:
            copies = jnp.broadcast_to(mine[j], (count,) + mine[j].shape[1:])
            queries.append([gather_at_once(copies)])
        else:
            queries.append(gather_doubling(mine[j]))

    fresh_parts = fresh(me, mine, queries[-1][0], block, tokens)
    before = []
    for j in range(kv_local):
        parts = attention(queries[j], block, cache_keys, cache_values, cache_lens, me, j)
        parts = lax.all_to_all(parts.astype(jnp.float16), "seq", 0, 0).astype(jnp.float32)
        new_out, new_stat = fresh_parts[2 * j : 2 * j + 2]
        last = j == kv_local - 1
        attended = merge(
            me, parts, new_out, new_stat, before if last else [], count if last else 1
        )
        before.append(attended)
    attended = gather_at_once(before[-1])
    mixed = output_halves(place, output_weight, attended, block, tokens, heads)

    keep, send = mixed
    mixed = keep + swap(send, "head", 1)
    mask = 2
    while mask < heads:
        bit = place[0] // mask % 2
        pairs = mixed.reshape((-1, 2) + mixed.shape[1:])
        keep = lax.dynamic_index_in_dim(pairs, bit, 1, False)
        send = lax.dynamic_index_in_dim(pairs, 1 - bit, 1, False) * MIXED_SCALE
        received = swap(send.astype(jnp.float16), "head", mask).astype(jnp.float32)
        mixed = keep + received * (1.0 / MIXED_SCALE)
        mask *= 2
    return mixed[0].astype(jnp.bfloat16)


def solution(mesh):
    placed = (
        P(None, "seq"),
        P("seq", "head"),
        P("seq", "head"),
        P("seq", "head"),
        P("head", "seq"),
        P("seq", "head"),
        P("seq", "head"),
        P("seq"),
    )
    return jax.shard_map(
        shards, mesh=mesh, in_specs=placed, out_specs=P("head", "seq"), check_vma=False
    )
```

```python
import functools
import math

import jax
import jax.numpy as jnp
from jax import lax
from jax.experimental import pallas as pl
from jax.experimental.pallas import tpu as pltpu
from jax.sharding import PartitionSpec as P

QH = 64
KVH = 8
HD = 128

NEG_BIG = -1e30
LANES = 128
STAT_ROWS = 8
VMEM_GRANT = 51 << 20
PROJECT_GRANT = 56 << 20
SMALL_GRANT = 16 << 20
NT = (((1,), (1,)), ((), ()))

OUTPUT_SCALE = 2.0**12
MIXED_SCALE = 2.0**-3


def vmem_spec():
    return pl.BlockSpec(memory_space=pltpu.VMEM)


def smem_spec():
    return pl.BlockSpec(memory_space=pltpu.SMEM)


def hbm_spec():
    return pl.BlockSpec(memory_space=pl.ANY)


def swap(array, axis, mask):
    size = lax.axis_size(axis)
    return lax.ppermute(array, axis, [(i, i ^ mask) for i in range(size)])


def owners_sum(keep, received, me):
    total = keep + received
    mask = 2
    while mask < lax.axis_size("seq"):
        bit = me // mask % 2
        pairs = total.reshape((-1, 2) + total.shape[1:])
        keep = lax.dynamic_index_in_dim(pairs, bit, 1, False)
        send = lax.dynamic_index_in_dim(pairs, 1 - bit, 1, False)
        total = keep + swap(send, "seq", mask)
        mask *= 2
    return total.astype(jnp.bfloat16)


def doubling_masks(size):
    masks = []
    while size > 2:
        size //= 2
        masks.append(size)
    return masks


def gather_doubling(block):
    for mask in doubling_masks(lax.axis_size("seq")):
        block = jnp.concatenate([block, swap(block, "seq", mask)])
    return [block, swap(block, "seq", 1)]


def doubling_offsets(size):
    offsets = [0]
    for mask in doubling_masks(size):
        offsets = offsets + [offset ^ mask for offset in offsets]
    return offsets + [offset ^ 1 for offset in offsets]


def gather_at_once(copies):
    return lax.all_to_all(copies, "seq", 0, 0)


def project_kernel(me_ref, hidden_ref, *refs, extra, carried, chunk, blocks, pieces):
    weight_refs, refs = refs[: 1 + extra], refs[1 + extra + carried :]
    refs = refs[:2] + refs[2 + carried :]
    keep_ref, send_ref, q_all, *others_all, sems = refs
    tokens, depth = hidden_ref.shape
    odd = lax.rem(me_ref[0], 2) == 1
    rows = depth // pieces
    columns = q_all.shape[1]
    copies = [
        pltpu.make_async_copy(
            weight_refs[0].at[pl.ds(i * rows, rows), pl.ds(chunk * columns, columns)],
            q_all.at[pl.ds(i * rows, rows), :],
            sems.at[i],
        )
        for i in range(pieces)
    ]
    for i in range(extra):
        copies.append(
            pltpu.make_async_copy(weight_refs[1 + i], others_all[i], sems.at[pieces + i])
        )
    for copy in copies:
        copy.start()

    def deal(product, kind):
        block = blocks[kind]
        first = kind * blocks[0]
        parts = [
            product[e * block : (e + 1) * block, c * LANES : (c + 1) * LANES]
            for c in range(product.shape[1] // LANES)
            for e in range(tokens // block)
        ]
        for i, (even_part, odd_part) in enumerate(zip(parts[0::2], parts[1::2])):
            keep_ref[i, first : first + block, :] = jnp.where(odd, odd_part, even_part)
            send_ref[i, first : first + block, :] = jnp.where(odd, even_part, odd_part)

    total = None
    for i in range(pieces):
        copies[i].wait()
        here = slice(i * rows, (i + 1) * rows)
        term = jnp.dot(hidden_ref[:, here], q_all[here, :], preferred_element_type=jnp.float32)
        total = term if total is None else total + term
    deal(total, 0)
    if extra:
        both = []
        for i in range(extra):
            copies[pieces + i].wait()
            both.append(
                jnp.dot(hidden_ref[...], others_all[i][...], preferred_element_type=jnp.float32)
            )
        deal(jnp.concatenate(both, axis=1), 1)


def project(me, hidden, query_weight, others, carried, chunk, columns, count):
    tokens, depth = hidden.shape
    wide = columns + sum(other.shape[1] for other in others)
    pieces = max(1, depth // 256)
    blocks = [width // LANES * tokens // count for width in (columns, wide - columns)]
    shape = jax.ShapeDtypeStruct((count // 2, sum(blocks), LANES), jnp.float32)
    return pl.pallas_call(
        functools.partial(
            project_kernel,
            extra=len(others),
            carried=len(carried),
            chunk=chunk,
            blocks=blocks,
            pieces=pieces,
        ),
        out_shape=[shape] * 2 + [jax.ShapeDtypeStruct(one.shape, one.dtype) for one in carried],
        in_specs=[smem_spec(), vmem_spec()] + [hbm_spec()] * (1 + len(others) + len(carried)),
        out_specs=[vmem_spec()] * 2 + [hbm_spec()] * len(carried),
        input_output_aliases={3 + len(others) + i: 2 + i for i in range(len(carried))},
        scratch_shapes=[pltpu.VMEM((depth, columns), jnp.bfloat16)]
        + [pltpu.VMEM(other.shape, jnp.bfloat16) for other in others]
        + [pltpu.SemaphoreType.DMA((pieces + len(others),))],
        compiler_params=pltpu.CompilerParams(vmem_limit_bytes=PROJECT_GRANT),
        cost_estimate=pl.CostEstimate(
            flops=2 * tokens * depth * wide,
            bytes_accessed=2 * depth * wide,
            transcendentals=0,
        ),
    )(me, hidden, query_weight, *others, *carried)


def attention_kernel(len_ref, me_ref, *refs, sources, band, step, block, head):
    q_refs, refs = refs[:sources], refs[sources:]
    k_hbm, v_hbm, o_ref, k_ref, v_ref, sems = refs[:6]
    s_bufs, m_bufs = refs[6:8], refs[8:10]
    shift, acc, lse_all = refs[10:]
    half = q_refs[0].shape[0]
    rows = sources * half * block
    bands = rows // band
    share = band // block
    scale = math.log2(math.e) / math.sqrt(HD)
    piece = math.gcd(step, 1024)
    tiles = piece // LANES
    fold = math.gcd(band, 128)
    lanes = slice(head * HD, (head + 1) * HD)
    offsets = doubling_offsets(sources * half)

    def owner_of(k):
        return k if sources == 1 else me_ref[0] ^ offsets[k]

    length = len_ref[0]
    full = length // step
    rest = length - full * step

    def copy_in(source, target, which, i):
        where = pl.ds(pl.multiple_of(i * step, step), step)
        return pltpu.make_async_copy(
            source.at[where, :], target.at[where, :], sems.at[which, i]
        )

    def keys_in(i):
        return copy_in(k_hbm, k_ref, 0, i)

    def values_in(i):
        return copy_in(v_hbm, v_ref, 1, i)

    needed = (length + step - 1) // step

    def start_keys(i, carry):
        keys_in(i).start()
        return carry

    def start_values(i, carry):
        values_in(i).start()
        return carry

    lax.fori_loop(0, needed, start_keys, 0)
    lax.fori_loop(0, needed, start_values, 0)

    def score(r, i, first, masked):
        source = q_refs[r * share // half]
        at = r * share % half
        q = source[at : at + share, :block, :].reshape(band, HD)
        keys = k_ref[pl.ds(pl.multiple_of(i * step + first, piece), piece), lanes]
        s = lax.dot_general(q, keys, NT, preferred_element_type=jnp.float32)
        if masked:
            column = first + lax.broadcasted_iota(jnp.int32, (band, piece), 1)
            s = jnp.where(column < rest, s, NEG_BIG)
        s_bufs[r % 2][i, :, first : first + piece] = s
        tops = [s[:, c * LANES : (c + 1) * LANES] for c in range(tiles)]
        while len(tops) > 1:
            tops = [jnp.maximum(a, b) for a, b in zip(tops[0::2], tops[1::2])]
        m_bufs[r % 2][...] = jnp.maximum(m_bufs[r % 2][...], tops[0])

    def weigh(r, i, first):
        blocks = []
        for top in range(0, band, fold):
            here = slice(top, top + fold)
            low = shift[here, :]
            tiled = [
                s_bufs[r % 2][i, here, first + c * LANES : first + (c + 1) * LANES]
                for c in range(tiles)
            ]
            tiled = [jnp.exp2(s * scale - low).astype(jnp.bfloat16) for s in tiled]
            blocks.append(jnp.concatenate(tiled, axis=1))
        weights = jnp.concatenate(blocks, axis=0)
        values = v_ref[pl.ds(pl.multiple_of(i * step + first, piece), piece), lanes]
        wide = jnp.concatenate([values, jnp.ones((piece, LANES), jnp.bfloat16)], axis=1)
        acc[...] += jnp.dot(weights, wide, preferred_element_type=jnp.float32)

    for r in range(bands + 1):
        scores, weighs = r < bands, r > 0
        if scores:
            m_bufs[r % 2][...] = jnp.full((band, LANES), -3e38, jnp.float32)
        if weighs:
            top = jnp.max(m_bufs[(r - 1) % 2][...], axis=1, keepdims=True)
            shift[...] = jnp.broadcast_to(top * scale, (band, LANES))
            acc[...] = jnp.zeros(acc.shape, jnp.float32)

        def both(i, masked):
            if r == 0:
                keys_in(i).wait()
            if r == 1:
                values_in(i).wait()
            for first in range(0, step, piece):
                if weighs:
                    weigh(r - 1, i, first)
                if scores:
                    score(r, i, first, masked)

        def body(i, carry):
            both(i, False)
            return carry

        lax.fori_loop(0, full, body, 0)

        @pl.when(rest > 0)
        def _():
            both(full, True)

        if weighs:
            totals = acc[:, LANES:]
            mean = acc[:, :LANES] / totals * OUTPUT_SCALE
            levels = shift[...] + jnp.log2(totals)
            for e in range(share):
                k = (r - 1) * share + e
                owner = owner_of(k)
                here = slice(e * block, (e + 1) * block)
                o_ref[owner, :block, :] = mean[here, :]
                lse_all[pl.ds(pl.multiple_of(owner * block, block), block), :] = levels[here, :]

    per = LANES // block
    for g in range(rows // LANES):
        stats = encode_levels(lse_all[g * LANES : (g + 1) * LANES, :].T[:STAT_ROWS, :])
        for e in range(per):
            o_ref[g * per + e, block:, :] = stats


def encode_levels(level):
    row = lax.broadcasted_iota(jnp.int32, level.shape, 0)
    exponent = jnp.floor(jnp.log2(jnp.maximum(jnp.abs(level), 1e-30)))
    exponent = jnp.minimum(exponent, 120.0)
    rest = level * jnp.exp2(-exponent)
    first = jnp.floor(rest * 2.0**9 + 0.5)
    rest = rest - first * 2.0**-9
    second = jnp.floor(rest * 2.0**20 + 0.5)
    third = (rest - second * 2.0**-20) * 2.0**31
    stats = jnp.where(row == 0, exponent, jnp.where(row == 1, first, second))
    return jnp.where(row >= 3, third, stats)


def flipped_kernel(len_ref, me_ref, *refs, sources, band, step, block, head):
    q_refs, refs = refs[:sources], refs[sources:]
    k_hbm, v_hbm, o_ref, k_ref, v_ref, sems = refs[:6]
    s_bufs, m_bufs = refs[6:8], refs[8:10]
    shift, acc, turned = refs[10:]
    half = q_refs[0].shape[0]
    bands = sources * half * block // band
    share = band // block
    scale = math.log2(math.e) / math.sqrt(HD)
    piece = math.gcd(step, 1024)
    lanes = slice(head * HD, (head + 1) * HD)
    offsets = doubling_offsets(sources * half)

    def owner_of(k):
        return k if sources == 1 else me_ref[0] ^ offsets[k]

    length = len_ref[0]
    full = length // step
    rest = length - full * step
    needed = (length + step - 1) // step

    def copy_in(source, target, which, i):
        where = pl.ds(pl.multiple_of(i * step, step), step)
        return pltpu.make_async_copy(
            source.at[where, :], target.at[where, :], sems.at[which, i]
        )

    def keys_in(i):
        return copy_in(k_hbm, k_ref, 0, i)

    def values_in(i):
        return copy_in(v_hbm, v_ref, 1, i)

    def start_keys(i, carry):
        keys_in(i).start()
        return carry

    def start_values(i, carry):
        values_in(i).start()
        return carry

    lax.fori_loop(0, needed, start_keys, 0)
    lax.fori_loop(0, needed, start_values, 0)
    turned[HD:, :] = jnp.ones((turned.shape[0] - HD, turned.shape[1]), jnp.bfloat16)

    def score(r, i, first, masked):
        source = q_refs[r * share // half]
        at = r * share % half
        q = source[at : at + share, :block, :].reshape(band, HD)
        keys = k_ref[pl.ds(pl.multiple_of(i * step + first, piece), piece), lanes]
        s = lax.dot_general(keys, q, NT, preferred_element_type=jnp.float32)
        if masked:
            slot = first + lax.broadcasted_iota(jnp.int32, s.shape, 0)
            s = jnp.where(slot < rest, s, NEG_BIG)
        s_bufs[r % 2][i, first : first + piece, :] = s
        tops = jnp.max(s.reshape(piece // 8, 8, band), axis=0)
        m_bufs[r % 2][...] = jnp.maximum(m_bufs[r % 2][...], tops)

    def weigh(r, i, first):
        here = pl.ds(pl.multiple_of(i * step + first, piece), piece)
        if r == 0:
            turned[:HD, here] = v_ref[here, lanes].T
        s = s_bufs[r % 2][i, first : first + piece, :]
        weights = jnp.exp2(s * scale - shift[0:1, :]).astype(jnp.bfloat16)
        acc[...] += jnp.dot(turned[:, here], weights, preferred_element_type=jnp.float32)

    for r in range(bands + 1):
        scores, weighs = r < bands, r > 0
        if scores:
            m_bufs[r % 2][...] = jnp.full((8, band), -3e38, jnp.float32)
        if weighs:
            top = jnp.max(m_bufs[(r - 1) % 2][...], axis=0, keepdims=True)
            shift[...] = jnp.broadcast_to(top * scale, (8, band))
            acc[...] = jnp.zeros(acc.shape, jnp.float32)

        def both(i, masked):
            if r == 0:
                keys_in(i).wait()
            if r == 1:
                values_in(i).wait()
            for first in range(0, step, piece):
                if weighs:
                    weigh(r - 1, i, first)
                if scores:
                    score(r, i, first, masked)

        def body(i, carry):
            both(i, False)
            return carry

        lax.fori_loop(0, full, body, 0)

        @pl.when(rest > 0)
        def _():
            both(full, True)

        if weighs:
            totals = acc[HD : HD + 8, :]
            levels = encode_levels(shift[...] + jnp.log2(totals))
            for e in range(share):
                owner = owner_of((r - 1) * share + e)
                here = slice(e * block, (e + 1) * block)
                mean = acc[:HD, here] * (OUTPUT_SCALE / totals[0:1, here])
                o_ref[owner, :block, :] = mean.T
                o_ref[owner, block:, :] = levels[:, here]


def attention(queries, block, keys, values, length, me, head, flipped):
    sources = len(queries)
    count = sources * queries[0].shape[0]
    rows, slots = count * block, keys.shape[0]
    band = math.gcd(rows // 2, 512)
    step = math.gcd(slots, 2048)
    steps = slots // step
    if flipped:
        kernel = flipped_kernel
        scratch = [
            pltpu.VMEM((steps, step, band), jnp.float32),
            pltpu.VMEM((steps, step, band), jnp.float32),
            pltpu.VMEM((8, band), jnp.float32),
            pltpu.VMEM((8, band), jnp.float32),
            pltpu.VMEM((8, band), jnp.float32),
            pltpu.VMEM((HD + 16, band), jnp.float32),
            pltpu.VMEM((HD + 16, slots), jnp.bfloat16),
        ]
    else:
        kernel = attention_kernel
        scratch = [
            pltpu.VMEM((steps, band, step), jnp.float32),
            pltpu.VMEM((steps, band, step), jnp.float32),
            pltpu.VMEM((band, LANES), jnp.float32),
            pltpu.VMEM((band, LANES), jnp.float32),
            pltpu.VMEM((band, LANES), jnp.float32),
            pltpu.VMEM((band, 2 * LANES), jnp.float32),
            pltpu.VMEM((rows, LANES), jnp.float32),
        ]
    return pl.pallas_call(
        functools.partial(
            kernel, sources=sources, band=band, step=step, block=block, head=head
        ),
        out_shape=jax.ShapeDtypeStruct((count, block + STAT_ROWS, HD), jnp.float32),
        in_specs=[smem_spec()] * 2 + [vmem_spec()] * sources + [hbm_spec()] * 2,
        out_specs=vmem_spec(),
        scratch_shapes=[
            pltpu.VMEM(keys.shape, keys.dtype),
            pltpu.VMEM(values.shape, values.dtype),
            pltpu.SemaphoreType.DMA((2, steps)),
        ]
        + scratch,
        compiler_params=pltpu.CompilerParams(vmem_limit_bytes=VMEM_GRANT),
        cost_estimate=pl.CostEstimate(
            flops=8 * rows * slots * HD,
            bytes_accessed=4 * slots * HD,
            transcendentals=rows * slots,
        ),
    )(length, me, *queries, keys, values)


def fresh_kernel(me_ref, *refs, heads, block, tokens):
    q_refs, last_ref, outs, kv_all = refs[:heads], refs[heads], refs[heads + 1 : -1], refs[-1]
    kv_block = last_ref.shape[1] - block
    for k in range(last_ref.shape[0]):
        rows = last_ref[k, block:, :].astype(jnp.float32)
        kv_all[k * kv_block : (k + 1) * kv_block, :] = rows
    half = heads * tokens
    for head in range(heads):
        q_ref, (out_ref, stat_ref) = q_refs[head], outs[2 * head : 2 * head + 2]
        first = head * tokens
        keys = kv_all[first : first + tokens, :].astype(jnp.bfloat16)
        values = kv_all[half + first : half + first + tokens, :].astype(jnp.bfloat16)
        s = lax.dot_general(q_ref[0, :block, :], keys, NT, preferred_element_type=jnp.float32)
        s = s * (math.log2(math.e) / math.sqrt(HD))
        token = lax.rem(me_ref[0] * block, tokens) + lax.broadcasted_iota(jnp.int32, s.shape, 0)
        visible = lax.broadcasted_iota(jnp.int32, s.shape, 1) <= token
        s = jnp.where(visible, s, NEG_BIG)
        top = jnp.max(s, axis=1, keepdims=True)
        weights = jnp.where(visible, jnp.exp2(s - top), 0.0).astype(jnp.bfloat16)
        total = jnp.sum(weights.astype(jnp.float32), axis=1, keepdims=True)
        out_ref[...] = jnp.dot(weights, values, preferred_element_type=jnp.float32)
        lane = lax.broadcasted_iota(jnp.int32, stat_ref.shape, 1)
        stat_ref[...] = jnp.where(lane < LANES // 2, top, total)


def fresh(me, mine, last, block, tokens):
    heads = len(mine)
    kv_rows = last.shape[0] * (last.shape[1] - block)
    return pl.pallas_call(
        functools.partial(fresh_kernel, heads=heads, block=block, tokens=tokens),
        out_shape=[jax.ShapeDtypeStruct((block, HD), jnp.float32)] * (2 * heads),
        in_specs=[smem_spec()] + [vmem_spec()] * (heads + 1),
        out_specs=[vmem_spec()] * (2 * heads),
        scratch_shapes=[pltpu.VMEM((kv_rows, HD), jnp.float32)],
        compiler_params=pltpu.CompilerParams(vmem_limit_bytes=SMALL_GRANT),
    )(me, *mine, last)


def merge_kernel(me_ref, part_ref, out_ref, stat_ref, *refs):
    copies_ref, turned = refs[-2:]
    count = part_ref.shape[0]
    block = out_ref.shape[0]
    new_top = stat_ref[:, 0:1]
    new_total = stat_ref[:, LANES // 2 : LANES // 2 + 1]

    place = lax.rem(me_ref[0], LANES // block)
    pieces = part_ref[:, block : block + 4, :]
    level = pieces[:, 1, :] * 2.0**-9 + pieces[:, 2, :] * 2.0**-20 + pieces[:, 3, :] * 2.0**-31
    turned[...] = (level * jnp.exp2(pieces[:, 0, :])).T
    levels = turned[pl.ds(pl.multiple_of(place * block, block), block), :]
    joint = jnp.maximum(new_top, jnp.max(levels, axis=1, keepdims=True))
    factors = jnp.exp2(levels - joint)
    new_scale = jnp.exp2(new_top - joint)
    whole_out = out_ref[...] * new_scale
    whole_total = new_total * new_scale + jnp.sum(factors, axis=1, keepdims=True)
    scaled = factors * (1.0 / OUTPUT_SCALE)
    for k in range(count):
        whole_out = whole_out + part_ref[k, :block, :] * scaled[:, k : k + 1]
    attended = (whole_out / whole_total).astype(jnp.bfloat16)
    for k in range(copies_ref.shape[0]):
        for i, ref in enumerate(refs[:-2]):
            copies_ref[k, i * block : (i + 1) * block, :] = ref[0]
        copies_ref[k, (len(refs) - 2) * block :, :] = attended


def merge(me, parts, new_out, new_stat, before, copies):
    block = new_out.shape[0]
    shape = (copies, (len(before) + 1) * block, HD)
    return pl.pallas_call(
        merge_kernel,
        out_shape=jax.ShapeDtypeStruct(shape, jnp.bfloat16),
        in_specs=[smem_spec()] + [vmem_spec()] * (3 + len(before)),
        out_specs=vmem_spec(),
        scratch_shapes=[pltpu.VMEM((LANES, parts.shape[0]), jnp.float32)],
        compiler_params=pltpu.CompilerParams(vmem_limit_bytes=SMALL_GRANT),
    )(me, parts, new_out, new_stat, *before)


def output_kernel(place_ref, w_ref, a_ref, keep_ref, send_ref, total, *, block):
    count, rows = a_ref.shape[:2]
    tokens = total.shape[0]
    per = tokens // block
    groups = count // per
    product = None
    for j in range(rows // block):
        here = slice(j * block, (j + 1) * block)
        pieces = [
            a_ref[g * per : (g + 1) * per, here, :].reshape(tokens, HD) for g in range(groups)
        ]
        term = jnp.dot(
            jnp.concatenate(pieces, axis=1),
            w_ref[j * groups * HD : (j + 1) * groups * HD, :],
            preferred_element_type=jnp.float32,
        )
        product = term if product is None else product + term
    total[...] = product
    share = keep_ref.shape[1]
    odd = lax.rem(place_ref[0], 2)
    for i in range(keep_ref.shape[0]):
        for ref, parity in ((keep_ref, odd), (send_ref, 1 - odd)):
            start = pl.multiple_of((2 * i + parity) * share, share)
            ref[i] = total[pl.ds(start, share), :]


def output_halves(place, weight, attended, block, tokens, heads):
    depth, width = weight.shape
    shape = jax.ShapeDtypeStruct((heads // 2, tokens // heads, width), jnp.float32)
    return pl.pallas_call(
        functools.partial(output_kernel, block=block),
        out_shape=[shape] * 2,
        in_specs=[smem_spec()] + [vmem_spec()] * 2,
        out_specs=[vmem_spec()] * 2,
        scratch_shapes=[pltpu.VMEM((tokens, width), jnp.float32)],
        compiler_params=pltpu.CompilerParams(vmem_limit_bytes=SMALL_GRANT),
        cost_estimate=pl.CostEstimate(
            flops=2 * tokens * depth * width,
            bytes_accessed=2 * depth * width,
            transcendentals=0,
        ),
    )(place, weight, attended)


def shards(
    hidden,
    query_weight,
    key_weight,
    value_weight,
    output_weight,
    cache_keys,
    cache_values,
    cache_lens,
):
    tokens = hidden.shape[0]
    count = lax.axis_size("seq")
    heads = lax.axis_size("head")
    kv_local = cache_keys.shape[1] // HD
    columns = (QH // KVH) * HD
    block = (QH // KVH) * tokens // count
    me = lax.axis_index("seq").reshape(1)
    place = lax.axis_index("head").reshape(1)

    kept, received = [], []
    for j in range(kv_local):
        others = [key_weight, value_weight] if j == kv_local - 1 else []
        keep, send, *kept = project(
            me, hidden, query_weight, others, kept, j, columns, count
        )
        kept.append(keep)
        received.append(swap(send, "seq", 1))
    mine, queries = [], []
    for j in range(kv_local):
        mine.append(owners_sum(kept[j], received[j], me[0]))
        if j == kv_local - 1:
            copies = jnp.broadcast_to(mine[j], (count,) + mine[j].shape[1:])
            queries.append([gather_at_once(copies)])
        else:
            queries.append(gather_doubling(mine[j]))

    fresh_parts = fresh(me, mine, queries[-1][0], block, tokens)
    before = []
    for j in range(kv_local):
        flipped = j == 0 and block % LANES == 0
        parts = attention(
            queries[j], block, cache_keys, cache_values, cache_lens, me, j, flipped
        )
        parts = lax.all_to_all(parts.astype(jnp.float16), "seq", 0, 0).astype(jnp.float32)
        new_out, new_stat = fresh_parts[2 * j : 2 * j + 2]
        last = j == kv_local - 1
        attended = merge(
            me, parts, new_out, new_stat, before if last else [], count if last else 1
        )
        before.append(attended)
    attended = gather_at_once(before[-1])
    mixed = output_halves(place, output_weight, attended, block, tokens, heads)

    keep, send = mixed
    mixed = keep + swap(send, "head", 1)
    mask = 2
    while mask < heads:
        bit = place[0] // mask % 2
        pairs = mixed.reshape((-1, 2) + mixed.shape[1:])
        keep = lax.dynamic_index_in_dim(pairs, bit, 1, False)
        send = lax.dynamic_index_in_dim(pairs, 1 - bit, 1, False) * MIXED_SCALE
        received = swap(send.astype(jnp.float16), "head", mask).astype(jnp.float32)
        mixed = keep + received * (1.0 / MIXED_SCALE)
        mask *= 2
    return mixed[0].astype(jnp.bfloat16)


def solution(mesh):
    placed = (
        P(None, "seq"),
        P("seq", "head"),
        P("seq", "head"),
        P("seq", "head"),
        P("head", "seq"),
        P("seq", "head"),
        P("seq", "head"),
        P("seq"),
    )
    return jax.shard_map(
        shards, mesh=mesh, in_specs=placed, out_specs=P("head", "seq"), check_vma=False
    )
```

```python
import functools
import math

import jax
import jax.numpy as jnp
from jax import lax
from jax.experimental import pallas as pl
from jax.experimental.pallas import tpu as pltpu
from jax.sharding import PartitionSpec as P

QH = 64
KVH = 8
HD = 128

NEG_BIG = -1e30
LANES = 128
STAT_ROWS = 8
VMEM_GRANT = 51 << 20
PROJECT_GRANT = 56 << 20
SMALL_GRANT = 16 << 20
NT = (((1,), (1,)), ((), ()))

OUTPUT_SCALE = 2.0**12
MIXED_SCALE = 2.0**-3


def vmem_spec():
    return pl.BlockSpec(memory_space=pltpu.VMEM)


def smem_spec():
    return pl.BlockSpec(memory_space=pltpu.SMEM)


def hbm_spec():
    return pl.BlockSpec(memory_space=pl.ANY)


def swap(array, axis, mask):
    size = lax.axis_size(axis)
    return lax.ppermute(array, axis, [(i, i ^ mask) for i in range(size)])


def last_two(keep, received, me):
    mask = 2
    while mask < lax.axis_size("seq"):
        bit = me // mask % 2
        total = keep + received
        pairs = total.reshape((-1, 2) + total.shape[1:])
        keep = lax.dynamic_index_in_dim(pairs, bit, 1, False)
        send = lax.dynamic_index_in_dim(pairs, 1 - bit, 1, False)
        received = swap(send, "seq", mask)
        mask *= 2
    return [keep, received]


def collect_kernel(*refs):
    part_refs, (mine_ref, copies_ref) = refs[:-2], refs[-2:]
    total = None
    for ref in part_refs:
        for k in range(ref.shape[0]):
            total = ref[k] if total is None else total + ref[k]
    total = total.astype(jnp.bfloat16)
    mine_ref[0] = total
    for k in range(copies_ref.shape[0]):
        copies_ref[k] = total


def collect(parts, copies):
    shape = parts[0].shape[1:]
    return pl.pallas_call(
        collect_kernel,
        out_shape=[jax.ShapeDtypeStruct((n,) + shape, jnp.bfloat16) for n in (1, copies)],
        in_specs=[vmem_spec()] * len(parts),
        out_specs=[vmem_spec()] * 2,
        compiler_params=pltpu.CompilerParams(vmem_limit_bytes=SMALL_GRANT),
    )(*parts)


def project_kernel(me_ref, hidden_ref, *refs, extra, halved, chunk, blocks, pieces):
    weight_refs, refs = refs[: 1 + extra], refs[1 + extra :]
    outs, (q_all, *others_all, sems) = refs[: 1 + halved], refs[1 + halved :]
    tokens, depth = hidden_ref.shape
    odd = lax.rem(me_ref[0], 2) == 1
    rows = depth // pieces
    columns = q_all.shape[1]
    copies = [
        pltpu.make_async_copy(
            weight_refs[0].at[pl.ds(i * rows, rows), pl.ds(chunk * columns, columns)],
            q_all.at[pl.ds(i * rows, rows), :],
            sems.at[i],
        )
        for i in range(pieces)
    ]
    for i in range(extra):
        copies.append(
            pltpu.make_async_copy(weight_refs[1 + i], others_all[i], sems.at[pieces + i])
        )
    for copy in copies:
        copy.start()

    def deal(product, kind):
        block = blocks[kind]
        first = kind * blocks[0]
        parts = [
            product[e * block : (e + 1) * block, c * LANES : (c + 1) * LANES]
            for c in range(product.shape[1] // LANES)
            for e in range(tokens // block)
        ]
        if not halved:
            for i, part in enumerate(parts):
                outs[0][i, first : first + block, :] = part
            return
        for i, (even_part, odd_part) in enumerate(zip(parts[0::2], parts[1::2])):
            outs[0][i, first : first + block, :] = jnp.where(odd, odd_part, even_part)
            outs[1][i, first : first + block, :] = jnp.where(odd, even_part, odd_part)

    total = None
    for i in range(pieces):
        copies[i].wait()
        here = slice(i * rows, (i + 1) * rows)
        term = jnp.dot(hidden_ref[:, here], q_all[here, :], preferred_element_type=jnp.float32)
        total = term if total is None else total + term
    deal(total, 0)
    if extra:
        both = []
        for i in range(extra):
            copies[pieces + i].wait()
            both.append(
                jnp.dot(hidden_ref[...], others_all[i][...], preferred_element_type=jnp.float32)
            )
        deal(jnp.concatenate(both, axis=1), 1)


def project(me, hidden, query_weight, others, halved, chunk, columns, count):
    tokens, depth = hidden.shape
    wide = columns + sum(other.shape[1] for other in others)
    pieces = max(1, depth // 256)
    blocks = [width // LANES * tokens // count for width in (columns, wide - columns)]
    owners = count // 2 if halved else count
    shape = jax.ShapeDtypeStruct((owners, sum(blocks), LANES), jnp.float32)
    return pl.pallas_call(
        functools.partial(
            project_kernel,
            extra=len(others),
            halved=halved,
            chunk=chunk,
            blocks=blocks,
            pieces=pieces,
        ),
        out_shape=[shape] * (1 + halved),
        in_specs=[smem_spec(), vmem_spec()] + [hbm_spec()] * (1 + len(others)),
        out_specs=[vmem_spec()] * (1 + halved),
        scratch_shapes=[pltpu.VMEM((depth, columns), jnp.bfloat16)]
        + [pltpu.VMEM(other.shape, jnp.bfloat16) for other in others]
        + [pltpu.SemaphoreType.DMA((pieces + len(others),))],
        compiler_params=pltpu.CompilerParams(vmem_limit_bytes=PROJECT_GRANT),
        cost_estimate=pl.CostEstimate(
            flops=2 * tokens * depth * wide,
            bytes_accessed=2 * depth * wide,
            transcendentals=0,
        ),
    )(me, hidden, query_weight, *others)


def attention_kernel(len_ref, q_ref, k_hbm, v_hbm, o_ref, *refs, band, step, block, head, dma):
    k_ref, v_ref, sems = refs[:3]
    s_bufs, m_bufs = refs[3:5], refs[5:7]
    shift, acc, lse_all = refs[7:]
    count = q_ref.shape[0]
    rows = count * block
    bands = rows // band
    share = band // block
    scale = math.log2(math.e) / math.sqrt(HD)
    piece = math.gcd(step, 1024)
    tiles = piece // LANES
    fold = math.gcd(band, 128)
    lanes = slice(head * HD, (head + 1) * HD)

    length = len_ref[0]
    full = length // step
    rest = length - full * step

    def copy_in(source, target, which, i):
        where = pl.ds(pl.multiple_of(i * dma, dma), dma)
        return pltpu.make_async_copy(
            source.at[where, :], target.at[where, :], sems.at[which, i]
        )

    def keys_in(i):
        return copy_in(k_hbm, k_ref, 0, i)

    def values_in(i):
        return copy_in(v_hbm, v_ref, 1, i)

    needed = (length + step - 1) // step * (step // dma)

    def start_keys(i, carry):
        keys_in(i).start()
        return carry

    def start_values(i, carry):
        values_in(i).start()
        return carry

    lax.fori_loop(0, needed, start_keys, 0)
    lax.fori_loop(0, needed, start_values, 0)

    def score(r, i, first, masked):
        q = q_ref[r * share : (r + 1) * share, :block, :].reshape(band, HD)
        keys = k_ref[pl.ds(pl.multiple_of(i * step + first, piece), piece), lanes]
        s = lax.dot_general(q, keys, NT, preferred_element_type=jnp.float32)
        if masked:
            column = first + lax.broadcasted_iota(jnp.int32, (band, piece), 1)
            s = jnp.where(column < rest, s, NEG_BIG)
        s_bufs[r % 2][i, :, first : first + piece] = s
        tops = [s[:, c * LANES : (c + 1) * LANES] for c in range(tiles)]
        while len(tops) > 1:
            tops = [jnp.maximum(a, b) for a, b in zip(tops[0::2], tops[1::2])]
        m_bufs[r % 2][...] = jnp.maximum(m_bufs[r % 2][...], tops[0])

    def weigh(r, i, first):
        blocks = []
        for top in range(0, band, fold):
            here = slice(top, top + fold)
            low = shift[here, :]
            tiled = [
                s_bufs[r % 2][i, here, first + c * LANES : first + (c + 1) * LANES]
                for c in range(tiles)
            ]
            tiled = [jnp.exp2(s * scale - low).astype(jnp.bfloat16) for s in tiled]
            blocks.append(jnp.concatenate(tiled, axis=1))
        weights = jnp.concatenate(blocks, axis=0)
        values = v_ref[pl.ds(pl.multiple_of(i * step + first, piece), piece), lanes]
        wide = jnp.concatenate([values, jnp.ones((piece, LANES), jnp.bfloat16)], axis=1)
        acc[...] += jnp.dot(weights, wide, preferred_element_type=jnp.float32)

    for r in range(bands + 1):
        scores, weighs = r < bands, r > 0
        if scores:
            m_bufs[r % 2][...] = jnp.full((band, LANES), -3e38, jnp.float32)
        if weighs:
            top = jnp.max(m_bufs[(r - 1) % 2][...], axis=1, keepdims=True)
            shift[...] = jnp.broadcast_to(top * scale, (band, LANES))
            acc[...] = jnp.zeros(acc.shape, jnp.float32)

        def both(i, masked):
            for first in range(0, step, piece):
                arrived = i * (step // dma) + first // dma
                if r == 0 and first % dma == 0:
                    keys_in(arrived).wait()
                if r == 1 and first % dma == 0:
                    values_in(arrived).wait()
                if weighs:
                    weigh(r - 1, i, first)
                if scores:
                    score(r, i, first, masked)

        def body(i, carry):
            both(i, False)
            return carry

        lax.fori_loop(0, full, body, 0)

        @pl.when(rest > 0)
        def _():
            both(full, True)

        if weighs:
            totals = acc[:, LANES:]
            mean = acc[:, :LANES] / totals * OUTPUT_SCALE
            levels = shift[...] + jnp.log2(totals)
            o_ref[(r - 1) * share : r * share, :block, :] = mean.reshape(share, block, HD)
            lse_all[(r - 1) * band : r * band, :] = levels

    per = LANES // block
    for g in range(rows // LANES):
        stats = encode_levels(lse_all[g * LANES : (g + 1) * LANES, :].T[:STAT_ROWS, :])
        for e in range(per):
            o_ref[g * per + e, block:, :] = stats


def encode_levels(level):
    row = lax.broadcasted_iota(jnp.int32, level.shape, 0)
    exponent = jnp.floor(jnp.log2(jnp.maximum(jnp.abs(level), 1e-30)))
    exponent = jnp.minimum(exponent, 120.0)
    rest = level * jnp.exp2(-exponent)
    first = jnp.floor(rest * 2.0**9 + 0.5)
    rest = rest - first * 2.0**-9
    second = jnp.floor(rest * 2.0**20 + 0.5)
    third = (rest - second * 2.0**-20) * 2.0**31
    stats = jnp.where(row == 0, exponent, jnp.where(row == 1, first, second))
    return jnp.where(row >= 3, third, stats)


def attention(queries, block, keys, values, length, head):
    count = queries.shape[0]
    rows, slots = count * block, keys.shape[0]
    band = math.gcd(rows // 2, 512)
    step = math.gcd(slots, 4096)
    dma = math.gcd(step, 2048)
    steps = slots // step
    return pl.pallas_call(
        functools.partial(
            attention_kernel, band=band, step=step, block=block, head=head, dma=dma
        ),
        out_shape=jax.ShapeDtypeStruct((count, block + STAT_ROWS, HD), jnp.float32),
        in_specs=[smem_spec(), vmem_spec()] + [hbm_spec()] * 2,
        out_specs=vmem_spec(),
        scratch_shapes=[
            pltpu.VMEM(keys.shape, keys.dtype),
            pltpu.VMEM(values.shape, values.dtype),
            pltpu.SemaphoreType.DMA((2, slots // dma)),
            pltpu.VMEM((steps, band, step), jnp.float32),
            pltpu.VMEM((steps, band, step), jnp.float32),
            pltpu.VMEM((band, LANES), jnp.float32),
            pltpu.VMEM((band, LANES), jnp.float32),
            pltpu.VMEM((band, LANES), jnp.float32),
            pltpu.VMEM((band, 2 * LANES), jnp.float32),
            pltpu.VMEM((rows, LANES), jnp.float32),
        ],
        compiler_params=pltpu.CompilerParams(vmem_limit_bytes=VMEM_GRANT),
        cost_estimate=pl.CostEstimate(
            flops=8 * rows * slots * HD,
            bytes_accessed=4 * slots * HD,
            transcendentals=rows * slots,
        ),
    )(length, queries, keys, values)


def fresh_kernel(me_ref, *refs, heads, block, tokens):
    q_refs, last_ref, outs, kv_all = refs[:heads], refs[heads], refs[heads + 1 : -1], refs[-1]
    kv_block = last_ref.shape[1] - block
    for k in range(last_ref.shape[0]):
        rows = last_ref[k, block:, :].astype(jnp.float32)
        kv_all[k * kv_block : (k + 1) * kv_block, :] = rows
    half = heads * tokens
    for head in range(heads):
        q_ref, (out_ref, stat_ref) = q_refs[head], outs[2 * head : 2 * head + 2]
        first = head * tokens
        keys = kv_all[first : first + tokens, :].astype(jnp.bfloat16)
        values = kv_all[half + first : half + first + tokens, :].astype(jnp.bfloat16)
        s = lax.dot_general(q_ref[0, :block, :], keys, NT, preferred_element_type=jnp.float32)
        s = s * (math.log2(math.e) / math.sqrt(HD))
        token = lax.rem(me_ref[0] * block, tokens) + lax.broadcasted_iota(jnp.int32, s.shape, 0)
        visible = lax.broadcasted_iota(jnp.int32, s.shape, 1) <= token
        s = jnp.where(visible, s, NEG_BIG)
        top = jnp.max(s, axis=1, keepdims=True)
        weights = jnp.where(visible, jnp.exp2(s - top), 0.0).astype(jnp.bfloat16)
        total = jnp.sum(weights.astype(jnp.float32), axis=1, keepdims=True)
        out_ref[...] = jnp.dot(weights, values, preferred_element_type=jnp.float32)
        lane = lax.broadcasted_iota(jnp.int32, stat_ref.shape, 1)
        stat_ref[...] = jnp.where(lane < LANES // 2, top, total)


def fresh(me, mine, last, block, tokens):
    heads = len(mine)
    kv_rows = last.shape[0] * (last.shape[1] - block)
    return pl.pallas_call(
        functools.partial(fresh_kernel, heads=heads, block=block, tokens=tokens),
        out_shape=[jax.ShapeDtypeStruct((block, HD), jnp.float32)] * (2 * heads),
        in_specs=[smem_spec()] + [vmem_spec()] * (heads + 1),
        out_specs=[vmem_spec()] * (2 * heads),
        scratch_shapes=[pltpu.VMEM((kv_rows, HD), jnp.float32)],
        compiler_params=pltpu.CompilerParams(vmem_limit_bytes=SMALL_GRANT),
    )(me, *mine, last)


def merge_kernel(me_ref, part_ref, out_ref, stat_ref, *refs):
    copies_ref, turned = refs[-2:]
    count = part_ref.shape[0]
    block = out_ref.shape[0]
    new_top = stat_ref[:, 0:1]
    new_total = stat_ref[:, LANES // 2 : LANES // 2 + 1]

    place = lax.rem(me_ref[0], LANES // block)
    pieces = part_ref[:, block : block + 4, :]
    level = pieces[:, 1, :] * 2.0**-9 + pieces[:, 2, :] * 2.0**-20 + pieces[:, 3, :] * 2.0**-31
    turned[...] = (level * jnp.exp2(pieces[:, 0, :])).T
    levels = turned[pl.ds(pl.multiple_of(place * block, block), block), :]
    joint = jnp.maximum(new_top, jnp.max(levels, axis=1, keepdims=True))
    factors = jnp.exp2(levels - joint)
    new_scale = jnp.exp2(new_top - joint)
    whole_out = out_ref[...] * new_scale
    whole_total = new_total * new_scale + jnp.sum(factors, axis=1, keepdims=True)
    scaled = factors * (1.0 / OUTPUT_SCALE)
    for k in range(count):
        whole_out = whole_out + part_ref[k, :block, :] * scaled[:, k : k + 1]
    attended = (whole_out / whole_total).astype(jnp.bfloat16)
    for k in range(copies_ref.shape[0]):
        for i, ref in enumerate(refs[:-2]):
            copies_ref[k, i * block : (i + 1) * block, :] = ref[0]
        copies_ref[k, (len(refs) - 2) * block :, :] = attended


def merge(me, parts, new_out, new_stat, before, copies):
    block = new_out.shape[0]
    shape = (copies, (len(before) + 1) * block, HD)
    return pl.pallas_call(
        merge_kernel,
        out_shape=jax.ShapeDtypeStruct(shape, jnp.bfloat16),
        in_specs=[smem_spec()] + [vmem_spec()] * (3 + len(before)),
        out_specs=vmem_spec(),
        scratch_shapes=[pltpu.VMEM((LANES, parts.shape[0]), jnp.float32)],
        compiler_params=pltpu.CompilerParams(vmem_limit_bytes=SMALL_GRANT),
    )(me, parts, new_out, new_stat, *before)


def output_kernel(place_ref, w_ref, a_ref, keep_ref, send_ref, total, *, block):
    count, rows = a_ref.shape[:2]
    tokens = total.shape[0]
    per = tokens // block
    groups = count // per
    product = None
    for j in range(rows // block):
        here = slice(j * block, (j + 1) * block)
        pieces = [
            a_ref[g * per : (g + 1) * per, here, :].reshape(tokens, HD) for g in range(groups)
        ]
        term = jnp.dot(
            jnp.concatenate(pieces, axis=1),
            w_ref[j * groups * HD : (j + 1) * groups * HD, :],
            preferred_element_type=jnp.float32,
        )
        product = term if product is None else product + term
    total[...] = product
    share = keep_ref.shape[1]
    odd = lax.rem(place_ref[0], 2)
    for i in range(keep_ref.shape[0]):
        for ref, parity in ((keep_ref, odd), (send_ref, 1 - odd)):
            start = pl.multiple_of((2 * i + parity) * share, share)
            ref[i] = total[pl.ds(start, share), :]


def bring_kernel(w_hbm, after_ref, w_ref, sem):
    copy = pltpu.make_async_copy(w_hbm, w_ref, sem)
    copy.start()
    copy.wait()


def bring(weight, after):
    return pl.pallas_call(
        bring_kernel,
        out_shape=jax.ShapeDtypeStruct(weight.shape, weight.dtype),
        in_specs=[hbm_spec()] * 2,
        out_specs=vmem_spec(),
        scratch_shapes=[pltpu.SemaphoreType.DMA],
        compiler_params=pltpu.CompilerParams(vmem_limit_bytes=SMALL_GRANT),
    )(weight, after)


def output_halves(place, weight, attended, block, tokens, heads):
    depth, width = weight.shape
    shape = jax.ShapeDtypeStruct((heads // 2, tokens // heads, width), jnp.float32)
    return pl.pallas_call(
        functools.partial(output_kernel, block=block),
        out_shape=[shape] * 2,
        in_specs=[smem_spec()] + [vmem_spec()] * 2,
        out_specs=[vmem_spec()] * 2,
        scratch_shapes=[pltpu.VMEM((tokens, width), jnp.float32)],
        compiler_params=pltpu.CompilerParams(vmem_limit_bytes=SMALL_GRANT),
        cost_estimate=pl.CostEstimate(
            flops=2 * tokens * depth * width,
            bytes_accessed=2 * depth * width,
            transcendentals=0,
        ),
    )(place, weight, attended)


def shards(
    hidden,
    query_weight,
    key_weight,
    value_weight,
    output_weight,
    cache_keys,
    cache_values,
    cache_lens,
):
    tokens = hidden.shape[0]
    count = lax.axis_size("seq")
    heads = lax.axis_size("head")
    kv_local = cache_keys.shape[1] // HD
    columns = (QH // KVH) * HD
    block = (QH // KVH) * tokens // count
    me = lax.axis_index("seq").reshape(1)
    place = lax.axis_index("head").reshape(1)

    partials = []
    for j in range(kv_local):
        last = j == kv_local - 1
        others = [key_weight, value_weight] if last else []
        partials.append(
            project(me, hidden, query_weight, others, int(last), j, columns, count)
        )
    mine, queries = [], []
    for j in range(kv_local):
        if j == kv_local - 1:
            keep, send = partials[j]
            parts = last_two(keep, swap(send, "seq", 1), me[0])
        else:
            parts = [lax.all_to_all(partials[j][0], "seq", 0, 0)]
        rows, copies = collect(parts, count)
        mine.append(rows)
        queries.append(lax.all_to_all(copies, "seq", 0, 0))

    fresh_parts = fresh(me, mine, queries[-1], block, tokens)
    before = []
    for j in range(kv_local):
        parts = attention(queries[j], block, cache_keys, cache_values, cache_lens, j)
        parts = lax.all_to_all(parts.astype(jnp.float16), "seq", 0, 0).astype(jnp.float32)
        new_out, new_stat = fresh_parts[2 * j : 2 * j + 2]
        last = j == kv_local - 1
        attended = merge(
            me, parts, new_out, new_stat, before if last else [], count if last else 1
        )
        before.append(attended)
    attended = lax.all_to_all(before[-1], "seq", 0, 0)
    weight = bring(output_weight, before[-1])
    mixed = output_halves(place, weight, attended, block, tokens, heads)

    keep, send = mixed
    mixed = keep + swap(send, "head", 1)
    mask = 2
    while mask < heads:
        bit = place[0] // mask % 2
        pairs = mixed.reshape((-1, 2) + mixed.shape[1:])
        keep = lax.dynamic_index_in_dim(pairs, bit, 1, False)
        send = lax.dynamic_index_in_dim(pairs, 1 - bit, 1, False) * MIXED_SCALE
        received = swap(send.astype(jnp.float16), "head", mask).astype(jnp.float32)
        mixed = keep + received * (1.0 / MIXED_SCALE)
        mask *= 2
    return mixed[0].astype(jnp.bfloat16)


def solution(mesh):
    placed = (
        P(None, "seq"),
        P("seq", "head"),
        P("seq", "head"),
        P("seq", "head"),
        P("head", "seq"),
        P("seq", "head"),
        P("seq", "head"),
        P("seq"),
    )
    return jax.shard_map(
        shards, mesh=mesh, in_specs=placed, out_specs=P("head", "seq"), check_vma=False
    )
```

```python
import functools
import math

import jax
import jax.numpy as jnp
from jax import lax
from jax.experimental import pallas as pl
from jax.experimental.pallas import tpu as pltpu
from jax.sharding import PartitionSpec as P

QH = 64
KVH = 8
HD = 128

NEG_BIG = -1e30
LANES = 128
STAT_ROWS = 8
VMEM_GRANT = 51 << 20
PROJECT_GRANT = 56 << 20
SMALL_GRANT = 16 << 20
NT = (((1,), (1,)), ((), ()))

OUTPUT_SCALE = 2.0**12
MIXED_SCALE = 2.0**-3


def vmem_spec():
    return pl.BlockSpec(memory_space=pltpu.VMEM)


def smem_spec():
    return pl.BlockSpec(memory_space=pltpu.SMEM)


def hbm_spec():
    return pl.BlockSpec(memory_space=pl.ANY)


def swap(array, axis, mask):
    size = lax.axis_size(axis)
    return lax.ppermute(array, axis, [(i, i ^ mask) for i in range(size)])


def last_two(keep, received, me):
    mask = 2
    while mask < lax.axis_size("seq"):
        bit = me // mask % 2
        total = keep + received
        pairs = total.reshape((-1, 2) + total.shape[1:])
        keep = lax.dynamic_index_in_dim(pairs, bit, 1, False)
        send = lax.dynamic_index_in_dim(pairs, 1 - bit, 1, False)
        received = swap(send, "seq", mask)
        mask *= 2
    return [keep, received]


def collect_kernel(*refs):
    part_refs, (mine_ref, copies_ref) = refs[:-2], refs[-2:]
    total = None
    for ref in part_refs:
        for k in range(ref.shape[0]):
            total = ref[k] if total is None else total + ref[k]
    total = total.astype(jnp.bfloat16)
    mine_ref[0] = total
    for k in range(copies_ref.shape[0]):
        copies_ref[k] = total


def collect(parts, copies):
    shape = parts[0].shape[1:]
    return pl.pallas_call(
        collect_kernel,
        out_shape=[jax.ShapeDtypeStruct((n,) + shape, jnp.bfloat16) for n in (1, copies)],
        in_specs=[vmem_spec()] * len(parts),
        out_specs=[vmem_spec()] * 2,
        compiler_params=pltpu.CompilerParams(vmem_limit_bytes=SMALL_GRANT),
    )(*parts)


def doubling_masks(size):
    masks = []
    while size > 2:
        size //= 2
        masks.append(size)
    return masks


def gather_doubling(block):
    for mask in doubling_masks(lax.axis_size("seq")):
        block = jnp.concatenate([block, swap(block, "seq", mask)])
    return [block, swap(block, "seq", 1)]


def doubling_offsets(size):
    offsets = [0]
    for mask in doubling_masks(size):
        offsets = offsets + [offset ^ mask for offset in offsets]
    return offsets + [offset ^ 1 for offset in offsets]


def gather_at_once(copies):
    return lax.all_to_all(copies, "seq", 0, 0)


def project_kernel(me_ref, hidden_ref, *refs, extra, carried, chunk, blocks, pieces):
    weight_refs, refs = refs[: 1 + extra], refs[1 + extra + carried :]
    refs = refs[:2] + refs[2 + carried :]
    keep_ref, send_ref, q_all, *others_all, sems = refs
    tokens, depth = hidden_ref.shape
    odd = lax.rem(me_ref[0], 2) == 1
    rows = depth // pieces
    columns = q_all.shape[1]
    copies = [
        pltpu.make_async_copy(
            weight_refs[0].at[pl.ds(i * rows, rows), pl.ds(chunk * columns, columns)],
            q_all.at[pl.ds(i * rows, rows), :],
            sems.at[i],
        )
        for i in range(pieces)
    ]
    for i in range(extra):
        copies.append(
            pltpu.make_async_copy(weight_refs[1 + i], others_all[i], sems.at[pieces + i])
        )
    for copy in copies:
        copy.start()

    def deal(product, kind):
        block = blocks[kind]
        first = kind * blocks[0]
        parts = [
            product[e * block : (e + 1) * block, c * LANES : (c + 1) * LANES]
            for c in range(product.shape[1] // LANES)
            for e in range(tokens // block)
        ]
        for i, (even_part, odd_part) in enumerate(zip(parts[0::2], parts[1::2])):
            keep_ref[i, first : first + block, :] = jnp.where(odd, odd_part, even_part)
            send_ref[i, first : first + block, :] = jnp.where(odd, even_part, odd_part)

    total = None
    for i in range(pieces):
        copies[i].wait()
        here = slice(i * rows, (i + 1) * rows)
        term = jnp.dot(hidden_ref[:, here], q_all[here, :], preferred_element_type=jnp.float32)
        total = term if total is None else total + term
    deal(total, 0)
    if extra:
        both = []
        for i in range(extra):
            copies[pieces + i].wait()
            both.append(
                jnp.dot(hidden_ref[...], others_all[i][...], preferred_element_type=jnp.float32)
            )
        deal(jnp.concatenate(both, axis=1), 1)


def project(me, hidden, query_weight, others, carried, chunk, columns, count):
    tokens, depth = hidden.shape
    wide = columns + sum(other.shape[1] for other in others)
    pieces = max(1, depth // 256)
    blocks = [width // LANES * tokens // count for width in (columns, wide - columns)]
    shape = jax.ShapeDtypeStruct((count // 2, sum(blocks), LANES), jnp.float32)
    return pl.pallas_call(
        functools.partial(
            project_kernel,
            extra=len(others),
            carried=len(carried),
            chunk=chunk,
            blocks=blocks,
            pieces=pieces,
        ),
        out_shape=[shape] * 2 + [jax.ShapeDtypeStruct(one.shape, one.dtype) for one in carried],
        in_specs=[smem_spec(), vmem_spec()] + [hbm_spec()] * (1 + len(others) + len(carried)),
        out_specs=[vmem_spec()] * 2 + [hbm_spec()] * len(carried),
        input_output_aliases={3 + len(others) + i: 2 + i for i in range(len(carried))},
        scratch_shapes=[pltpu.VMEM((depth, columns), jnp.bfloat16)]
        + [pltpu.VMEM(other.shape, jnp.bfloat16) for other in others]
        + [pltpu.SemaphoreType.DMA((pieces + len(others),))],
        compiler_params=pltpu.CompilerParams(vmem_limit_bytes=PROJECT_GRANT),
        cost_estimate=pl.CostEstimate(
            flops=2 * tokens * depth * wide,
            bytes_accessed=2 * depth * wide,
            transcendentals=0,
        ),
    )(me, hidden, query_weight, *others, *carried)


def attention_kernel(len_ref, me_ref, *refs, sources, band, step, dma, block, head):
    q_refs, refs = refs[:sources], refs[sources:]
    k_hbm, v_hbm, o_ref, k_ref, v_ref, sems = refs[:6]
    s_bufs, m_bufs = refs[6:8], refs[8:10]
    shift, acc, lse_all = refs[10:]
    half = q_refs[0].shape[0]
    rows = sources * half * block
    bands = rows // band
    share = band // block
    scale = math.log2(math.e) / math.sqrt(HD)
    piece = math.gcd(step, 1024)
    tiles = piece // LANES
    fold = math.gcd(band, 128)
    lanes = slice(head * HD, (head + 1) * HD)
    offsets = doubling_offsets(sources * half)

    def owner_of(k):
        return k if sources == 1 else me_ref[0] ^ offsets[k]

    length = len_ref[0]
    full = length // step
    rest = length - full * step

    def copy_in(source, target, which, i):
        where = pl.ds(pl.multiple_of(i * dma, dma), dma)
        return pltpu.make_async_copy(
            source.at[where, :], target.at[where, :], sems.at[which, i]
        )

    def keys_in(i):
        return copy_in(k_hbm, k_ref, 0, i)

    def values_in(i):
        return copy_in(v_hbm, v_ref, 1, i)

    needed = (length + step - 1) // step * (step // dma)

    def start_keys(i, carry):
        keys_in(i).start()
        return carry

    def start_values(i, carry):
        values_in(i).start()
        return carry

    lax.fori_loop(0, needed, start_keys, 0)
    lax.fori_loop(0, needed, start_values, 0)

    def score(r, i, first, masked):
        source = q_refs[r * share // half]
        at = r * share % half
        q = source[at : at + share, :block, :].reshape(band, HD)
        keys = k_ref[pl.ds(pl.multiple_of(i * step + first, piece), piece), lanes]
        s = lax.dot_general(q, keys, NT, preferred_element_type=jnp.float32)
        if masked:
            column = first + lax.broadcasted_iota(jnp.int32, (band, piece), 1)
            s = jnp.where(column < rest, s, NEG_BIG)
        s_bufs[r % 2][i, :, first : first + piece] = s
        tops = [s[:, c * LANES : (c + 1) * LANES] for c in range(tiles)]
        while len(tops) > 1:
            tops = [jnp.maximum(a, b) for a, b in zip(tops[0::2], tops[1::2])]
        m_bufs[r % 2][...] = jnp.maximum(m_bufs[r % 2][...], tops[0])

    def weigh(r, i, first):
        blocks = []
        for top in range(0, band, fold):
            here = slice(top, top + fold)
            low = shift[here, :]
            tiled = [
                s_bufs[r % 2][i, here, first + c * LANES : first + (c + 1) * LANES]
                for c in range(tiles)
            ]
            tiled = [jnp.exp2(s * scale - low).astype(jnp.bfloat16) for s in tiled]
            blocks.append(jnp.concatenate(tiled, axis=1))
        weights = jnp.concatenate(blocks, axis=0)
        values = v_ref[pl.ds(pl.multiple_of(i * step + first, piece), piece), lanes]
        wide = jnp.concatenate([values, jnp.ones((piece, LANES), jnp.bfloat16)], axis=1)
        acc[...] += jnp.dot(weights, wide, preferred_element_type=jnp.float32)

    for r in range(bands + 1):
        scores, weighs = r < bands, r > 0
        if scores:
            m_bufs[r % 2][...] = jnp.full((band, LANES), -3e38, jnp.float32)
        if weighs:
            top = jnp.max(m_bufs[(r - 1) % 2][...], axis=1, keepdims=True)
            shift[...] = jnp.broadcast_to(top * scale, (band, LANES))
            acc[...] = jnp.zeros(acc.shape, jnp.float32)

        def both(i, masked):
            for first in range(0, step, piece):
                arrived = i * (step // dma) + first // dma
                if r == 0 and first % dma == 0:
                    keys_in(arrived).wait()
                if r == 1 and first % dma == 0:
                    values_in(arrived).wait()
                if weighs:
                    weigh(r - 1, i, first)
                if scores:
                    score(r, i, first, masked)

        def body(i, carry):
            both(i, False)
            return carry

        lax.fori_loop(0, full, body, 0)

        @pl.when(rest > 0)
        def _():
            both(full, True)

        if weighs:
            totals = acc[:, LANES:]
            mean = acc[:, :LANES] / totals * OUTPUT_SCALE
            levels = shift[...] + jnp.log2(totals)
            for e in range(share):
                k = (r - 1) * share + e
                owner = owner_of(k)
                here = slice(e * block, (e + 1) * block)
                o_ref[owner, :block, :] = mean[here, :]
                lse_all[pl.ds(pl.multiple_of(owner * block, block), block), :] = levels[here, :]

    per = LANES // block
    for g in range(rows // LANES):
        stats = encode_levels(lse_all[g * LANES : (g + 1) * LANES, :].T[:STAT_ROWS, :])
        for e in range(per):
            o_ref[g * per + e, block:, :] = stats


def encode_levels(level):
    row = lax.broadcasted_iota(jnp.int32, level.shape, 0)
    exponent = jnp.floor(jnp.log2(jnp.maximum(jnp.abs(level), 1e-30)))
    exponent = jnp.minimum(exponent, 120.0)
    rest = level * jnp.exp2(-exponent)
    first = jnp.floor(rest * 2.0**9 + 0.5)
    rest = rest - first * 2.0**-9
    second = jnp.floor(rest * 2.0**20 + 0.5)
    third = (rest - second * 2.0**-20) * 2.0**31
    stats = jnp.where(row == 0, exponent, jnp.where(row == 1, first, second))
    return jnp.where(row >= 3, third, stats)


def attention(queries, block, keys, values, length, me, head, most_rows, most_slots):
    sources = len(queries)
    count = sources * queries[0].shape[0]
    rows, slots = count * block, keys.shape[0]
    band = math.gcd(rows // 2, most_rows)
    step = math.gcd(slots, most_slots)
    dma = math.gcd(step, 2048)
    steps = slots // step
    return pl.pallas_call(
        functools.partial(
            attention_kernel,
            sources=sources,
            band=band,
            step=step,
            dma=dma,
            block=block,
            head=head,
        ),
        out_shape=jax.ShapeDtypeStruct((count, block + STAT_ROWS, HD), jnp.float32),
        in_specs=[smem_spec()] * 2 + [vmem_spec()] * sources + [hbm_spec()] * 2,
        out_specs=vmem_spec(),
        scratch_shapes=[
            pltpu.VMEM(keys.shape, keys.dtype),
            pltpu.VMEM(values.shape, values.dtype),
            pltpu.SemaphoreType.DMA((2, slots // dma)),
            pltpu.VMEM((steps, band, step), jnp.float32),
            pltpu.VMEM((steps, band, step), jnp.float32),
            pltpu.VMEM((band, LANES), jnp.float32),
            pltpu.VMEM((band, LANES), jnp.float32),
            pltpu.VMEM((band, LANES), jnp.float32),
            pltpu.VMEM((band, 2 * LANES), jnp.float32),
            pltpu.VMEM((rows, LANES), jnp.float32),
        ],
        compiler_params=pltpu.CompilerParams(vmem_limit_bytes=VMEM_GRANT),
        cost_estimate=pl.CostEstimate(
            flops=8 * rows * slots * HD,
            bytes_accessed=4 * slots * HD,
            transcendentals=rows * slots,
        ),
    )(length, me, *queries, keys, values)


def fresh_kernel(me_ref, *refs, heads, block, tokens):
    q_refs, last_ref, outs, kv_all = refs[:heads], refs[heads], refs[heads + 1 : -1], refs[-1]
    kv_block = last_ref.shape[1] - block
    for k in range(last_ref.shape[0]):
        rows = last_ref[k, block:, :].astype(jnp.float32)
        kv_all[k * kv_block : (k + 1) * kv_block, :] = rows
    half = heads * tokens
    for head in range(heads):
        q_ref, (out_ref, stat_ref) = q_refs[head], outs[2 * head : 2 * head + 2]
        first = head * tokens
        keys = kv_all[first : first + tokens, :].astype(jnp.bfloat16)
        values = kv_all[half + first : half + first + tokens, :].astype(jnp.bfloat16)
        s = lax.dot_general(q_ref[0, :block, :], keys, NT, preferred_element_type=jnp.float32)
        s = s * (math.log2(math.e) / math.sqrt(HD))
        token = lax.rem(me_ref[0] * block, tokens) + lax.broadcasted_iota(jnp.int32, s.shape, 0)
        visible = lax.broadcasted_iota(jnp.int32, s.shape, 1) <= token
        s = jnp.where(visible, s, NEG_BIG)
        top = jnp.max(s, axis=1, keepdims=True)
        weights = jnp.where(visible, jnp.exp2(s - top), 0.0).astype(jnp.bfloat16)
        total = jnp.sum(weights.astype(jnp.float32), axis=1, keepdims=True)
        out_ref[...] = jnp.dot(weights, values, preferred_element_type=jnp.float32)
        lane = lax.broadcasted_iota(jnp.int32, stat_ref.shape, 1)
        stat_ref[...] = jnp.where(lane < LANES // 2, top, total)


def fresh(me, mine, last, block, tokens):
    heads = len(mine)
    kv_rows = last.shape[0] * (last.shape[1] - block)
    return pl.pallas_call(
        functools.partial(fresh_kernel, heads=heads, block=block, tokens=tokens),
        out_shape=[jax.ShapeDtypeStruct((block, HD), jnp.float32)] * (2 * heads),
        in_specs=[smem_spec()] + [vmem_spec()] * (heads + 1),
        out_specs=[vmem_spec()] * (2 * heads),
        scratch_shapes=[pltpu.VMEM((kv_rows, HD), jnp.float32)],
        compiler_params=pltpu.CompilerParams(vmem_limit_bytes=SMALL_GRANT),
    )(me, *mine, last)


def merge_kernel(me_ref, part_ref, out_ref, stat_ref, *refs):
    copies_ref, turned = refs[-2:]
    count = part_ref.shape[0]
    block = out_ref.shape[0]
    new_top = stat_ref[:, 0:1]
    new_total = stat_ref[:, LANES // 2 : LANES // 2 + 1]

    place = lax.rem(me_ref[0], LANES // block)
    pieces = part_ref[:, block : block + 4, :]
    level = pieces[:, 1, :] * 2.0**-9 + pieces[:, 2, :] * 2.0**-20 + pieces[:, 3, :] * 2.0**-31
    turned[...] = (level * jnp.exp2(pieces[:, 0, :])).T
    levels = turned[pl.ds(pl.multiple_of(place * block, block), block), :]
    joint = jnp.maximum(new_top, jnp.max(levels, axis=1, keepdims=True))
    factors = jnp.exp2(levels - joint)
    new_scale = jnp.exp2(new_top - joint)
    whole_out = out_ref[...] * new_scale
    whole_total = new_total * new_scale + jnp.sum(factors, axis=1, keepdims=True)
    scaled = factors * (1.0 / OUTPUT_SCALE)
    for k in range(count):
        whole_out = whole_out + part_ref[k, :block, :] * scaled[:, k : k + 1]
    attended = (whole_out / whole_total).astype(jnp.bfloat16)
    for k in range(copies_ref.shape[0]):
        for i, ref in enumerate(refs[:-2]):
            copies_ref[k, i * block : (i + 1) * block, :] = ref[0]
        copies_ref[k, (len(refs) - 2) * block :, :] = attended


def merge(me, parts, new_out, new_stat, before, copies):
    block = new_out.shape[0]
    shape = (copies, (len(before) + 1) * block, HD)
    return pl.pallas_call(
        merge_kernel,
        out_shape=jax.ShapeDtypeStruct(shape, jnp.bfloat16),
        in_specs=[smem_spec()] + [vmem_spec()] * (3 + len(before)),
        out_specs=vmem_spec(),
        scratch_shapes=[pltpu.VMEM((LANES, parts.shape[0]), jnp.float32)],
        compiler_params=pltpu.CompilerParams(vmem_limit_bytes=SMALL_GRANT),
    )(me, parts, new_out, new_stat, *before)


def output_kernel(place_ref, w_ref, a_ref, keep_ref, send_ref, total, *, block):
    count, rows = a_ref.shape[:2]
    tokens = total.shape[0]
    per = tokens // block
    groups = count // per
    product = None
    for j in range(rows // block):
        here = slice(j * block, (j + 1) * block)
        pieces = [
            a_ref[g * per : (g + 1) * per, here, :].reshape(tokens, HD) for g in range(groups)
        ]
        term = jnp.dot(
            jnp.concatenate(pieces, axis=1),
            w_ref[j * groups * HD : (j + 1) * groups * HD, :],
            preferred_element_type=jnp.float32,
        )
        product = term if product is None else product + term
    total[...] = product
    share = keep_ref.shape[1]
    odd = lax.rem(place_ref[0], 2)
    for i in range(keep_ref.shape[0]):
        for ref, parity in ((keep_ref, odd), (send_ref, 1 - odd)):
            start = pl.multiple_of((2 * i + parity) * share, share)
            ref[i] = total[pl.ds(start, share), :]


def output_halves(place, weight, attended, block, tokens, heads):
    depth, width = weight.shape
    shape = jax.ShapeDtypeStruct((heads // 2, tokens // heads, width), jnp.float32)
    return pl.pallas_call(
        functools.partial(output_kernel, block=block),
        out_shape=[shape] * 2,
        in_specs=[smem_spec()] + [vmem_spec()] * 2,
        out_specs=[vmem_spec()] * 2,
        scratch_shapes=[pltpu.VMEM((tokens, width), jnp.float32)],
        compiler_params=pltpu.CompilerParams(vmem_limit_bytes=SMALL_GRANT),
        cost_estimate=pl.CostEstimate(
            flops=2 * tokens * depth * width,
            bytes_accessed=2 * depth * width,
            transcendentals=0,
        ),
    )(place, weight, attended)


def shards(
    hidden,
    query_weight,
    key_weight,
    value_weight,
    output_weight,
    cache_keys,
    cache_values,
    cache_lens,
):
    tokens = hidden.shape[0]
    count = lax.axis_size("seq")
    heads = lax.axis_size("head")
    kv_local = cache_keys.shape[1] // HD
    columns = (QH // KVH) * HD
    block = (QH // KVH) * tokens // count
    me = lax.axis_index("seq").reshape(1)
    place = lax.axis_index("head").reshape(1)

    kept, received = [], []
    for j in range(kv_local):
        others = [key_weight, value_weight] if j == kv_local - 1 else []
        keep, send, *kept = project(
            me, hidden, query_weight, others, kept, j, columns, count
        )
        kept.append(keep)
        received.append(swap(send, "seq", 1))
    mine, queries = [], []
    for j in range(kv_local):
        parts = last_two(kept[j], received[j], me[0])
        if j == kv_local - 1:
            rows, copies = collect(parts, count)
            mine.append(rows)
            queries.append([gather_at_once(copies)])
        else:
            mine.append((parts[0] + parts[1]).astype(jnp.bfloat16))
            queries.append(gather_doubling(mine[j]))

    fresh_parts = fresh(me, mine, queries[-1][0], block, tokens)
    before = []
    for j in range(kv_local):
        shape = (256, 8192) if j == kv_local - 1 else (512, 4096)
        parts = attention(
            queries[j], block, cache_keys, cache_values, cache_lens, me, j, *shape
        )
        parts = lax.all_to_all(parts.astype(jnp.float16), "seq", 0, 0).astype(jnp.float32)
        new_out, new_stat = fresh_parts[2 * j : 2 * j + 2]
        last = j == kv_local - 1
        attended = merge(
            me, parts, new_out, new_stat, before if last else [], count if last else 1
        )
        before.append(attended)
    attended = gather_at_once(before[-1])
    mixed = output_halves(place, output_weight, attended, block, tokens, heads)

    keep, send = mixed
    mixed = keep + swap(send, "head", 1)
    mask = 2
    while mask < heads:
        bit = place[0] // mask % 2
        pairs = mixed.reshape((-1, 2) + mixed.shape[1:])
        keep = lax.dynamic_index_in_dim(pairs, bit, 1, False)
        send = lax.dynamic_index_in_dim(pairs, 1 - bit, 1, False) * MIXED_SCALE
        received = swap(send.astype(jnp.float16), "head", mask).astype(jnp.float32)
        mixed = keep + received * (1.0 / MIXED_SCALE)
        mask *= 2
    return mixed[0].astype(jnp.bfloat16)


def solution(mesh):
    placed = (
        P(None, "seq"),
        P("seq", "head"),
        P("seq", "head"),
        P("seq", "head"),
        P("head", "seq"),
        P("seq", "head"),
        P("seq", "head"),
        P("seq"),
    )
    return jax.shard_map(
        shards, mesh=mesh, in_specs=placed, out_specs=P("head", "seq"), check_vma=False
    )
```

```python
import functools
import math

import jax
import jax.numpy as jnp
from jax import lax
from jax.experimental import pallas as pl
from jax.experimental.pallas import tpu as pltpu
from jax.sharding import PartitionSpec as P

QH = 64
KVH = 8
HD = 128

NEG_BIG = -1e30
LANES = 128
STAT_ROWS = 8
VMEM_GRANT = 51 << 20
PROJECT_GRANT = 56 << 20
SMALL_GRANT = 16 << 20
NT = (((1,), (1,)), ((), ()))

OUTPUT_SCALE = 2.0**12
MIXED_SCALE = 2.0**-3


def vmem_spec():
    return pl.BlockSpec(memory_space=pltpu.VMEM)


def smem_spec():
    return pl.BlockSpec(memory_space=pltpu.SMEM)


def hbm_spec():
    return pl.BlockSpec(memory_space=pl.ANY)


def swap(array, axis, mask):
    size = lax.axis_size(axis)
    return lax.ppermute(array, axis, [(i, i ^ mask) for i in range(size)])


def last_two(keep, received, me):
    mask = 2
    while mask < lax.axis_size("seq"):
        bit = me // mask % 2
        total = keep + received
        pairs = total.reshape((-1, 2) + total.shape[1:])
        keep = lax.dynamic_index_in_dim(pairs, bit, 1, False)
        send = lax.dynamic_index_in_dim(pairs, 1 - bit, 1, False)
        received = swap(send, "seq", mask)
        mask *= 2
    return [keep, received]


def collect_kernel(*refs):
    part_refs, (mine_ref, copies_ref) = refs[:-2], refs[-2:]
    total = None
    for ref in part_refs:
        for k in range(ref.shape[0]):
            total = ref[k] if total is None else total + ref[k]
    total = total.astype(jnp.bfloat16)
    mine_ref[0] = total
    for k in range(copies_ref.shape[0]):
        copies_ref[k] = total


def collect(parts, copies):
    shape = parts[0].shape[1:]
    return pl.pallas_call(
        collect_kernel,
        out_shape=[jax.ShapeDtypeStruct((n,) + shape, jnp.bfloat16) for n in (1, copies)],
        in_specs=[vmem_spec()] * len(parts),
        out_specs=[vmem_spec()] * 2,
        compiler_params=pltpu.CompilerParams(vmem_limit_bytes=SMALL_GRANT),
    )(*parts)


def doubling_masks(size):
    masks = []
    while size > 2:
        size //= 2
        masks.append(size)
    return masks


def gather_doubling(block, skip=0):
    for mask in doubling_masks(lax.axis_size("seq"))[skip:]:
        block = jnp.concatenate([block, swap(block, "seq", mask)])
    return [block, swap(block, "seq", 1)]


def first_doubling(block):
    mask = doubling_masks(lax.axis_size("seq"))[0]
    return jnp.concatenate([block, swap(block, "seq", mask)])


def doubling_offsets(size):
    offsets = [0]
    for mask in doubling_masks(size):
        offsets = offsets + [offset ^ mask for offset in offsets]
    return offsets + [offset ^ 1 for offset in offsets]


def gather_at_once(copies):
    return lax.all_to_all(copies, "seq", 0, 0)


def project_kernel(me_ref, hidden_ref, *refs, extra, carried, chunk, blocks, pieces):
    weight_refs, refs = refs[: 1 + extra], refs[1 + extra + carried :]
    refs = refs[:2] + refs[2 + carried :]
    keep_ref, send_ref, q_all, *others_all, sems = refs
    tokens, depth = hidden_ref.shape
    odd = lax.rem(me_ref[0], 2) == 1
    rows = depth // pieces
    columns = q_all.shape[1]
    copies = [
        pltpu.make_async_copy(
            weight_refs[0].at[pl.ds(i * rows, rows), pl.ds(chunk * columns, columns)],
            q_all.at[pl.ds(i * rows, rows), :],
            sems.at[i],
        )
        for i in range(pieces)
    ]
    for i in range(extra):
        copies.append(
            pltpu.make_async_copy(weight_refs[1 + i], others_all[i], sems.at[pieces + i])
        )
    for copy in copies:
        copy.start()

    def deal(product, kind):
        block = blocks[kind]
        first = kind * blocks[0]
        parts = [
            product[e * block : (e + 1) * block, c * LANES : (c + 1) * LANES]
            for c in range(product.shape[1] // LANES)
            for e in range(tokens // block)
        ]
        for i, (even_part, odd_part) in enumerate(zip(parts[0::2], parts[1::2])):
            keep_ref[i, first : first + block, :] = jnp.where(odd, odd_part, even_part)
            send_ref[i, first : first + block, :] = jnp.where(odd, even_part, odd_part)

    total = None
    for i in range(pieces):
        copies[i].wait()
        here = slice(i * rows, (i + 1) * rows)
        term = jnp.dot(hidden_ref[:, here], q_all[here, :], preferred_element_type=jnp.float32)
        total = term if total is None else total + term
    deal(total, 0)
    if extra:
        both = []
        for i in range(extra):
            copies[pieces + i].wait()
            both.append(
                jnp.dot(hidden_ref[...], others_all[i][...], preferred_element_type=jnp.float32)
            )
        deal(jnp.concatenate(both, axis=1), 1)


def project(me, hidden, query_weight, others, carried, chunk, columns, count):
    tokens, depth = hidden.shape
    wide = columns + sum(other.shape[1] for other in others)
    pieces = max(1, depth // 256)
    blocks = [width // LANES * tokens // count for width in (columns, wide - columns)]
    shape = jax.ShapeDtypeStruct((count // 2, sum(blocks), LANES), jnp.float32)
    return pl.pallas_call(
        functools.partial(
            project_kernel,
            extra=len(others),
            carried=len(carried),
            chunk=chunk,
            blocks=blocks,
            pieces=pieces,
        ),
        out_shape=[shape] * 2 + [jax.ShapeDtypeStruct(one.shape, one.dtype) for one in carried],
        in_specs=[smem_spec(), vmem_spec()] + [hbm_spec()] * (1 + len(others) + len(carried)),
        out_specs=[vmem_spec()] * 2 + [hbm_spec()] * len(carried),
        input_output_aliases={3 + len(others) + i: 2 + i for i in range(len(carried))},
        scratch_shapes=[pltpu.VMEM((depth, columns), jnp.bfloat16)]
        + [pltpu.VMEM(other.shape, jnp.bfloat16) for other in others]
        + [pltpu.SemaphoreType.DMA((pieces + len(others),))],
        compiler_params=pltpu.CompilerParams(vmem_limit_bytes=PROJECT_GRANT),
        cost_estimate=pl.CostEstimate(
            flops=2 * tokens * depth * wide,
            bytes_accessed=2 * depth * wide,
            transcendentals=0,
        ),
    )(me, hidden, query_weight, *others, *carried)


def attention_kernel(len_ref, me_ref, *refs, sources, band, step, dma, block, head):
    q_refs, refs = refs[:sources], refs[sources:]
    k_hbm, v_hbm, o_ref, k_ref, v_ref, sems = refs[:6]
    s_bufs, m_bufs = refs[6:8], refs[8:10]
    shift, acc, lse_all = refs[10:]
    half = q_refs[0].shape[0]
    rows = sources * half * block
    bands = rows // band
    share = band // block
    scale = math.log2(math.e) / math.sqrt(HD)
    piece = math.gcd(step, 1024)
    tiles = piece // LANES
    fold = math.gcd(band, 128)
    lanes = slice(head * HD, (head + 1) * HD)
    offsets = doubling_offsets(sources * half)

    def owner_of(k):
        return k if sources == 1 else me_ref[0] ^ offsets[k]

    length = len_ref[0]
    full = length // step
    rest = length - full * step

    def copy_in(source, target, which, i):
        where = pl.ds(pl.multiple_of(i * dma, dma), dma)
        return pltpu.make_async_copy(
            source.at[where, :], target.at[where, :], sems.at[which, i]
        )

    def keys_in(i):
        return copy_in(k_hbm, k_ref, 0, i)

    def values_in(i):
        return copy_in(v_hbm, v_ref, 1, i)

    needed = (length + step - 1) // step * (step // dma)

    def start_keys(i, carry):
        keys_in(i).start()
        return carry

    def start_values(i, carry):
        values_in(i).start()
        return carry

    lax.fori_loop(0, needed, start_keys, 0)
    lax.fori_loop(0, needed, start_values, 0)

    def score(r, i, first, masked):
        source = q_refs[r * share // half]
        at = r * share % half
        q = source[at : at + share, :block, :].reshape(band, HD)
        keys = k_ref[pl.ds(pl.multiple_of(i * step + first, piece), piece), lanes]
        s = lax.dot_general(q, keys, NT, preferred_element_type=jnp.float32)
        if masked:
            column = first + lax.broadcasted_iota(jnp.int32, (band, piece), 1)
            s = jnp.where(column < rest, s, NEG_BIG)
        s_bufs[r % 2][i, :, first : first + piece] = s
        tops = [s[:, c * LANES : (c + 1) * LANES] for c in range(tiles)]
        while len(tops) > 1:
            tops = [jnp.maximum(a, b) for a, b in zip(tops[0::2], tops[1::2])]
        m_bufs[r % 2][...] = jnp.maximum(m_bufs[r % 2][...], tops[0])

    def weigh(r, i, first):
        blocks = []
        for top in range(0, band, fold):
            here = slice(top, top + fold)
            low = shift[here, :]
            tiled = [
                s_bufs[r % 2][i, here, first + c * LANES : first + (c + 1) * LANES]
                for c in range(tiles)
            ]
            tiled = [jnp.exp2(s * scale - low).astype(jnp.bfloat16) for s in tiled]
            blocks.append(jnp.concatenate(tiled, axis=1))
        weights = jnp.concatenate(blocks, axis=0)
        values = v_ref[pl.ds(pl.multiple_of(i * step + first, piece), piece), lanes]
        wide = jnp.concatenate([values, jnp.ones((piece, LANES), jnp.bfloat16)], axis=1)
        acc[...] += jnp.dot(weights, wide, preferred_element_type=jnp.float32)

    for r in range(bands + 1):
        scores, weighs = r < bands, r > 0
        if scores:
            m_bufs[r % 2][...] = jnp.full((band, LANES), -3e38, jnp.float32)
        if weighs:
            top = jnp.max(m_bufs[(r - 1) % 2][...], axis=1, keepdims=True)
            shift[...] = jnp.broadcast_to(top * scale, (band, LANES))
            acc[...] = jnp.zeros(acc.shape, jnp.float32)

        def both(i, masked):
            for first in range(0, step, piece):
                arrived = i * (step // dma) + first // dma
                if r == 0 and first % dma == 0:
                    keys_in(arrived).wait()
                if r == 1 and first % dma == 0:
                    values_in(arrived).wait()
                if weighs:
                    weigh(r - 1, i, first)
                if scores:
                    score(r, i, first, masked)

        def body(i, carry):
            both(i, False)
            return carry

        lax.fori_loop(0, full, body, 0)

        @pl.when(rest > 0)
        def _():
            both(full, True)

        if weighs:
            totals = acc[:, LANES:]
            mean = acc[:, :LANES] / totals * OUTPUT_SCALE
            levels = shift[...] + jnp.log2(totals)
            for e in range(share):
                k = (r - 1) * share + e
                owner = owner_of(k)
                here = slice(e * block, (e + 1) * block)
                o_ref[owner, :block, :] = mean[here, :]
                lse_all[pl.ds(pl.multiple_of(owner * block, block), block), :] = levels[here, :]

    per = LANES // block
    for g in range(rows // LANES):
        stats = encode_levels(lse_all[g * LANES : (g + 1) * LANES, :].T[:STAT_ROWS, :])
        for e in range(per):
            o_ref[g * per + e, block:, :] = stats


def encode_levels(level):
    row = lax.broadcasted_iota(jnp.int32, level.shape, 0)
    exponent = jnp.floor(jnp.log2(jnp.maximum(jnp.abs(level), 1e-30)))
    exponent = jnp.minimum(exponent, 120.0)
    rest = level * jnp.exp2(-exponent)
    first = jnp.floor(rest * 2.0**9 + 0.5)
    rest = rest - first * 2.0**-9
    second = jnp.floor(rest * 2.0**20 + 0.5)
    third = (rest - second * 2.0**-20) * 2.0**31
    stats = jnp.where(row == 0, exponent, jnp.where(row == 1, first, second))
    return jnp.where(row >= 3, third, stats)


def attention(queries, block, keys, values, length, me, head, most_rows, most_slots):
    sources = len(queries)
    count = sources * queries[0].shape[0]
    rows, slots = count * block, keys.shape[0]
    band = math.gcd(rows // 2, most_rows)
    step = math.gcd(slots, most_slots)
    dma = math.gcd(step, 2048)
    steps = slots // step
    return pl.pallas_call(
        functools.partial(
            attention_kernel,
            sources=sources,
            band=band,
            step=step,
            dma=dma,
            block=block,
            head=head,
        ),
        out_shape=jax.ShapeDtypeStruct((count, block + STAT_ROWS, HD), jnp.float32),
        in_specs=[smem_spec()] * 2 + [vmem_spec()] * sources + [hbm_spec()] * 2,
        out_specs=vmem_spec(),
        scratch_shapes=[
            pltpu.VMEM(keys.shape, keys.dtype),
            pltpu.VMEM(values.shape, values.dtype),
            pltpu.SemaphoreType.DMA((2, slots // dma)),
            pltpu.VMEM((steps, band, step), jnp.float32),
            pltpu.VMEM((steps, band, step), jnp.float32),
            pltpu.VMEM((band, LANES), jnp.float32),
            pltpu.VMEM((band, LANES), jnp.float32),
            pltpu.VMEM((band, LANES), jnp.float32),
            pltpu.VMEM((band, 2 * LANES), jnp.float32),
            pltpu.VMEM((rows, LANES), jnp.float32),
        ],
        compiler_params=pltpu.CompilerParams(vmem_limit_bytes=VMEM_GRANT),
        cost_estimate=pl.CostEstimate(
            flops=8 * rows * slots * HD,
            bytes_accessed=4 * slots * HD,
            transcendentals=rows * slots,
        ),
    )(length, me, *queries, keys, values)


def fresh_kernel(me_ref, *refs, heads, block, tokens):
    q_refs, last_ref, outs, kv_all = refs[:heads], refs[heads], refs[heads + 1 : -1], refs[-1]
    kv_block = last_ref.shape[1] - block
    for k in range(last_ref.shape[0]):
        rows = last_ref[k, block:, :].astype(jnp.float32)
        kv_all[k * kv_block : (k + 1) * kv_block, :] = rows
    half = heads * tokens
    for head in range(heads):
        q_ref, (out_ref, stat_ref) = q_refs[head], outs[2 * head : 2 * head + 2]
        first = head * tokens
        keys = kv_all[first : first + tokens, :].astype(jnp.bfloat16)
        values = kv_all[half + first : half + first + tokens, :].astype(jnp.bfloat16)
        s = lax.dot_general(q_ref[0, :block, :], keys, NT, preferred_element_type=jnp.float32)
        s = s * (math.log2(math.e) / math.sqrt(HD))
        token = lax.rem(me_ref[0] * block, tokens) + lax.broadcasted_iota(jnp.int32, s.shape, 0)
        visible = lax.broadcasted_iota(jnp.int32, s.shape, 1) <= token
        s = jnp.where(visible, s, NEG_BIG)
        top = jnp.max(s, axis=1, keepdims=True)
        weights = jnp.where(visible, jnp.exp2(s - top), 0.0).astype(jnp.bfloat16)
        total = jnp.sum(weights.astype(jnp.float32), axis=1, keepdims=True)
        out_ref[...] = jnp.dot(weights, values, preferred_element_type=jnp.float32)
        lane = lax.broadcasted_iota(jnp.int32, stat_ref.shape, 1)
        stat_ref[...] = jnp.where(lane < LANES // 2, top, total)


def fresh(me, mine, last, block, tokens):
    heads = len(mine)
    kv_rows = last.shape[0] * (last.shape[1] - block)
    return pl.pallas_call(
        functools.partial(fresh_kernel, heads=heads, block=block, tokens=tokens),
        out_shape=[jax.ShapeDtypeStruct((block, HD), jnp.float32)] * (2 * heads),
        in_specs=[smem_spec()] + [vmem_spec()] * (heads + 1),
        out_specs=[vmem_spec()] * (2 * heads),
        scratch_shapes=[pltpu.VMEM((kv_rows, HD), jnp.float32)],
        compiler_params=pltpu.CompilerParams(vmem_limit_bytes=SMALL_GRANT),
    )(me, *mine, last)


def merge_kernel(me_ref, part_ref, out_ref, stat_ref, *refs):
    copies_ref, turned = refs[-2:]
    count = part_ref.shape[0]
    block = out_ref.shape[0]
    new_top = stat_ref[:, 0:1]
    new_total = stat_ref[:, LANES // 2 : LANES // 2 + 1]

    place = lax.rem(me_ref[0], LANES // block)
    pieces = part_ref[:, block : block + 4, :]
    level = pieces[:, 1, :] * 2.0**-9 + pieces[:, 2, :] * 2.0**-20 + pieces[:, 3, :] * 2.0**-31
    turned[...] = (level * jnp.exp2(pieces[:, 0, :])).T
    levels = turned[pl.ds(pl.multiple_of(place * block, block), block), :]
    joint = jnp.maximum(new_top, jnp.max(levels, axis=1, keepdims=True))
    factors = jnp.exp2(levels - joint)
    new_scale = jnp.exp2(new_top - joint)
    whole_out = out_ref[...] * new_scale
    whole_total = new_total * new_scale + jnp.sum(factors, axis=1, keepdims=True)
    scaled = factors * (1.0 / OUTPUT_SCALE)
    for k in range(count):
        whole_out = whole_out + part_ref[k, :block, :] * scaled[:, k : k + 1]
    attended = (whole_out / whole_total).astype(jnp.bfloat16)
    for k in range(copies_ref.shape[0]):
        copies_ref[k] = attended


def merge(me, parts, new_out, new_stat, copies, after):
    return pl.pallas_call(
        merge_kernel,
        out_shape=jax.ShapeDtypeStruct((copies,) + new_out.shape, jnp.bfloat16),
        in_specs=[smem_spec()] + [vmem_spec()] * 3 + [hbm_spec()] * len(after),
        out_specs=vmem_spec(),
        scratch_shapes=[pltpu.VMEM((LANES, parts.shape[0]), jnp.float32)],
        compiler_params=pltpu.CompilerParams(vmem_limit_bytes=SMALL_GRANT),
    )(me, parts, new_out, new_stat, *after)


def output_kernel(me_ref, place_ref, w_ref, *refs, sources, tokens):
    a_refs, (keep_ref, send_ref, a_all, total) = refs[: sum(sources)], refs[sum(sources) :]
    groups = a_all.shape[0]
    product, first = None, 0
    for j, parts in enumerate(sources):
        chunk_refs, first = a_refs[first : first + parts], first + parts
        held, block = chunk_refs[0].shape[:2]
        per = tokens // block
        if parts == 1:
            pieces = [
                chunk_refs[0][g * per : (g + 1) * per].reshape(tokens, HD)
                for g in range(groups)
            ]
        else:
            for k, offset in enumerate(doubling_offsets(parts * held)):
                owner = me_ref[0] ^ offset
                start = pl.multiple_of(lax.rem(owner, per) * block, block)
                a_all[owner // per, pl.ds(start, block), :] = chunk_refs[k // held][k % held]
            pieces = [a_all[g] for g in range(groups)]
        term = jnp.dot(
            jnp.concatenate(pieces, axis=1),
            w_ref[j * groups * HD : (j + 1) * groups * HD, :],
            preferred_element_type=jnp.float32,
        )
        product = term if product is None else product + term
    total[...] = product
    share = keep_ref.shape[1]
    odd = lax.rem(place_ref[0], 2)
    for i in range(keep_ref.shape[0]):
        for ref, parity in ((keep_ref, odd), (send_ref, 1 - odd)):
            start = pl.multiple_of((2 * i + parity) * share, share)
            ref[i] = total[pl.ds(start, share), :]


def output_halves(me, place, weight, attended, tokens, heads):
    depth, width = weight.shape
    sources = tuple(len(rows) for rows in attended)
    shape = jax.ShapeDtypeStruct((heads // 2, tokens // heads, width), jnp.float32)
    return pl.pallas_call(
        functools.partial(output_kernel, sources=sources, tokens=tokens),
        out_shape=[shape] * 2,
        in_specs=[smem_spec()] * 2 + [vmem_spec()] * (1 + sum(sources)),
        out_specs=[vmem_spec()] * 2,
        scratch_shapes=[
            pltpu.VMEM((depth // HD // len(sources), tokens, HD), jnp.bfloat16),
            pltpu.VMEM((tokens, width), jnp.float32),
        ],
        compiler_params=pltpu.CompilerParams(vmem_limit_bytes=SMALL_GRANT),
        cost_estimate=pl.CostEstimate(
            flops=2 * tokens * depth * width,
            bytes_accessed=2 * depth * width,
            transcendentals=0,
        ),
    )(me, place, weight, *[part for rows in attended for part in rows])


def shards(
    hidden,
    query_weight,
    key_weight,
    value_weight,
    output_weight,
    cache_keys,
    cache_values,
    cache_lens,
):
    tokens = hidden.shape[0]
    count = lax.axis_size("seq")
    heads = lax.axis_size("head")
    kv_local = cache_keys.shape[1] // HD
    columns = (QH // KVH) * HD
    block = (QH // KVH) * tokens // count
    me = lax.axis_index("seq").reshape(1)
    place = lax.axis_index("head").reshape(1)

    kept, received = [], []
    for j in range(kv_local):
        others = [key_weight, value_weight] if j == kv_local - 1 else []
        keep, send, *kept = project(
            me, hidden, query_weight, others, kept, j, columns, count
        )
        kept.append(keep)
        received.append(swap(send, "seq", 1))
    mine, queries = [], []
    for j in range(kv_local):
        parts = last_two(kept[j], received[j], me[0])
        if j == kv_local - 1:
            rows, copies = collect(parts, count)
            mine.append(rows)
            queries.append([gather_at_once(copies)])
        else:
            mine.append((parts[0] + parts[1]).astype(jnp.bfloat16))
            queries.append(gather_doubling(mine[j]))

    fresh_parts = fresh(me, mine, queries[-1][0], block, tokens)
    attended, doubled = [], []
    for j in range(kv_local):
        parts = attention(
            queries[j], block, cache_keys, cache_values, cache_lens, me, j, 512, 4096
        )
        parts = lax.all_to_all(parts.astype(jnp.float16), "seq", 0, 0).astype(jnp.float32)
        new_out, new_stat = fresh_parts[2 * j : 2 * j + 2]
        if j == kv_local - 1:
            copies = merge(me, parts, new_out, new_stat, count, doubled)
            attended.append([gather_at_once(copies)])
        else:
            doubled = [first_doubling(merge(me, parts, new_out, new_stat, 1, []))]
            attended.append(gather_doubling(doubled[0], 1))
    mixed = output_halves(me, place, output_weight, attended, tokens, heads)

    keep, send = mixed
    mixed = keep + swap(send, "head", 1)
    mask = 2
    while mask < heads:
        bit = place[0] // mask % 2
        pairs = mixed.reshape((-1, 2) + mixed.shape[1:])
        keep = lax.dynamic_index_in_dim(pairs, bit, 1, False)
        send = lax.dynamic_index_in_dim(pairs, 1 - bit, 1, False) * MIXED_SCALE
        received = swap(send.astype(jnp.float16), "head", mask).astype(jnp.float32)
        mixed = keep + received * (1.0 / MIXED_SCALE)
        mask *= 2
    return mixed[0].astype(jnp.bfloat16)


def solution(mesh):
    placed = (
        P(None, "seq"),
        P("seq", "head"),
        P("seq", "head"),
        P("seq", "head"),
        P("head", "seq"),
        P("seq", "head"),
        P("seq", "head"),
        P("seq"),
    )
    return jax.shard_map(
        shards, mesh=mesh, in_specs=placed, out_specs=P("head", "seq"), check_vma=False
    )
```

```python
import functools
import math

import jax
import jax.numpy as jnp
from jax import lax
from jax.experimental import pallas as pl
from jax.experimental.pallas import tpu as pltpu
from jax.sharding import PartitionSpec as P

QH = 64
KVH = 8
HD = 128

NEG_BIG = -1e30
LANES = 128
STAT_ROWS = 8
VMEM_GRANT = 51 << 20
PROJECT_GRANT = 56 << 20
SMALL_GRANT = 16 << 20
NT = (((1,), (1,)), ((), ()))

OUTPUT_SCALE = 2.0**12
MIXED_SCALE = 2.0**-3


def vmem_spec():
    return pl.BlockSpec(memory_space=pltpu.VMEM)


def smem_spec():
    return pl.BlockSpec(memory_space=pltpu.SMEM)


def hbm_spec():
    return pl.BlockSpec(memory_space=pl.ANY)


def swap(array, axis, mask):
    size = lax.axis_size(axis)
    return lax.ppermute(array, axis, [(i, i ^ mask) for i in range(size)])


def last_two(keep, received, me):
    mask = 2
    while mask < lax.axis_size("seq"):
        bit = me // mask % 2
        total = keep + received
        pairs = total.reshape((-1, 2) + total.shape[1:])
        keep = lax.dynamic_index_in_dim(pairs, bit, 1, False)
        send = lax.dynamic_index_in_dim(pairs, 1 - bit, 1, False)
        received = swap(send, "seq", mask)
        mask *= 2
    return [keep, received]


def collect_kernel(*refs):
    part_refs, (mine_ref, copies_ref) = refs[:-2], refs[-2:]
    total = None
    for ref in part_refs:
        for k in range(ref.shape[0]):
            total = ref[k] if total is None else total + ref[k]
    total = total.astype(jnp.bfloat16)
    mine_ref[0] = total
    for k in range(copies_ref.shape[0]):
        copies_ref[k] = total


def collect(parts, copies):
    shape = parts[0].shape[1:]
    return pl.pallas_call(
        collect_kernel,
        out_shape=[jax.ShapeDtypeStruct((n,) + shape, jnp.bfloat16) for n in (1, copies)],
        in_specs=[vmem_spec()] * len(parts),
        out_specs=[vmem_spec()] * 2,
        compiler_params=pltpu.CompilerParams(vmem_limit_bytes=SMALL_GRANT),
    )(*parts)


def doubling_masks(size):
    masks = []
    while size > 2:
        size //= 2
        masks.append(size)
    return masks


def gather_doubling(block):
    for mask in doubling_masks(lax.axis_size("seq")):
        block = jnp.concatenate([block, swap(block, "seq", mask)])
    return [block, swap(block, "seq", 1)]


def doubling_offsets(size):
    offsets = [0]
    for mask in doubling_masks(size):
        offsets = offsets + [offset ^ mask for offset in offsets]
    return offsets + [offset ^ 1 for offset in offsets]


def gather_at_once(copies):
    return lax.all_to_all(copies, "seq", 0, 0)


def project_kernel(me_ref, hidden_ref, *refs, extra, carried, chunk, blocks, pieces):
    weight_refs, refs = refs[: 1 + extra], refs[1 + extra + carried :]
    refs = refs[:2] + refs[2 + carried :]
    keep_ref, send_ref, q_all, *others_all, sems = refs
    tokens, depth = hidden_ref.shape
    odd = lax.rem(me_ref[0], 2) == 1
    rows = depth // pieces
    columns = q_all.shape[1]
    copies = [
        pltpu.make_async_copy(
            weight_refs[0].at[pl.ds(i * rows, rows), pl.ds(chunk * columns, columns)],
            q_all.at[pl.ds(i * rows, rows), :],
            sems.at[i],
        )
        for i in range(pieces)
    ]
    for i in range(extra):
        copies.append(
            pltpu.make_async_copy(weight_refs[1 + i], others_all[i], sems.at[pieces + i])
        )
    for copy in copies:
        copy.start()

    def deal(product, kind):
        block = blocks[kind]
        first = kind * blocks[0]
        parts = [
            product[e * block : (e + 1) * block, c * LANES : (c + 1) * LANES]
            for c in range(product.shape[1] // LANES)
            for e in range(tokens // block)
        ]
        for i, (even_part, odd_part) in enumerate(zip(parts[0::2], parts[1::2])):
            keep_ref[i, first : first + block, :] = jnp.where(odd, odd_part, even_part)
            send_ref[i, first : first + block, :] = jnp.where(odd, even_part, odd_part)

    total = None
    for i in range(pieces):
        copies[i].wait()
        here = slice(i * rows, (i + 1) * rows)
        term = jnp.dot(hidden_ref[:, here], q_all[here, :], preferred_element_type=jnp.float32)
        total = term if total is None else total + term
    deal(total, 0)
    if extra:
        both = []
        for i in range(extra):
            copies[pieces + i].wait()
            both.append(
                jnp.dot(hidden_ref[...], others_all[i][...], preferred_element_type=jnp.float32)
            )
        deal(jnp.concatenate(both, axis=1), 1)


def project(me, hidden, query_weight, others, carried, chunk, columns, count):
    tokens, depth = hidden.shape
    wide = columns + sum(other.shape[1] for other in others)
    pieces = max(1, depth // 256)
    blocks = [width // LANES * tokens // count for width in (columns, wide - columns)]
    shape = jax.ShapeDtypeStruct((count // 2, sum(blocks), LANES), jnp.float32)
    return pl.pallas_call(
        functools.partial(
            project_kernel,
            extra=len(others),
            carried=len(carried),
            chunk=chunk,
            blocks=blocks,
            pieces=pieces,
        ),
        out_shape=[shape] * 2 + [jax.ShapeDtypeStruct(one.shape, one.dtype) for one in carried],
        in_specs=[smem_spec(), vmem_spec()] + [hbm_spec()] * (1 + len(others) + len(carried)),
        out_specs=[vmem_spec()] * 2 + [hbm_spec()] * len(carried),
        input_output_aliases={3 + len(others) + i: 2 + i for i in range(len(carried))},
        scratch_shapes=[pltpu.VMEM((depth, columns), jnp.bfloat16)]
        + [pltpu.VMEM(other.shape, jnp.bfloat16) for other in others]
        + [pltpu.SemaphoreType.DMA((pieces + len(others),))],
        compiler_params=pltpu.CompilerParams(vmem_limit_bytes=PROJECT_GRANT),
        cost_estimate=pl.CostEstimate(
            flops=2 * tokens * depth * wide,
            bytes_accessed=2 * depth * wide,
            transcendentals=0,
        ),
    )(me, hidden, query_weight, *others, *carried)


def attention_kernel(len_ref, me_ref, *refs, sources, band, step, dma, block, head):
    q_refs, refs = refs[:sources], refs[sources:]
    k_hbm, v_hbm, o_ref, k_ref, v_ref, sems = refs[:6]
    s_bufs, m_bufs = refs[6:8], refs[8:10]
    shift, acc, lse_all = refs[10:]
    half = q_refs[0].shape[0]
    rows = sources * half * block
    bands = rows // band
    share = band // block
    scale = math.log2(math.e) / math.sqrt(HD)
    piece = math.gcd(step, 1024)
    tiles = piece // LANES
    fold = math.gcd(band, 128)
    lanes = slice(head * HD, (head + 1) * HD)
    offsets = doubling_offsets(sources * half)

    def owner_of(k):
        return k if sources == 1 else me_ref[0] ^ offsets[k]

    length = len_ref[0]
    full = length // step
    rest = length - full * step

    def copy_in(source, target, which, i):
        where = pl.ds(pl.multiple_of(i * dma, dma), dma)
        return pltpu.make_async_copy(
            source.at[where, :], target.at[where, :], sems.at[which, i]
        )

    def keys_in(i):
        return copy_in(k_hbm, k_ref, 0, i)

    def values_in(i):
        return copy_in(v_hbm, v_ref, 1, i)

    needed = (length + step - 1) // step * (step // dma)

    def start_keys(i, carry):
        keys_in(i).start()
        return carry

    def start_values(i, carry):
        values_in(i).start()
        return carry

    lax.fori_loop(0, needed, start_keys, 0)
    lax.fori_loop(0, needed, start_values, 0)

    def score(r, i, first, masked):
        source = q_refs[r * share // half]
        at = r * share % half
        q = source[at : at + share, :block, :].reshape(band, HD)
        keys = k_ref[pl.ds(pl.multiple_of(i * step + first, piece), piece), lanes]
        s = lax.dot_general(q, keys, NT, preferred_element_type=jnp.float32)
        if masked:
            column = first + lax.broadcasted_iota(jnp.int32, (band, piece), 1)
            s = jnp.where(column < rest, s, NEG_BIG)
        s_bufs[r % 2][i, :, first : first + piece] = s
        tops = [s[:, c * LANES : (c + 1) * LANES] for c in range(tiles)]
        while len(tops) > 1:
            tops = [jnp.maximum(a, b) for a, b in zip(tops[0::2], tops[1::2])]
        m_bufs[r % 2][...] = jnp.maximum(m_bufs[r % 2][...], tops[0])

    def weigh(r, i, first):
        blocks = []
        for top in range(0, band, fold):
            here = slice(top, top + fold)
            low = shift[here, :]
            tiled = [
                s_bufs[r % 2][i, here, first + c * LANES : first + (c + 1) * LANES]
                for c in range(tiles)
            ]
            tiled = [jnp.exp2(s * scale - low).astype(jnp.bfloat16) for s in tiled]
            blocks.append(jnp.concatenate(tiled, axis=1))
        weights = jnp.concatenate(blocks, axis=0)
        values = v_ref[pl.ds(pl.multiple_of(i * step + first, piece), piece), lanes]
        wide = jnp.concatenate([values, jnp.ones((piece, LANES), jnp.bfloat16)], axis=1)
        acc[...] += jnp.dot(weights, wide, preferred_element_type=jnp.float32)

    for r in range(bands + 1):
        scores, weighs = r < bands, r > 0
        if scores:
            m_bufs[r % 2][...] = jnp.full((band, LANES), -3e38, jnp.float32)
        if weighs:
            top = jnp.max(m_bufs[(r - 1) % 2][...], axis=1, keepdims=True)
            shift[...] = jnp.broadcast_to(top * scale, (band, LANES))
            acc[...] = jnp.zeros(acc.shape, jnp.float32)

        def both(i, masked):
            for first in range(0, step, piece):
                arrived = i * (step // dma) + first // dma
                if r == 0 and first % dma == 0:
                    keys_in(arrived).wait()
                if r == 1 and first % dma == 0:
                    values_in(arrived).wait()
                if weighs:
                    weigh(r - 1, i, first)
                if scores:
                    score(r, i, first, masked)

        def body(i, carry):
            both(i, False)
            return carry

        lax.fori_loop(0, full, body, 0)

        @pl.when(rest > 0)
        def _():
            both(full, True)

        if weighs:
            totals = acc[:, LANES:]
            mean = acc[:, :LANES] / totals * OUTPUT_SCALE
            levels = shift[...] + jnp.log2(totals)
            for e in range(share):
                k = (r - 1) * share + e
                owner = owner_of(k)
                here = slice(e * block, (e + 1) * block)
                o_ref[owner, :block, :] = mean[here, :]
                lse_all[pl.ds(pl.multiple_of(owner * block, block), block), :] = levels[here, :]

    per = LANES // block
    for g in range(rows // LANES):
        stats = encode_levels(lse_all[g * LANES : (g + 1) * LANES, :].T[:STAT_ROWS, :])
        for e in range(per):
            o_ref[g * per + e, block:, :] = stats


def encode_levels(level):
    row = lax.broadcasted_iota(jnp.int32, level.shape, 0)
    exponent = jnp.floor(jnp.log2(jnp.maximum(jnp.abs(level), 1e-30)))
    exponent = jnp.minimum(exponent, 120.0)
    rest = level * jnp.exp2(-exponent)
    first = jnp.floor(rest * 2.0**9 + 0.5)
    rest = rest - first * 2.0**-9
    second = jnp.floor(rest * 2.0**20 + 0.5)
    third = (rest - second * 2.0**-20) * 2.0**31
    stats = jnp.where(row == 0, exponent, jnp.where(row == 1, first, second))
    return jnp.where(row >= 3, third, stats)


def attention(queries, block, keys, values, length, me, head, most_rows, most_slots):
    sources = len(queries)
    count = sources * queries[0].shape[0]
    rows, slots = count * block, keys.shape[0]
    band = math.gcd(rows // 2, most_rows)
    step = math.gcd(slots, most_slots)
    dma = math.gcd(step, 2048)
    steps = slots // step
    return pl.pallas_call(
        functools.partial(
            attention_kernel,
            sources=sources,
            band=band,
            step=step,
            dma=dma,
            block=block,
            head=head,
        ),
        out_shape=jax.ShapeDtypeStruct((count, block + STAT_ROWS, HD), jnp.float32),
        in_specs=[smem_spec()] * 2 + [vmem_spec()] * sources + [hbm_spec()] * 2,
        out_specs=vmem_spec(),
        scratch_shapes=[
            pltpu.VMEM(keys.shape, keys.dtype),
            pltpu.VMEM(values.shape, values.dtype),
            pltpu.SemaphoreType.DMA((2, slots // dma)),
            pltpu.VMEM((steps, band, step), jnp.float32),
            pltpu.VMEM((steps, band, step), jnp.float32),
            pltpu.VMEM((band, LANES), jnp.float32),
            pltpu.VMEM((band, LANES), jnp.float32),
            pltpu.VMEM((band, LANES), jnp.float32),
            pltpu.VMEM((band, 2 * LANES), jnp.float32),
            pltpu.VMEM((rows, LANES), jnp.float32),
        ],
        compiler_params=pltpu.CompilerParams(vmem_limit_bytes=VMEM_GRANT),
        cost_estimate=pl.CostEstimate(
            flops=8 * rows * slots * HD,
            bytes_accessed=4 * slots * HD,
            transcendentals=rows * slots,
        ),
    )(length, me, *queries, keys, values)


def fresh_kernel(me_ref, *refs, heads, block, tokens):
    q_refs, last_ref, outs, kv_all = refs[:heads], refs[heads], refs[heads + 1 : -1], refs[-1]
    kv_block = last_ref.shape[1] - block
    for k in range(last_ref.shape[0]):
        rows = last_ref[k, block:, :].astype(jnp.float32)
        kv_all[k * kv_block : (k + 1) * kv_block, :] = rows
    half = heads * tokens
    for head in range(heads):
        q_ref, (out_ref, stat_ref) = q_refs[head], outs[2 * head : 2 * head + 2]
        first = head * tokens
        keys = kv_all[first : first + tokens, :].astype(jnp.bfloat16)
        values = kv_all[half + first : half + first + tokens, :].astype(jnp.bfloat16)
        s = lax.dot_general(q_ref[0, :block, :], keys, NT, preferred_element_type=jnp.float32)
        s = s * (math.log2(math.e) / math.sqrt(HD))
        token = lax.rem(me_ref[0] * block, tokens) + lax.broadcasted_iota(jnp.int32, s.shape, 0)
        visible = lax.broadcasted_iota(jnp.int32, s.shape, 1) <= token
        s = jnp.where(visible, s, NEG_BIG)
        top = jnp.max(s, axis=1, keepdims=True)
        weights = jnp.where(visible, jnp.exp2(s - top), 0.0).astype(jnp.bfloat16)
        total = jnp.sum(weights.astype(jnp.float32), axis=1, keepdims=True)
        out_ref[...] = jnp.dot(weights, values, preferred_element_type=jnp.float32)
        lane = lax.broadcasted_iota(jnp.int32, stat_ref.shape, 1)
        stat_ref[...] = jnp.where(lane < LANES // 2, top, total)


def fresh(me, mine, last, block, tokens):
    heads = len(mine)
    kv_rows = last.shape[0] * (last.shape[1] - block)
    return pl.pallas_call(
        functools.partial(fresh_kernel, heads=heads, block=block, tokens=tokens),
        out_shape=[jax.ShapeDtypeStruct((block, HD), jnp.float32)] * (2 * heads),
        in_specs=[smem_spec()] + [vmem_spec()] * (heads + 1),
        out_specs=[vmem_spec()] * (2 * heads),
        scratch_shapes=[pltpu.VMEM((kv_rows, HD), jnp.float32)],
        compiler_params=pltpu.CompilerParams(vmem_limit_bytes=SMALL_GRANT),
    )(me, *mine, last)


def merge_kernel(me_ref, part_ref, out_ref, stat_ref, *refs):
    copies_ref, turned = refs[-2:]
    count = part_ref.shape[0]
    block = out_ref.shape[0]
    new_top = stat_ref[:, 0:1]
    new_total = stat_ref[:, LANES // 2 : LANES // 2 + 1]

    place = lax.rem(me_ref[0], LANES // block)
    pieces = part_ref[:, block : block + 4, :]
    level = pieces[:, 1, :] * 2.0**-9 + pieces[:, 2, :] * 2.0**-20 + pieces[:, 3, :] * 2.0**-31
    turned[...] = (level * jnp.exp2(pieces[:, 0, :])).T
    levels = turned[pl.ds(pl.multiple_of(place * block, block), block), :]
    joint = jnp.maximum(new_top, jnp.max(levels, axis=1, keepdims=True))
    factors = jnp.exp2(levels - joint)
    new_scale = jnp.exp2(new_top - joint)
    whole_out = out_ref[...] * new_scale
    whole_total = new_total * new_scale + jnp.sum(factors, axis=1, keepdims=True)
    scaled = factors * (1.0 / OUTPUT_SCALE)
    for k in range(count):
        whole_out = whole_out + part_ref[k, :block, :] * scaled[:, k : k + 1]
    attended = (whole_out / whole_total).astype(jnp.bfloat16)
    for k in range(copies_ref.shape[0]):
        for i, ref in enumerate(refs[:-2]):
            copies_ref[k, i * block : (i + 1) * block, :] = ref[0]
        copies_ref[k, (len(refs) - 2) * block :, :] = attended


def merge(me, parts, new_out, new_stat, before, copies):
    block = new_out.shape[0]
    shape = (copies, (len(before) + 1) * block, HD)
    return pl.pallas_call(
        merge_kernel,
        out_shape=jax.ShapeDtypeStruct(shape, jnp.bfloat16),
        in_specs=[smem_spec()] + [vmem_spec()] * (3 + len(before)),
        out_specs=vmem_spec(),
        scratch_shapes=[pltpu.VMEM((LANES, parts.shape[0]), jnp.float32)],
        compiler_params=pltpu.CompilerParams(vmem_limit_bytes=SMALL_GRANT),
    )(me, parts, new_out, new_stat, *before)


def output_kernel(place_ref, w_ref, a_ref, keep_ref, send_ref, total, *, block):
    count, rows = a_ref.shape[:2]
    tokens = total.shape[0]
    per = tokens // block
    groups = count // per
    product = None
    for j in range(rows // block):
        here = slice(j * block, (j + 1) * block)
        pieces = [
            a_ref[g * per : (g + 1) * per, here, :].reshape(tokens, HD) for g in range(groups)
        ]
        term = jnp.dot(
            jnp.concatenate(pieces, axis=1),
            w_ref[j * groups * HD : (j + 1) * groups * HD, :],
            preferred_element_type=jnp.float32,
        )
        product = term if product is None else product + term
    total[...] = product
    share = keep_ref.shape[1]
    odd = lax.rem(place_ref[0], 2)
    for i in range(keep_ref.shape[0]):
        for ref, parity in ((keep_ref, odd), (send_ref, 1 - odd)):
            start = pl.multiple_of((2 * i + parity) * share, share)
            ref[i] = total[pl.ds(start, share), :]


def output_halves(place, weight, attended, block, tokens, heads):
    depth, width = weight.shape
    shape = jax.ShapeDtypeStruct((heads // 2, tokens // heads, width), jnp.float32)
    return pl.pallas_call(
        functools.partial(output_kernel, block=block),
        out_shape=[shape] * 2,
        in_specs=[smem_spec()] + [vmem_spec()] * 2,
        out_specs=[vmem_spec()] * 2,
        scratch_shapes=[pltpu.VMEM((tokens, width), jnp.float32)],
        compiler_params=pltpu.CompilerParams(vmem_limit_bytes=SMALL_GRANT),
        cost_estimate=pl.CostEstimate(
            flops=2 * tokens * depth * width,
            bytes_accessed=2 * depth * width,
            transcendentals=0,
        ),
    )(place, weight, attended)


def shards(
    hidden,
    query_weight,
    key_weight,
    value_weight,
    output_weight,
    cache_keys,
    cache_values,
    cache_lens,
):
    tokens = hidden.shape[0]
    count = lax.axis_size("seq")
    heads = lax.axis_size("head")
    kv_local = cache_keys.shape[1] // HD
    columns = (QH // KVH) * HD
    block = (QH // KVH) * tokens // count
    me = lax.axis_index("seq").reshape(1)
    place = lax.axis_index("head").reshape(1)

    kept, received = [], []
    for j in range(kv_local):
        others = [key_weight, value_weight] if j == kv_local - 1 else []
        keep, send, *kept = project(
            me, hidden, query_weight, others, kept, j, columns, count
        )
        kept.append(keep)
        received.append(swap(send, "seq", 1))
    mine, queries = [], []
    for j in range(kv_local):
        parts = last_two(kept[j], received[j], me[0])
        if j == kv_local - 1:
            rows, copies = collect(parts, count)
            mine.append(rows)
            queries.append([gather_at_once(copies)])
        else:
            mine.append((parts[0] + parts[1]).astype(jnp.bfloat16))
            queries.append(gather_doubling(mine[j]))

    fresh_parts = fresh(me, mine, queries[-1][0], block, tokens)
    before = []
    for j in range(kv_local):
        parts = attention(
            queries[j], block, cache_keys, cache_values, cache_lens, me, j, 512, 4096
        )
        parts = lax.all_to_all(parts.astype(jnp.float16), "seq", 0, 0).astype(jnp.float32)
        new_out, new_stat = fresh_parts[2 * j : 2 * j + 2]
        last = j == kv_local - 1
        attended = merge(
            me, parts, new_out, new_stat, before if last else [], count if last else 1
        )
        before.append(attended)
    attended = gather_at_once(before[-1])
    mixed = output_halves(place, output_weight, attended, block, tokens, heads)

    keep, send = mixed
    mixed = keep + swap(send, "head", 1)
    mask = 2
    while mask < heads:
        bit = place[0] // mask % 2
        pairs = mixed.reshape((-1, 2) + mixed.shape[1:])
        keep = lax.dynamic_index_in_dim(pairs, bit, 1, False)
        send = lax.dynamic_index_in_dim(pairs, 1 - bit, 1, False) * MIXED_SCALE
        received = swap(send.astype(jnp.float16), "head", mask).astype(jnp.float32)
        mixed = keep + received * (1.0 / MIXED_SCALE)
        mask *= 2
    return mixed[0].astype(jnp.bfloat16)


def solution(mesh):
    placed = (
        P(None, "seq"),
        P("seq", "head"),
        P("seq", "head"),
        P("seq", "head"),
        P("head", "seq"),
        P("seq", "head"),
        P("seq", "head"),
        P("seq"),
    )
    return jax.shard_map(
        shards, mesh=mesh, in_specs=placed, out_specs=P("head", "seq"), check_vma=False
    )
```

```python
import functools
import math

import jax
import jax.numpy as jnp
from jax import lax
from jax.experimental import pallas as pl
from jax.experimental.pallas import tpu as pltpu
from jax.sharding import PartitionSpec as P

QH = 64
KVH = 8
HD = 128

NEG_BIG = -1e30
LANES = 128
STAT_ROWS = 8
VMEM_GRANT = 51 << 20
PROJECT_GRANT = 56 << 20
SMALL_GRANT = 16 << 20
NT = (((1,), (1,)), ((), ()))

OUTPUT_SCALE = 2.0**12
MIXED_SCALE = 2.0**-3


def vmem_spec():
    return pl.BlockSpec(memory_space=pltpu.VMEM)


def smem_spec():
    return pl.BlockSpec(memory_space=pltpu.SMEM)


def hbm_spec():
    return pl.BlockSpec(memory_space=pl.ANY)


def swap(array, axis, mask):
    size = lax.axis_size(axis)
    return lax.ppermute(array, axis, [(i, i ^ mask) for i in range(size)])


def owners_sum(keep, received, me):
    total = keep + received
    mask = 2
    while mask < lax.axis_size("seq"):
        bit = me // mask % 2
        pairs = total.reshape((-1, 2) + total.shape[1:])
        keep = lax.dynamic_index_in_dim(pairs, bit, 1, False)
        send = lax.dynamic_index_in_dim(pairs, 1 - bit, 1, False)
        total = keep + swap(send, "seq", mask)
        mask *= 2
    return total.astype(jnp.bfloat16)


def doubling_masks(size):
    masks = []
    while size > 2:
        size //= 2
        masks.append(size)
    return masks


def gather_doubling(block):
    for mask in doubling_masks(lax.axis_size("seq")):
        block = jnp.concatenate([block, swap(block, "seq", mask)])
    return [block, swap(block, "seq", 1)]


def doubling_offsets(size):
    offsets = [0]
    for mask in doubling_masks(size):
        offsets = offsets + [offset ^ mask for offset in offsets]
    return offsets + [offset ^ 1 for offset in offsets]


def gather_at_once(copies):
    return lax.all_to_all(copies, "seq", 0, 0)


def project_kernel(me_ref, hidden_ref, *refs, extra, carried, chunk, blocks, pieces):
    weight_refs, refs = refs[: 1 + extra], refs[1 + extra + carried :]
    refs = refs[:2] + refs[2 + carried :]
    keep_ref, send_ref, q_all, *others_all, sems = refs
    tokens, depth = hidden_ref.shape
    odd = lax.rem(me_ref[0], 2) == 1
    rows = depth // pieces
    columns = q_all.shape[1]
    copies = [
        pltpu.make_async_copy(
            weight_refs[0].at[pl.ds(i * rows, rows), pl.ds(chunk * columns, columns)],
            q_all.at[pl.ds(i * rows, rows), :],
            sems.at[i],
        )
        for i in range(pieces)
    ]
    for i in range(extra):
        copies.append(
            pltpu.make_async_copy(weight_refs[1 + i], others_all[i], sems.at[pieces + i])
        )
    for copy in copies:
        copy.start()

    def deal(product, kind):
        block = blocks[kind]
        first = kind * blocks[0]
        parts = [
            product[e * block : (e + 1) * block, c * LANES : (c + 1) * LANES]
            for c in range(product.shape[1] // LANES)
            for e in range(tokens // block)
        ]
        for i, (even_part, odd_part) in enumerate(zip(parts[0::2], parts[1::2])):
            keep_ref[i, first : first + block, :] = jnp.where(odd, odd_part, even_part)
            send_ref[i, first : first + block, :] = jnp.where(odd, even_part, odd_part)

    total = None
    for i in range(pieces):
        copies[i].wait()
        here = slice(i * rows, (i + 1) * rows)
        term = jnp.dot(hidden_ref[:, here], q_all[here, :], preferred_element_type=jnp.float32)
        total = term if total is None else total + term
    deal(total, 0)
    if extra:
        both = []
        for i in range(extra):
            copies[pieces + i].wait()
            both.append(
                jnp.dot(hidden_ref[...], others_all[i][...], preferred_element_type=jnp.float32)
            )
        deal(jnp.concatenate(both, axis=1), 1)


def project(me, hidden, query_weight, others, carried, chunk, columns, count):
    tokens, depth = hidden.shape
    wide = columns + sum(other.shape[1] for other in others)
    pieces = max(1, depth // 256)
    blocks = [width // LANES * tokens // count for width in (columns, wide - columns)]
    shape = jax.ShapeDtypeStruct((count // 2, sum(blocks), LANES), jnp.float32)
    return pl.pallas_call(
        functools.partial(
            project_kernel,
            extra=len(others),
            carried=len(carried),
            chunk=chunk,
            blocks=blocks,
            pieces=pieces,
        ),
        out_shape=[shape] * 2 + [jax.ShapeDtypeStruct(one.shape, one.dtype) for one in carried],
        in_specs=[smem_spec(), vmem_spec()] + [hbm_spec()] * (1 + len(others) + len(carried)),
        out_specs=[vmem_spec()] * 2 + [hbm_spec()] * len(carried),
        input_output_aliases={3 + len(others) + i: 2 + i for i in range(len(carried))},
        scratch_shapes=[pltpu.VMEM((depth, columns), jnp.bfloat16)]
        + [pltpu.VMEM(other.shape, jnp.bfloat16) for other in others]
        + [pltpu.SemaphoreType.DMA((pieces + len(others),))],
        compiler_params=pltpu.CompilerParams(vmem_limit_bytes=PROJECT_GRANT),
        cost_estimate=pl.CostEstimate(
            flops=2 * tokens * depth * wide,
            bytes_accessed=2 * depth * wide,
            transcendentals=0,
        ),
    )(me, hidden, query_weight, *others, *carried)


def attention_kernel(len_ref, me_ref, *refs, sources, band, step, block, head):
    q_refs, refs = refs[:sources], refs[sources:]
    k_hbm, v_hbm, o_ref, k_ref, v_ref, sems = refs[:6]
    s_bufs, m_bufs = refs[6:8], refs[8:10]
    shift, acc, lse_all = refs[10:]
    half = q_refs[0].shape[0]
    rows = sources * half * block
    bands = rows // band
    share = band // block
    scale = math.log2(math.e) / math.sqrt(HD)
    piece = math.gcd(step, 1024)
    tiles = piece // LANES
    fold = math.gcd(band, 128)
    lanes = slice(head * HD, (head + 1) * HD)
    offsets = doubling_offsets(sources * half)

    def owner_of(k):
        return k if sources == 1 else me_ref[0] ^ offsets[k]

    length = len_ref[0]
    full = length // step
    rest = length - full * step

    def copy_in(source, target, which, i):
        where = pl.ds(pl.multiple_of(i * step, step), step)
        return pltpu.make_async_copy(
            source.at[where, :], target.at[where, :], sems.at[which, i]
        )

    def keys_in(i):
        return copy_in(k_hbm, k_ref, 0, i)

    def values_in(i):
        return copy_in(v_hbm, v_ref, 1, i)

    needed = (length + step - 1) // step

    def start_keys(i, carry):
        keys_in(i).start()
        return carry

    def start_values(i, carry):
        values_in(i).start()
        return carry

    lax.fori_loop(0, needed, start_keys, 0)
    lax.fori_loop(0, needed, start_values, 0)

    def score(r, i, first, masked):
        source = q_refs[r * share // half]
        at = r * share % half
        q = source[at : at + share, :block, :].reshape(band, HD)
        keys = k_ref[pl.ds(pl.multiple_of(i * step + first, piece), piece), lanes]
        s = lax.dot_general(q, keys, NT, preferred_element_type=jnp.float32)
        if masked:
            column = first + lax.broadcasted_iota(jnp.int32, (band, piece), 1)
            s = jnp.where(column < rest, s, NEG_BIG)
        s_bufs[r % 2][i, :, first : first + piece] = s
        tops = [s[:, c * LANES : (c + 1) * LANES] for c in range(tiles)]
        while len(tops) > 1:
            tops = [jnp.maximum(a, b) for a, b in zip(tops[0::2], tops[1::2])]
        m_bufs[r % 2][...] = jnp.maximum(m_bufs[r % 2][...], tops[0])

    def weigh(r, i, first):
        blocks = []
        for top in range(0, band, fold):
            here = slice(top, top + fold)
            low = shift[here, :]
            tiled = [
                s_bufs[r % 2][i, here, first + c * LANES : first + (c + 1) * LANES]
                for c in range(tiles)
            ]
            tiled = [jnp.exp2(s * scale - low).astype(jnp.bfloat16) for s in tiled]
            blocks.append(jnp.concatenate(tiled, axis=1))
        weights = jnp.concatenate(blocks, axis=0)
        values = v_ref[pl.ds(pl.multiple_of(i * step + first, piece), piece), lanes]
        wide = jnp.concatenate([values, jnp.ones((piece, LANES), jnp.bfloat16)], axis=1)
        acc[...] += jnp.dot(weights, wide, preferred_element_type=jnp.float32)

    for r in range(bands + 1):
        scores, weighs = r < bands, r > 0
        if scores:
            m_bufs[r % 2][...] = jnp.full((band, LANES), -3e38, jnp.float32)
        if weighs:
            top = jnp.max(m_bufs[(r - 1) % 2][...], axis=1, keepdims=True)
            shift[...] = jnp.broadcast_to(top * scale, (band, LANES))
            acc[...] = jnp.zeros(acc.shape, jnp.float32)

        def both(i, masked):
            if r == 0:
                keys_in(i).wait()
            if r == 1:
                values_in(i).wait()
            for first in range(0, step, piece):
                if weighs:
                    weigh(r - 1, i, first)
                if scores:
                    score(r, i, first, masked)

        def body(i, carry):
            both(i, False)
            return carry

        lax.fori_loop(0, full, body, 0)

        @pl.when(rest > 0)
        def _():
            both(full, True)

        if weighs:
            totals = acc[:, LANES:]
            mean = acc[:, :LANES] / totals * OUTPUT_SCALE
            levels = shift[...] + jnp.log2(totals)
            for e in range(share):
                k = (r - 1) * share + e
                owner = owner_of(k)
                here = slice(e * block, (e + 1) * block)
                o_ref[owner, :block, :] = mean[here, :]
                lse_all[pl.ds(pl.multiple_of(owner * block, block), block), :] = levels[here, :]

    per = LANES // block
    for g in range(rows // LANES):
        stats = encode_levels(lse_all[g * LANES : (g + 1) * LANES, :].T[:STAT_ROWS, :])
        for e in range(per):
            o_ref[g * per + e, block:, :] = stats


def encode_levels(level):
    row = lax.broadcasted_iota(jnp.int32, level.shape, 0)
    exponent = jnp.floor(jnp.log2(jnp.maximum(jnp.abs(level), 1e-30)))
    exponent = jnp.minimum(exponent, 120.0)
    rest = level * jnp.exp2(-exponent)
    first = jnp.floor(rest * 2.0**9 + 0.5)
    rest = rest - first * 2.0**-9
    second = jnp.floor(rest * 2.0**20 + 0.5)
    third = (rest - second * 2.0**-20) * 2.0**31
    stats = jnp.where(row == 0, exponent, jnp.where(row == 1, first, second))
    return jnp.where(row >= 3, third, stats)


def flipped_kernel(len_ref, me_ref, *refs, sources, band, step, block, head):
    q_refs, refs = refs[:sources], refs[sources:]
    k_hbm, v_hbm, o_ref, k_ref, v_ref, sems = refs[:6]
    s_bufs, m_bufs = refs[6:8], refs[8:10]
    shift, acc, turned = refs[10:]
    half = q_refs[0].shape[0]
    bands = sources * half * block // band
    share = band // block
    scale = math.log2(math.e) / math.sqrt(HD)
    piece = math.gcd(step, 1024)
    lanes = slice(head * HD, (head + 1) * HD)
    offsets = doubling_offsets(sources * half)

    def owner_of(k):
        return k if sources == 1 else me_ref[0] ^ offsets[k]

    length = len_ref[0]
    full = length // step
    rest = length - full * step
    needed = (length + step - 1) // step

    def copy_in(source, target, which, i):
        where = pl.ds(pl.multiple_of(i * step, step), step)
        return pltpu.make_async_copy(
            source.at[where, :], target.at[where, :], sems.at[which, i]
        )

    def keys_in(i):
        return copy_in(k_hbm, k_ref, 0, i)

    def values_in(i):
        return copy_in(v_hbm, v_ref, 1, i)

    def start_keys(i, carry):
        keys_in(i).start()
        return carry

    def start_values(i, carry):
        values_in(i).start()
        return carry

    lax.fori_loop(0, needed, start_keys, 0)
    lax.fori_loop(0, needed, start_values, 0)
    turned[HD:, :] = jnp.ones((turned.shape[0] - HD, turned.shape[1]), jnp.bfloat16)

    def score(r, i, first, masked):
        source = q_refs[r * share // half]
        at = r * share % half
        q = source[at : at + share, :block, :].reshape(band, HD)
        keys = k_ref[pl.ds(pl.multiple_of(i * step + first, piece), piece), lanes]
        s = lax.dot_general(keys, q, NT, preferred_element_type=jnp.float32)
        if masked:
            slot = first + lax.broadcasted_iota(jnp.int32, s.shape, 0)
            s = jnp.where(slot < rest, s, NEG_BIG)
        s_bufs[r % 2][i, first : first + piece, :] = s
        tops = jnp.max(s.reshape(piece // 8, 8, band), axis=0)
        m_bufs[r % 2][...] = jnp.maximum(m_bufs[r % 2][...], tops)

    def weigh(r, i, first):
        here = pl.ds(pl.multiple_of(i * step + first, piece), piece)
        if r == 0:
            turned[:HD, here] = v_ref[here, lanes].T
        s = s_bufs[r % 2][i, first : first + piece, :]
        weights = jnp.exp2(s * scale - shift[0:1, :]).astype(jnp.bfloat16)
        acc[...] += jnp.dot(turned[:, here], weights, preferred_element_type=jnp.float32)

    for r in range(bands + 1):
        scores, weighs = r < bands, r > 0
        if scores:
            m_bufs[r % 2][...] = jnp.full((8, band), -3e38, jnp.float32)
        if weighs:
            top = jnp.max(m_bufs[(r - 1) % 2][...], axis=0, keepdims=True)
            shift[...] = jnp.broadcast_to(top * scale, (8, band))
            acc[...] = jnp.zeros(acc.shape, jnp.float32)

        def both(i, masked):
            if r == 0:
                keys_in(i).wait()
            if r == 1:
                values_in(i).wait()
            for first in range(0, step, piece):
                if weighs:
                    weigh(r - 1, i, first)
                if scores:
                    score(r, i, first, masked)

        def body(i, carry):
            both(i, False)
            return carry

        lax.fori_loop(0, full, body, 0)

        @pl.when(rest > 0)
        def _():
            both(full, True)

        if weighs:
            totals = acc[HD : HD + 8, :]
            levels = encode_levels(shift[...] + jnp.log2(totals))
            for e in range(share):
                owner = owner_of((r - 1) * share + e)
                here = slice(e * block, (e + 1) * block)
                mean = acc[:HD, here] * (OUTPUT_SCALE / totals[0:1, here])
                o_ref[owner, :block, :] = mean.T
                o_ref[owner, block:, :] = levels[:, here]


def attention(queries, block, keys, values, length, me, head, flipped):
    sources = len(queries)
    count = sources * queries[0].shape[0]
    rows, slots = count * block, keys.shape[0]
    band = math.gcd(rows // 2, 512)
    step = math.gcd(slots, 2048)
    steps = slots // step
    if flipped:
        kernel = flipped_kernel
        scratch = [
            pltpu.VMEM((steps, step, band), jnp.float32),
            pltpu.VMEM((steps, step, band), jnp.float32),
            pltpu.VMEM((8, band), jnp.float32),
            pltpu.VMEM((8, band), jnp.float32),
            pltpu.VMEM((8, band), jnp.float32),
            pltpu.VMEM((HD + 16, band), jnp.float32),
            pltpu.VMEM((HD + 16, slots), jnp.bfloat16),
        ]
    else:
        kernel = attention_kernel
        scratch = [
            pltpu.VMEM((steps, band, step), jnp.float32),
            pltpu.VMEM((steps, band, step), jnp.float32),
            pltpu.VMEM((band, LANES), jnp.float32),
            pltpu.VMEM((band, LANES), jnp.float32),
            pltpu.VMEM((band, LANES), jnp.float32),
            pltpu.VMEM((band, 2 * LANES), jnp.float32),
            pltpu.VMEM((rows, LANES), jnp.float32),
        ]
    return pl.pallas_call(
        functools.partial(
            kernel, sources=sources, band=band, step=step, block=block, head=head
        ),
        out_shape=jax.ShapeDtypeStruct((count, block + STAT_ROWS, HD), jnp.float32),
        in_specs=[smem_spec()] * 2 + [vmem_spec()] * sources + [hbm_spec()] * 2,
        out_specs=vmem_spec(),
        scratch_shapes=[
            pltpu.VMEM(keys.shape, keys.dtype),
            pltpu.VMEM(values.shape, values.dtype),
            pltpu.SemaphoreType.DMA((2, steps)),
        ]
        + scratch,
        compiler_params=pltpu.CompilerParams(vmem_limit_bytes=VMEM_GRANT),
        cost_estimate=pl.CostEstimate(
            flops=8 * rows * slots * HD,
            bytes_accessed=4 * slots * HD,
            transcendentals=rows * slots,
        ),
    )(length, me, *queries, keys, values)


def fresh_kernel(me_ref, *refs, heads, block, tokens):
    q_refs, last_ref, outs, kv_all = refs[:heads], refs[heads], refs[heads + 1 : -1], refs[-1]
    kv_block = last_ref.shape[1] - block
    for k in range(last_ref.shape[0]):
        rows = last_ref[k, block:, :].astype(jnp.float32)
        kv_all[k * kv_block : (k + 1) * kv_block, :] = rows
    half = heads * tokens
    for head in range(heads):
        q_ref, (out_ref, stat_ref) = q_refs[head], outs[2 * head : 2 * head + 2]
        first = head * tokens
        keys = kv_all[first : first + tokens, :].astype(jnp.bfloat16)
        values = kv_all[half + first : half + first + tokens, :].astype(jnp.bfloat16)
        s = lax.dot_general(q_ref[0, :block, :], keys, NT, preferred_element_type=jnp.float32)
        s = s * (math.log2(math.e) / math.sqrt(HD))
        token = lax.rem(me_ref[0] * block, tokens) + lax.broadcasted_iota(jnp.int32, s.shape, 0)
        visible = lax.broadcasted_iota(jnp.int32, s.shape, 1) <= token
        s = jnp.where(visible, s, NEG_BIG)
        top = jnp.max(s, axis=1, keepdims=True)
        weights = jnp.where(visible, jnp.exp2(s - top), 0.0).astype(jnp.bfloat16)
        total = jnp.sum(weights.astype(jnp.float32), axis=1, keepdims=True)
        out_ref[...] = jnp.dot(weights, values, preferred_element_type=jnp.float32)
        lane = lax.broadcasted_iota(jnp.int32, stat_ref.shape, 1)
        stat_ref[...] = jnp.where(lane < LANES // 2, top, total)


def fresh(me, mine, last, block, tokens):
    heads = len(mine)
    kv_rows = last.shape[0] * (last.shape[1] - block)
    return pl.pallas_call(
        functools.partial(fresh_kernel, heads=heads, block=block, tokens=tokens),
        out_shape=[jax.ShapeDtypeStruct((block, HD), jnp.float32)] * (2 * heads),
        in_specs=[smem_spec()] + [vmem_spec()] * (heads + 1),
        out_specs=[vmem_spec()] * (2 * heads),
        scratch_shapes=[pltpu.VMEM((kv_rows, HD), jnp.float32)],
        compiler_params=pltpu.CompilerParams(vmem_limit_bytes=SMALL_GRANT),
    )(me, *mine, last)


def merge_kernel(me_ref, part_ref, out_ref, stat_ref, *refs):
    copies_ref, turned = refs[-2:]
    count = part_ref.shape[0]
    block = out_ref.shape[0]
    new_top = stat_ref[:, 0:1]
    new_total = stat_ref[:, LANES // 2 : LANES // 2 + 1]

    place = lax.rem(me_ref[0], LANES // block)
    pieces = part_ref[:, block : block + 4, :]
    level = pieces[:, 1, :] * 2.0**-9 + pieces[:, 2, :] * 2.0**-20 + pieces[:, 3, :] * 2.0**-31
    turned[...] = (level * jnp.exp2(pieces[:, 0, :])).T
    levels = turned[pl.ds(pl.multiple_of(place * block, block), block), :]
    joint = jnp.maximum(new_top, jnp.max(levels, axis=1, keepdims=True))
    factors = jnp.exp2(levels - joint)
    new_scale = jnp.exp2(new_top - joint)
    whole_out = out_ref[...] * new_scale
    whole_total = new_total * new_scale + jnp.sum(factors, axis=1, keepdims=True)
    scaled = factors * (1.0 / OUTPUT_SCALE)
    for k in range(count):
        whole_out = whole_out + part_ref[k, :block, :] * scaled[:, k : k + 1]
    attended = (whole_out / whole_total).astype(jnp.bfloat16)
    for k in range(copies_ref.shape[0]):
        for i, ref in enumerate(refs[:-2]):
            copies_ref[k, i * block : (i + 1) * block, :] = ref[0]
        copies_ref[k, (len(refs) - 2) * block :, :] = attended


def merge(me, parts, new_out, new_stat, before, copies):
    block = new_out.shape[0]
    shape = (copies, (len(before) + 1) * block, HD)
    return pl.pallas_call(
        merge_kernel,
        out_shape=jax.ShapeDtypeStruct(shape, jnp.bfloat16),
        in_specs=[smem_spec()] + [vmem_spec()] * (3 + len(before)),
        out_specs=vmem_spec(),
        scratch_shapes=[pltpu.VMEM((LANES, parts.shape[0]), jnp.float32)],
        compiler_params=pltpu.CompilerParams(vmem_limit_bytes=SMALL_GRANT),
    )(me, parts, new_out, new_stat, *before)


def output_kernel(place_ref, w_hbm, a_ref, keep_ref, send_ref, total, w_ref, sems, *, block):
    count, rows = a_ref.shape[:2]
    tokens = total.shape[0]
    per = tokens // block
    groups = count // per
    part = groups * HD
    copies = []
    for j in range(rows // block):
        where = pl.ds(j * part, part)
        copies.append(pltpu.make_async_copy(w_hbm.at[where, :], w_ref.at[where, :], sems.at[j]))
        copies[-1].start()
    product = None
    for j in range(rows // block):
        here = slice(j * block, (j + 1) * block)
        pieces = [
            a_ref[g * per : (g + 1) * per, here, :].reshape(tokens, HD) for g in range(groups)
        ]
        copies[j].wait()
        term = jnp.dot(
            jnp.concatenate(pieces, axis=1),
            w_ref[j * groups * HD : (j + 1) * groups * HD, :],
            preferred_element_type=jnp.float32,
        )
        product = term if product is None else product + term
    total[...] = product
    share = keep_ref.shape[1]
    odd = lax.rem(place_ref[0], 2)
    for i in range(keep_ref.shape[0]):
        for ref, parity in ((keep_ref, odd), (send_ref, 1 - odd)):
            start = pl.multiple_of((2 * i + parity) * share, share)
            ref[i] = total[pl.ds(start, share), :]


def output_halves(place, weight, attended, block, tokens, heads):
    depth, width = weight.shape
    shape = jax.ShapeDtypeStruct((heads // 2, tokens // heads, width), jnp.float32)
    return pl.pallas_call(
        functools.partial(output_kernel, block=block),
        out_shape=[shape] * 2,
        in_specs=[smem_spec(), hbm_spec(), vmem_spec()],
        out_specs=[vmem_spec()] * 2,
        scratch_shapes=[
            pltpu.VMEM((tokens, width), jnp.float32),
            pltpu.VMEM((depth, width), jnp.bfloat16),
            pltpu.SemaphoreType.DMA((attended.shape[1] // block,)),
        ],
        compiler_params=pltpu.CompilerParams(vmem_limit_bytes=VMEM_GRANT),
        cost_estimate=pl.CostEstimate(
            flops=2 * tokens * depth * width,
            bytes_accessed=2 * depth * width,
            transcendentals=0,
        ),
    )(place, weight, attended)


def shards(
    hidden,
    query_weight,
    key_weight,
    value_weight,
    output_weight,
    cache_keys,
    cache_values,
    cache_lens,
):
    tokens = hidden.shape[0]
    count = lax.axis_size("seq")
    heads = lax.axis_size("head")
    kv_local = cache_keys.shape[1] // HD
    columns = (QH // KVH) * HD
    block = (QH // KVH) * tokens // count
    me = lax.axis_index("seq").reshape(1)
    place = lax.axis_index("head").reshape(1)

    kept, received = [], []
    for j in range(kv_local):
        others = [key_weight, value_weight] if j == kv_local - 1 else []
        keep, send, *kept = project(
            me, hidden, query_weight, others, kept, j, columns, count
        )
        kept.append(keep)
        received.append(swap(send, "seq", 1))
    mine, queries = [], []
    for j in range(kv_local):
        mine.append(owners_sum(kept[j], received[j], me[0]))
        if j == kv_local - 1:
            copies = jnp.broadcast_to(mine[j], (count,) + mine[j].shape[1:])
            queries.append([gather_at_once(copies)])
        else:
            queries.append(gather_doubling(mine[j]))

    fresh_parts = fresh(me, mine, queries[-1][0], block, tokens)
    before = []
    for j in range(kv_local):
        flipped = j == 0 and block % LANES == 0
        parts = attention(
            queries[j], block, cache_keys, cache_values, cache_lens, me, j, flipped
        )
        parts = lax.all_to_all(parts.astype(jnp.float16), "seq", 0, 0).astype(jnp.float32)
        new_out, new_stat = fresh_parts[2 * j : 2 * j + 2]
        last = j == kv_local - 1
        attended = merge(
            me, parts, new_out, new_stat, before if last else [], count if last else 1
        )
        before.append(attended)
    attended = gather_at_once(before[-1])
    mixed = output_halves(place, output_weight, attended, block, tokens, heads)

    keep, send = mixed
    mixed = keep + swap(send, "head", 1)
    mask = 2
    while mask < heads:
        bit = place[0] // mask % 2
        pairs = mixed.reshape((-1, 2) + mixed.shape[1:])
        keep = lax.dynamic_index_in_dim(pairs, bit, 1, False)
        send = lax.dynamic_index_in_dim(pairs, 1 - bit, 1, False) * MIXED_SCALE
        received = swap(send.astype(jnp.float16), "head", mask).astype(jnp.float32)
        mixed = keep + received * (1.0 / MIXED_SCALE)
        mask *= 2
    return mixed[0].astype(jnp.bfloat16)


def solution(mesh):
    placed = (
        P(None, "seq"),
        P("seq", "head"),
        P("seq", "head"),
        P("seq", "head"),
        P("head", "seq"),
        P("seq", "head"),
        P("seq", "head"),
        P("seq"),
    )
    return jax.shard_map(
        shards, mesh=mesh, in_specs=placed, out_specs=P("head", "seq"), check_vma=False
    )
```
